32 devices in a mesh: dp: 8 (over z, core), seq: 4 (over y, x).
Axes of the slice: x: 2, y: 2, z: 4, core: 2. Of those that a mesh axis runs over, the one named last changes fastest.
Arguments:
- layer_input: bfloat16 [8, 1024, 2048], P('dp', 'seq'), may hold values from -6 to 6
- segment_ids: int32 [8, 1024], P('dp', 'seq'), may hold values from 0 to 2, as said below
- mix_gain: bfloat16 [2048], P(('dp', 'seq')), may hold values from 0.5 to 1.5
- bound_logit: bfloat16 [2048], P(('dp', 'seq')), may hold values from 2.2 to 9, as said below
- query_weight: bfloat16 [2048, 2048], P(('dp', 'seq')), may hold values from -0.125 to 0.125
- forget_weight: bfloat16 [2048, 2048], P(('dp', 'seq')), may hold values from -0.125 to 0.125
- input_weight: bfloat16 [2048, 2048], P(('dp', 'seq')), may hold values from -0.125 to 0.125
- output_gate_weight: bfloat16 [2048, 2048], P(('dp', 'seq')), may hold values from -0.125 to 0.125
- output_weight: bfloat16 [2048, 2048], P(('dp', 'seq')), may hold values from -0.1875 to 0.1875
- ffn_gain: bfloat16 [2048], P(('dp', 'seq')), may hold values from 0.5 to 1.5
- ffn_gate_weight: bfloat16 [2048, 5632], P(('dp', 'seq')), may hold values from -0.125 to 0.125
- ffn_up_weight: bfloat16 [2048, 5632], P(('dp', 'seq')), may hold values from -0.125 to 0.125
- ffn_down_weight: bfloat16 [2048, 5632], P(('dp', 'seq')), may hold values from -0.109375 to 0.109375
- output_cotangent: bfloat16 [8, 1024, 2048], P('dp', 'seq'), may hold values from -6 to 6
Outputs:
- block_output: bfloat16 [8, 1024, 2048], P('dp', 'seq')
- input_grad: float32 [8, 1024, 2048], P('dp', 'seq')
- mix_gain_grad: float32 [2048], P(('dp', 'seq'))
- bound_logit_grad: float32 [2048], P(('dp', 'seq'))
- query_weight_grad: float32 [2048, 2048], P(('dp', 'seq'))
- forget_weight_grad: float32 [2048, 2048], P(('dp', 'seq'))
- input_weight_grad: float32 [2048, 2048], P(('dp', 'seq'))
- output_gate_weight_grad: float32 [2048, 2048], P(('dp', 'seq'))
- output_weight_grad: float32 [2048, 2048], P(('dp', 'seq'))
- ffn_gain_grad: float32 [2048], P(('dp', 'seq'))
- ffn_gate_weight_grad: float32 [2048, 5632], P(('dp', 'seq'))
- ffn_up_weight_grad: float32 [2048, 5632], P(('dp', 'seq'))
- ffn_down_weight_grad: float32 [2048, 5632], P(('dp', 'seq'))
The draws below stay inside these ranges and needn't reach their ends.
Inputs may be any that keep to these rules, and one draw needn't show every extreme that they name: `segment_ids`: along each row the ids never fall; each row has three sequences, the middle one starting within the row's first 256 tokens, not at its first token, and ending within its last 256. sigmoid(bound_logit) is 0.9 or more for every feature.
All inputs are finite; a program needn't handle non-finite values.
Results may differ from the reference program's by a relative error of at most 0.009.
Values may be sent and summed in bfloat16 or wider, within the bound.
No kernel may reach another device: no remote copies, remote signals or barrier semaphores. Data moves between devices by JAX's collectives and lax.ppermute only.
A program may use at most 768 MiB of HBM per device.

```python
import jax
import jax.numpy as jnp
from jax import lax

MODEL_WIDTH = 2048
HEAD_COUNT = 16
HEAD_FEATURES = 128
FF = 5632
SHARD_TOKENS = 256
BLOCK = 64
PACKED_ROWS = 8
ROW_TOKENS = 1024


def draw_segment_ids(key, part):
    key = jax.random.fold_in(key, 5)
    first_key, final_piece_key = jax.random.split(key)
    first = jax.random.randint(first_key, (PACKED_ROWS, 1), 1, SHARD_TOKENS)
    final_piece = ROW_TOKENS - jax.random.randint(final_piece_key, (PACKED_ROWS, 1), 1, SHARD_TOKENS)
    positions = jnp.arange(ROW_TOKENS)[None, :]
    return (positions >= first).astype(jnp.int32) + (positions >= final_piece).astype(jnp.int32)


def draw_bound_logit(key, part):
    key = jax.random.fold_in(key, 11)
    order_key, slow_key, fast_key = jax.random.split(key, 3)
    order = jax.random.permutation(order_key, HEAD_COUNT)
    slow_heads = order < HEAD_COUNT // 2
    slow = jnp.log(0.5 * ROW_TOKENS) + jax.random.uniform(slow_key, (HEAD_COUNT, HEAD_FEATURES), minval=-0.5, maxval=0.5)
    fast = jax.random.uniform(fast_key, (HEAD_COUNT, HEAD_FEATURES), minval=2.3, maxval=3.4)
    return jnp.where(slow_heads[:, None], slow, fast).reshape(MODEL_WIDTH).astype(jnp.bfloat16)


def block_levels(own_key, shape, cuts, smallest, largest):
    loudness = 1.0
    for dim, shards_of in cuts:
        heights = jax.random.uniform(jax.random.fold_in(jax.random.fold_in(own_key, 6), dim), (shards_of,), jnp.float32, smallest / len(cuts), largest / len(cuts))
        loudness = loudness * jnp.repeat(jnp.exp(heights), shape[dim] // shards_of).reshape((-1,) + (1,) * (len(shape) - 1 - dim))
    return loudness


def gaussian(key, extent, scale, most, cuts=(), held_as=jnp.bfloat16):
    result = jax.random.normal(key, extent, jnp.float32) * scale
    if len(cuts) > 0:
        result = block_levels(key, extent, cuts, -0.22, 0.18) * result
    return jnp.clip(result, min=-most, max=most).astype(held_as)


def setup_inputs(seed: int = 0) -> dict:
    key_of = jax.random.split(jax.random.key(seed), 15)
    layer_input = gaussian(key_of[0], (PACKED_ROWS, ROW_TOKENS, MODEL_WIDTH), 1.0, 6.0, ((0, 8), (1, 4)))
    segment_ids = draw_segment_ids(jax.random.fold_in(key_of[14], 71), 0)
    mix_gain = jnp.clip(1.0 + 0.1 * jax.random.normal(key_of[2], (MODEL_WIDTH,), jnp.float32), 0.5, 1.5).astype(jnp.bfloat16)
    bound_logit = draw_bound_logit(jax.random.fold_in(key_of[14], 71), 0)
    query_weight = gaussian(key_of[4], (MODEL_WIDTH, MODEL_WIDTH), MODEL_WIDTH ** -0.5, 0.125, ((0, 32),))
    forget_weight = gaussian(key_of[5], (MODEL_WIDTH, MODEL_WIDTH), MODEL_WIDTH ** -0.5, 0.125, ((0, 32),))
    input_weight = gaussian(key_of[6], (MODEL_WIDTH, MODEL_WIDTH), MODEL_WIDTH ** -0.5, 0.125, ((0, 32),))
    output_gate_weight = gaussian(key_of[7], (MODEL_WIDTH, MODEL_WIDTH), MODEL_WIDTH ** -0.5, 0.125, ((0, 32),))
    output_weight = gaussian(key_of[8], (MODEL_WIDTH, MODEL_WIDTH), (MODEL_WIDTH // 2) ** -0.5, 0.1875, ((0, 32),))
    ffn_gain = jnp.clip(1.0 + 0.1 * jax.random.normal(key_of[9], (MODEL_WIDTH,), jnp.float32), 0.5, 1.5).astype(jnp.bfloat16)
    ffn_gate_weight = gaussian(key_of[10], (MODEL_WIDTH, FF), MODEL_WIDTH ** -0.5, 0.125, ((0, 32),))
    ffn_up_weight = gaussian(key_of[11], (MODEL_WIDTH, FF), MODEL_WIDTH ** -0.5, 0.125, ((0, 32),))
    ffn_down_weight = gaussian(key_of[12], (MODEL_WIDTH, FF), (FF // 2) ** -0.5, 0.109375, ((0, 32),))
    output_cotangent = gaussian(key_of[13], (PACKED_ROWS, ROW_TOKENS, MODEL_WIDTH), 1.0, 6.0, ((0, 8), (1, 4)))
    return {"layer_input": layer_input, "segment_ids": segment_ids, "mix_gain": mix_gain, "bound_logit": bound_logit, "query_weight": query_weight, "forget_weight": forget_weight, "input_weight": input_weight, "output_gate_weight": output_gate_weight, "output_weight": output_weight, "ffn_gain": ffn_gain, "ffn_gate_weight": ffn_gate_weight, "ffn_up_weight": ffn_up_weight, "ffn_down_weight": ffn_down_weight, "output_cotangent": output_cotangent}


eps_model = 1e-06
eps_group = 1e-05
highest = lax.Precision.HIGHEST

@jax.custom_vjp
def low(v):
    return lax.optimization_barrier(v.astype(jnp.bfloat16)).astype(jnp.float32)

@jax.custom_vjp
def low_back(v):
    return v

def low_keep(v):
    return (low(v), None)

def low_pass(kept, grad):
    return (grad,)

def back_keep(v):
    return (v, None)

def back_low(kept, grad):
    return (low(grad),)
low.defvjp(low_keep, low_pass)
low_back.defvjp(back_keep, back_low)

def run_block(queries, key_gate, value_rows, segments, prior, start_state, block_len):
    rows, length, heads, width = queries.shape
    count = length // block_len
    log_keep = jnp.log1p(-key_gate)

    def split_blocks(array):
        shaped = array.reshape((rows, count, block_len) + array.shape[2:])
        return jnp.moveaxis(shaped, 1, 0)
    pieces = (split_blocks(queries), split_blocks(key_gate), split_blocks(value_rows), split_blocks(log_keep), split_blocks(segments))
    causal = jnp.arange(block_len)[:, None] >= jnp.arange(block_len)[None, :]

    def step(carry, piece):
        state, before = carry
        query_c, gate_c, value_c, log_c, seg_c = piece
        cumul = jnp.cumsum(log_c, axis=1)
        query_d = query_c * jnp.exp(cumul)
        gate_d = gate_c * jnp.exp(-cumul)
        same = (seg_c[:, :, None] == seg_c[:, None, :]) & causal[None]
        scores = jnp.einsum('rthk,rshk->rhts', query_d, gate_d, precision=highest)
        scores = jnp.where(same[:, None], scores, 0.0)
        output = jnp.einsum('rhts,rshv->rthv', scores, value_c, precision=highest)
        linked = (seg_c == before[:, None]).astype(jnp.float32)
        output = output + jnp.einsum('rthk,rhkv->rthv', query_d * linked[:, :, None, None], state, precision=highest)
        last_log = cumul[:, -1]
        tail = (seg_c == seg_c[:, -1:]).astype(jnp.float32)
        gate_t = gate_c * jnp.exp(last_log[:, None] - cumul) * tail[:, :, None, None]
        keep_old = jnp.exp(last_log) * linked[:, -1][:, None, None]
        state = keep_old[..., None] * state + jnp.einsum('rshk,rshv->rhkv', gate_t, value_c, precision=highest)
        return ((state, seg_c[:, -1]), output)
    (final, unused), outputs = lax.scan(jax.checkpoint(step), (start_state, prior), pieces)
    outputs = jnp.moveaxis(outputs, 0, 1).reshape(rows, length, heads, width)
    return (outputs, final)

def matmul(left, right):
    return jnp.dot(left, right, precision=highest, preferred_element_type=jnp.float32)

def forward(layer_input, mix_gain, bound_logit, query_weight, forget_weight, input_weight, output_gate_weight, output_weight, ffn_gain, ffn_gate_weight, ffn_up_weight, ffn_down_weight, segment_ids):
    rows, length, width = layer_input.shape
    tokens = rows * length
    inputs = layer_input.reshape(tokens, width)
    factor_in = lax.rsqrt(lax.optimization_barrier(jnp.mean(inputs * inputs, axis=-1, keepdims=True)) + eps_model)
    normed_in = low(inputs * factor_in * mix_gain)
    query_pre = low_back(matmul(normed_in, query_weight))
    forget_pre = low_back(matmul(normed_in, forget_weight))
    input_pre = low_back(matmul(normed_in, input_weight))
    outgate_pre = low_back(matmul(normed_in, output_gate_weight))
    key_gate = jax.nn.sigmoid(-bound_logit) * jax.nn.sigmoid(-forget_pre)
    queries = jax.nn.silu(query_pre)
    head_shape = (rows, length, HEAD_COUNT, HEAD_FEATURES)
    start_state = jnp.zeros((rows, HEAD_COUNT, HEAD_FEATURES, HEAD_FEATURES), jnp.float32)
    mixed, unused = run_block(queries.reshape(head_shape), key_gate.reshape(head_shape), input_pre.reshape(head_shape), segment_ids, segment_ids[:, 0], start_state, BLOCK)
    group_factor = lax.rsqrt(lax.optimization_barrier(jnp.mean(mixed * mixed, axis=-1, keepdims=True)) + eps_group)
    normed_mix = (mixed * group_factor).reshape(tokens, width)
    gated = low(normed_mix * jax.nn.silu(outgate_pre))
    branch = low_back(matmul(gated, output_weight))
    resid = inputs + branch
    factor_mid = lax.rsqrt(lax.optimization_barrier(jnp.mean(resid * resid, axis=-1, keepdims=True)) + eps_model)
    normed_mid = low(resid * factor_mid * ffn_gain)
    gate_h = low_back(matmul(normed_mid, ffn_gate_weight))
    up_h = low_back(matmul(normed_mid, ffn_up_weight))
    hidden = low(jax.nn.silu(gate_h) * up_h)
    ffn_out = low_back(matmul(hidden, ffn_down_weight.T))
    return (resid + ffn_out).reshape(rows, length, width)

def reference(layer_input, segment_ids, mix_gain, bound_logit, query_weight, forget_weight, input_weight, output_gate_weight, output_weight, ffn_gain, ffn_gate_weight, ffn_up_weight, ffn_down_weight, output_cotangent):
    floats = tuple((array.astype(jnp.float32) for array in (layer_input, mix_gain, bound_logit, query_weight, forget_weight, input_weight, output_gate_weight, output_weight, ffn_gain, ffn_gate_weight, ffn_up_weight, ffn_down_weight)))

    def wrapped(*params):
        return forward(*params, segment_ids)
    output, pullback = jax.vjp(wrapped, *floats)
    grads = pullback(output_cotangent.astype(jnp.float32))
    return (output.astype(jnp.bfloat16), grads[0], grads[1], grads[2], grads[3], grads[4], grads[5], grads[6], grads[7], grads[8], grads[9], grads[10], grads[11])
```

```python
import functools

import jax
import jax.numpy as jnp
from jax import lax
from jax.experimental import pallas as pl
from jax.experimental.pallas import tpu as pltpu
from jax.sharding import PartitionSpec as P

HEAD_FEATURES = 128
CHUNK = 128

eps_model = 1e-06
eps_group = 1e-05
highest = lax.Precision.HIGHEST
f32 = jnp.float32
bf16 = jnp.bfloat16


def flip(block, axis, bits):
    return lax.ppermute(block, axis, [(i, i ^ bits) for i in range(lax.axis_size(axis))])


def gather_small(block, axis):
    count, mine = (lax.axis_size(axis), lax.axis_index(axis))
    bit = 1
    while bit < count:
        other = flip(block, axis, bit)
        upper = (mine & bit) != 0
        block = jnp.concatenate(
            (jnp.where(upper, other, block), jnp.where(upper, block, other)), axis=0
        )
        bit *= 2
    return block


def sum_small(block, axis):
    count = lax.axis_size(axis)
    bit = 1
    while bit < count:
        block = block + flip(block, axis, bit)
        bit *= 2
    return block


def gather_seq(block):
    count = lax.axis_size("seq")
    if count != 4:
        return gather_small(block, "seq")
    mine = lax.axis_index("seq")
    tokens = block.shape[0]
    half = tokens // 2
    near = flip(block, "seq", 1)
    far = flip(block, "seq", 2)
    corner_top = flip(near[:half], "seq", 2)
    corner_low = flip(far[half:], "seq", 1)
    whole = jnp.zeros((4 * tokens,) + block.shape[1:], block.dtype)
    whole = lax.dynamic_update_slice_in_dim(whole, block, mine * tokens, 0)
    whole = lax.dynamic_update_slice_in_dim(whole, near, (mine ^ 1) * tokens, 0)
    whole = lax.dynamic_update_slice_in_dim(whole, far, (mine ^ 2) * tokens, 0)
    whole = lax.dynamic_update_slice_in_dim(whole, corner_top, (mine ^ 3) * tokens, 0)
    return lax.dynamic_update_slice_in_dim(whole, corner_low, (mine ^ 3) * tokens + half, 0)


def scatter_seq(partial):
    count = lax.axis_size("seq")
    pieces = partial.astype(bf16).reshape((count, partial.shape[0] // count) + partial.shape[1:])
    pieces = lax.all_to_all(pieces, "seq", split_axis=0, concat_axis=0, tiled=True)
    return jnp.sum(pieces.astype(f32), axis=0)


def gather_columns(weights):
    count = lax.axis_size("seq")
    rows = weights[0].shape[0]
    parts = [jnp.moveaxis(w.reshape(rows, count, w.shape[1] // count), 1, 0) for w in weights]
    pieces = jnp.concatenate(parts, axis=2)
    pieces = lax.all_to_all(pieces, "seq", split_axis=0, concat_axis=0, tiled=True)
    return lax.all_gather(pieces.reshape(count * rows, pieces.shape[2]), "dp", axis=0, tiled=True)


def scatter_columns(grad, parts):
    count = lax.axis_size("seq")
    mine = lax.psum_scatter(grad, "dp", scatter_dimension=0, tiled=True)
    rows = mine.shape[0] // count
    pieces = lax.all_to_all(
        mine.reshape(count, rows, mine.shape[1]), "seq", split_axis=0, concat_axis=0, tiled=True
    )
    width = mine.shape[1] // parts
    return [
        jnp.moveaxis(pieces[:, :, i * width : (i + 1) * width], 0, 1)
        .reshape(rows, count * width)
        .astype(f32)
        for i in range(parts)
    ]


def row_route():
    count, ranks = (lax.axis_size("dp"), lax.axis_size("seq"))
    return [(b, (b % count) * ranks + b // count) for b in range(count * ranks)]


def gather_rows(weight):
    moved = lax.ppermute(weight, ("dp", "seq"), row_route())
    return lax.all_gather(moved, "dp", axis=0, tiled=True)


def scatter_rows(grad):
    mine = lax.psum_scatter(grad, "dp", scatter_dimension=0, tiled=True)
    back = [(b, a) for a, b in row_route()]
    return lax.ppermute(mine, ("dp", "seq"), back).astype(f32)


def product(left, right, left_dim, right_dim, precision=highest):
    return lax.dot_general(
        left,
        right,
        (((left_dim,), (right_dim,)), ((), ())),
        precision=precision,
        preferred_element_type=f32,
    )


def chunk_parts(step, seg_ref, seg_col_ref, seg_row_ref, pre_ref, bound_ref, width):
    size = pre_ref.shape[0]
    first = step * size
    prior = seg_ref[jnp.maximum(first - 1, 0)]
    last = seg_ref[first + size - 1]
    seg_col = seg_col_ref[...]
    at = lax.broadcasted_iota(jnp.int32, (size, size), 0)
    of = lax.broadcasted_iota(jnp.int32, (size, size), 1)
    seen = (seg_col == seg_row_ref[...]) & (at >= of)
    linked = (seg_col == prior).astype(f32)
    tail = (seg_col == last).astype(f32)
    linked_last = (prior == last).astype(f32)
    query_pre = pre_ref[:, 0:width]
    forget_pre = pre_ref[:, width : 2 * width]
    value = pre_ref[:, 2 * width : 3 * width]
    outgate_pre = pre_ref[:, 3 * width : 4 * width]
    forget_sig = jax.nn.sigmoid(-forget_pre)
    key = bound_ref[...] * forget_sig
    query_sig = jax.nn.sigmoid(query_pre)
    lower = (at >= of).astype(f32)
    cumul = product(lower, jnp.log1p(-key), 1, 0)
    grow = jnp.exp(cumul)
    shrink = jnp.exp(-cumul)
    end = grow[size - 1 :, :]
    query_d = query_pre * query_sig * grow
    key_d = key * shrink
    key_t = key_d * end * tail
    keep = end * linked_last
    return locals()


def forward_kernel(seg_ref, seg_col_ref, seg_row_ref, pre_ref, bound_ref, gated_ref, mixed_ref, states_ref, state_ref):
    step = pl.program_id(0)
    width = mixed_ref.shape[1]
    heads = width // HEAD_FEATURES

    @pl.when(step == 0)
    def _():
        state_ref[...] = jnp.zeros_like(state_ref)

    p = chunk_parts(step, seg_ref, seg_col_ref, seg_row_ref, pre_ref, bound_ref, width)
    outgate_pre = p["outgate_pre"]
    gate_act = outgate_pre * jax.nn.sigmoid(outgate_pre)
    for h in range(heads):
        cols = slice(h * HEAD_FEATURES, (h + 1) * HEAD_FEATURES)
        query_d, key_d, value = p["query_d"][:, cols], p["key_d"][:, cols], p["value"][:, cols]
        state = state_ref[h]
        states_ref[0, h] = state
        scores = jnp.where(p["seen"], product(query_d, key_d, 1, 1), 0.0)
        mixed = product(scores, value, 1, 0) + product(query_d * p["linked"], state, 1, 1)
        mixed_ref[:, cols] = mixed
        factor = lax.rsqrt(jnp.mean(mixed * mixed, axis=-1, keepdims=True) + eps_group)
        gated_ref[:, cols] = (mixed * factor * gate_act[:, cols]).astype(bf16)
        state_ref[h] = state * p["keep"][:, cols] + product(value, p["key_t"][:, cols], 0, 0)


def backward_kernel(seg_ref, seg_col_ref, seg_row_ref, pre_ref, bound_ref, mixed_ref, gated_grad_ref, states_ref, grads_ref, logit_ref, back_ref, through_ref):
    step = pl.program_id(0)
    chunk = pl.num_programs(0) - 1 - step
    width = mixed_ref.shape[1]
    heads = width // HEAD_FEATURES

    @pl.when(step == 0)
    def _():
        back_ref[...] = jnp.zeros_like(back_ref)
        through_ref[...] = jnp.zeros_like(through_ref)
        logit_ref[...] = jnp.zeros_like(logit_ref)

    p = chunk_parts(chunk, seg_ref, seg_col_ref, seg_row_ref, pre_ref, bound_ref, width)
    size = pre_ref.shape[0]
    outgate_pre, query_pre, query_sig = p["outgate_pre"], p["query_pre"], p["query_sig"]
    outgate_sig = jax.nn.sigmoid(outgate_pre)
    upper = (p["at"] <= p["of"]).astype(f32)
    for h in range(heads):
        cols = slice(h * HEAD_FEATURES, (h + 1) * HEAD_FEATURES)
        query_d, key_d, key_t, value = (p[k][:, cols] for k in ("query_d", "key_d", "key_t", "value"))
        grow, shrink, end, keep, key = (p[k][:, cols] for k in ("grow", "shrink", "end", "keep", "key"))
        state = states_ref[0, h]
        back = back_ref[h]
        mixed = mixed_ref[:, cols]
        factor = lax.rsqrt(jnp.mean(mixed * mixed, axis=-1, keepdims=True) + eps_group)
        normed = mixed * factor
        gated_grad = gated_grad_ref[:, cols]
        gate, gate_sig = outgate_pre[:, cols], outgate_sig[:, cols]
        outgate_grad = gated_grad * normed * (gate_sig * (1.0 + gate * (1.0 - gate_sig)))
        weighted = gated_grad * (gate * gate_sig)
        mixed_grad = factor * (
            weighted - normed * jnp.mean(weighted * normed, axis=-1, keepdims=True)
        )
        scores = jnp.where(p["seen"], product(query_d, key_d, 1, 1), 0.0)
        scores_grad = jnp.where(p["seen"], product(mixed_grad, value, 1, 1), 0.0)
        value_grad = product(scores, mixed_grad, 0, 0) + product(key_t, back, 1, 1)
        query_d_grad = product(scores_grad, key_d, 1, 0) + p["linked"] * product(mixed_grad, state, 1, 0)
        key_d_grad = product(scores_grad, query_d, 0, 0)
        key_t_grad = product(value, back, 1, 0)
        key_grad = key_d_grad * shrink + (p["tail"] * end * shrink) * key_t_grad
        change = query_d * query_d_grad - key_d * key_d_grad - key_t * key_t_grad
        through = product(upper, change, 1, 0) + through_ref[:, cols]
        key_total = key_grad - through / (1.0 - key)
        new_back = back * keep + product(mixed_grad, query_d * p["linked"], 0, 0)
        back_ref[h] = new_back
        through_ref[:, cols] = jnp.sum(new_back * state, axis=0, keepdims=True)
        sig = query_sig[:, cols]
        query_grad = query_d_grad * grow * (sig * (1.0 + query_pre[:, cols] * (1.0 - sig)))
        weighted_key = key_total * key
        forget_grad = -weighted_key * (1.0 - p["forget_sig"][:, cols])
        logit_ref[:, cols] += jnp.sum(weighted_key, axis=0, keepdims=True)
        for part, grad in enumerate((query_grad, forget_grad, value_grad, outgate_grad)):
            lo = part * width + h * HEAD_FEATURES
            grads_ref[:, lo : lo + HEAD_FEATURES] = grad.astype(bf16)


def recurrence_forward(segments, pre, bound):
    tokens, wide = pre.shape
    width = wide // 4
    heads = width // HEAD_FEATURES
    steps = tokens // CHUNK
    return pl.pallas_call(
        forward_kernel,
        grid_spec=pltpu.PrefetchScalarGridSpec(
            num_scalar_prefetch=1,
            grid=(steps,),
            in_specs=[
                pl.BlockSpec((CHUNK, 1), lambda i, s: (i, 0)),
                pl.BlockSpec((1, CHUNK), lambda i, s: (0, i)),
                pl.BlockSpec((CHUNK, wide), lambda i, s: (i, 0)),
                pl.BlockSpec((1, width), lambda i, s: (0, 0)),
            ],
            out_specs=[
                pl.BlockSpec((CHUNK, width), lambda i, s: (i, 0)),
                pl.BlockSpec((CHUNK, width), lambda i, s: (i, 0)),
                pl.BlockSpec((1, heads, HEAD_FEATURES, HEAD_FEATURES), lambda i, s: (i, 0, 0, 0)),
            ],
            scratch_shapes=[pltpu.VMEM((heads, HEAD_FEATURES, HEAD_FEATURES), f32)],
        ),
        out_shape=[
            jax.ShapeDtypeStruct((tokens, width), bf16),
            jax.ShapeDtypeStruct((tokens, width), f32),
            jax.ShapeDtypeStruct((steps, heads, HEAD_FEATURES, HEAD_FEATURES), f32),
        ],
        compiler_params=pltpu.CompilerParams(vmem_limit_bytes=32 * 1024 * 1024),
        name="recurrence_forward",
    )(segments, segments[:, None], segments[None, :], pre, bound)


def recurrence_backward(segments, pre, bound, mixed, gated_grad, states):
    tokens, wide = pre.shape
    width = wide // 4
    heads = width // HEAD_FEATURES
    steps = tokens // CHUNK
    return pl.pallas_call(
        backward_kernel,
        grid_spec=pltpu.PrefetchScalarGridSpec(
            num_scalar_prefetch=1,
            grid=(steps,),
            in_specs=[
                pl.BlockSpec((CHUNK, 1), lambda i, s: (steps - 1 - i, 0)),
                pl.BlockSpec((1, CHUNK), lambda i, s: (0, steps - 1 - i)),
                pl.BlockSpec((CHUNK, wide), lambda i, s: (steps - 1 - i, 0)),
                pl.BlockSpec((1, width), lambda i, s: (0, 0)),
                pl.BlockSpec((CHUNK, width), lambda i, s: (steps - 1 - i, 0)),
                pl.BlockSpec((CHUNK, width), lambda i, s: (steps - 1 - i, 0)),
                pl.BlockSpec(
                    (1, heads, HEAD_FEATURES, HEAD_FEATURES), lambda i, s: (steps - 1 - i, 0, 0, 0)
                ),
            ],
            out_specs=[
                pl.BlockSpec((CHUNK, wide), lambda i, s: (steps - 1 - i, 0)),
                pl.BlockSpec((1, width), lambda i, s: (0, 0)),
            ],
            scratch_shapes=[
                pltpu.VMEM((heads, HEAD_FEATURES, HEAD_FEATURES), f32),
                pltpu.VMEM((1, width), f32),
            ],
        ),
        out_shape=[
            jax.ShapeDtypeStruct((tokens, wide), bf16),
            jax.ShapeDtypeStruct((1, width), f32),
        ],
        compiler_params=pltpu.CompilerParams(vmem_limit_bytes=32 * 1024 * 1024),
        name="recurrence_backward",
    )(segments, segments[:, None], segments[None, :], pre, bound, mixed, gated_grad, states)


def matmul(left, right, left_dim=1, right_dim=0):
    return lax.dot_general(
        left, right, (((left_dim,), (right_dim,)), ((), ())), preferred_element_type=f32
    )


def rms_factor(value):
    return lax.rsqrt(jnp.mean(value * value, axis=-1, keepdims=True) + eps_model)


def rms_back(grad_unit, unit, factor):
    return factor * (grad_unit - unit * jnp.mean(grad_unit * unit, axis=-1, keepdims=True))


def local(
    layer_input,
    segment_ids,
    mix_gain,
    bound_logit,
    query_weight,
    forget_weight,
    input_weight,
    output_gate_weight,
    output_weight,
    ffn_gain,
    ffn_gate_weight,
    ffn_up_weight,
    ffn_down_weight,
    output_cotangent,
):
    rows, length, width = layer_input.shape
    ranks, rank = (lax.axis_size("seq"), lax.axis_index("seq"))
    my_width = width // ranks
    tokens = rows * length
    x_low = layer_input.reshape(tokens, width)
    cotangent_low = output_cotangent.reshape(tokens, width)

    mix_cols = gather_columns([query_weight, forget_weight, input_weight, output_gate_weight])
    out_rows = gather_rows(output_weight)
    ffn_cols = gather_columns([ffn_gate_weight, ffn_up_weight])
    down_cols = gather_columns([ffn_down_weight])
    vectors = jnp.stack((mix_gain, bound_logit, ffn_gain), axis=1)
    vectors = gather_small(gather_small(vectors, "seq"), "dp").astype(f32)
    gain_in, logit, gain_mid = (vectors[:, 0], vectors[:, 1], vectors[:, 2])
    segments = gather_small(segment_ids[0], "seq")
    bound = jax.nn.sigmoid(-lax.dynamic_slice_in_dim(logit, rank * my_width, my_width))

    x_all = gather_seq(x_low).astype(f32)
    normed_in = (x_all * rms_factor(x_all) * gain_in).astype(bf16)
    pre = matmul(normed_in, mix_cols)
    gated, mixed, states = recurrence_forward(segments, pre, bound[None, :])
    inputs = x_low.astype(f32)
    resid = inputs + scatter_seq(matmul(gated, out_rows))
    factor_mid = rms_factor(resid)
    unit_mid = resid * factor_mid
    normed_mid = gather_seq((unit_mid * gain_mid).astype(bf16))

    half = ffn_cols.shape[1] // 2
    both = matmul(normed_mid, ffn_cols)
    gate_h, up_h = (both[:, :half], both[:, half:])
    gate_sig = jax.nn.sigmoid(gate_h)
    gate_silu = gate_h * gate_sig
    hidden = (gate_silu * up_h).astype(bf16)
    cotangent_all = gather_seq(cotangent_low)
    down_grad = matmul(cotangent_all, hidden, 0, 0).astype(bf16)
    hidden_grad = matmul(cotangent_all, down_cols)
    gate_grad = (hidden_grad * up_h * (gate_sig * (1.0 + gate_h * (1.0 - gate_sig)))).astype(bf16)
    up_grad = (hidden_grad * gate_silu).astype(bf16)
    ffn_right = jnp.concatenate((gate_grad, up_grad), axis=1)
    mid_grad = scatter_seq(matmul(ffn_right, ffn_cols, 1, 1))
    ffn_grad = matmul(normed_mid, ffn_right, 0, 0).astype(bf16)
    block_output = (resid + scatter_seq(matmul(hidden, down_cols, 1, 1))).astype(bf16)

    cotangent = cotangent_low.astype(f32)
    resid_grad = cotangent + rms_back(mid_grad * gain_mid, unit_mid, factor_mid)
    branch_low = gather_seq(resid_grad.astype(bf16))
    gated_grad = matmul(branch_low, out_rows, 1, 1)
    mix_right, logit_part = recurrence_backward(segments, pre, bound[None, :], mixed, gated_grad, states)
    out_grad = matmul(gated, branch_low, 0, 0).astype(bf16)
    mix_grad = matmul(normed_in, mix_right, 0, 0).astype(bf16)
    in_grad = scatter_seq(matmul(mix_right, mix_cols, 1, 1))
    factor_in = rms_factor(inputs)
    input_grad = resid_grad + rms_back(in_grad * gain_in, inputs * factor_in, factor_in)

    (ffn_down_weight_grad,) = scatter_columns(down_grad, 1)
    ffn_gate_weight_grad, ffn_up_weight_grad = scatter_columns(ffn_grad, 2)
    output_weight_grad = scatter_rows(out_grad)
    query_weight_grad, forget_weight_grad, input_weight_grad, output_gate_weight_grad = scatter_columns(
        mix_grad, 4
    )
    logit_sum = gather_small(sum_small(-logit_part[0] * (1.0 - bound), "dp"), "seq")
    my_rows = mix_gain.shape[0]
    at = (lax.axis_index("dp") * ranks + rank) * my_rows
    bound_logit_grad = lax.dynamic_slice_in_dim(logit_sum, at, my_rows)

    def gain_grad(gain, pairs):
        total = sum(jnp.sum(weight.astype(f32) * grad, axis=1) for weight, grad in pairs)
        return total / gain.astype(f32)

    mix_gain_grad = gain_grad(
        mix_gain,
        (
            (query_weight, query_weight_grad),
            (forget_weight, forget_weight_grad),
            (input_weight, input_weight_grad),
            (output_gate_weight, output_gate_weight_grad),
        ),
    )
    ffn_gain_grad = gain_grad(
        ffn_gain, ((ffn_gate_weight, ffn_gate_weight_grad), (ffn_up_weight, ffn_up_weight_grad))
    )
    return (
        block_output.reshape(rows, length, width),
        input_grad.reshape(rows, length, width),
        mix_gain_grad,
        bound_logit_grad,
        query_weight_grad,
        forget_weight_grad,
        input_weight_grad,
        output_gate_weight_grad,
        output_weight_grad,
        ffn_gain_grad,
        ffn_gate_weight_grad,
        ffn_up_weight_grad,
        ffn_down_weight_grad,
    )


def solution(mesh):
    by_token = P("dp", "seq", None)
    vector = P(("dp", "seq"))
    matrix = P(("dp", "seq"), None)
    return jax.shard_map(
        local,
        mesh=mesh,
        in_specs=(by_token, P("dp", "seq"), vector, vector)
        + (matrix,) * 5
        + (vector,)
        + (matrix,) * 3
        + (by_token,),
        out_specs=(by_token, by_token, vector, vector) + (matrix,) * 5 + (vector,) + (matrix,) * 3,
        check_vma=False,
    )
```

```python
import functools

import jax
import jax.numpy as jnp
from jax import lax
from jax.experimental import pallas as pl
from jax.experimental.pallas import tpu as pltpu
from jax.sharding import PartitionSpec as P

HEAD_FEATURES = 128
LANES = 128

eps_model = 1e-06
eps_group = 1e-05
highest = lax.Precision.HIGHEST
f32 = jnp.float32
bf16 = jnp.bfloat16

vmem = pltpu.CompilerParams(vmem_limit_bytes=48 * 1024 * 1024)


def cost(flops, moved=0):
    return pl.CostEstimate(flops=flops, bytes_accessed=moved, transcendentals=0)


def flip(block, axis, bits):
    return lax.ppermute(block, axis, [(i, i ^ bits) for i in range(lax.axis_size(axis))])


def gather_small(block, axis):
    count, mine = (lax.axis_size(axis), lax.axis_index(axis))
    bit = 1
    while bit < count:
        other = flip(block, axis, bit)
        upper = (mine & bit) != 0
        block = jnp.concatenate(
            (jnp.where(upper, other, block), jnp.where(upper, block, other)), axis=0
        )
        bit *= 2
    return block


def sum_small(block, axis):
    count = lax.axis_size(axis)
    bit = 1
    while bit < count:
        block = block + flip(block, axis, bit)
        bit *= 2
    return block


def slots():
    if lax.axis_size("seq") == 4:
        return [(1, 0), (3, 0), (2, 1), (3, 1), (0, 0), (0, 1), (2, 0), (1, 1)]
    return [(k, h) for k in range(lax.axis_size("seq")) for h in range(2)]


def slot_table():
    place = {slot: i for i, slot in enumerate(slots())}
    count = lax.axis_size("seq")
    table = jnp.array([[place[k, h] for h in range(2)] for k in range(count)], jnp.int32)
    return table[jnp.arange(count) ^ lax.axis_index("seq")].reshape(2 * count)


def row_places():
    k, h = (jnp.array(bits, jnp.int32) for bits in zip(*slots()))
    return (k ^ lax.axis_index("seq")) * 2 + h


def gather_seq(block, second=()):
    count = lax.axis_size("seq")
    half = block.shape[0] // 2
    if count == 4:
        near = flip(block, "seq", 1)
        far = flip(block, "seq", 2)
        corner_top = flip(after(near[:half], *second), "seq", 2)
        corner_low = flip(after(far[half:], *second), "seq", 1)
        found = {(3, 0): (3, 0), (3, 1): (4, 0)}
        for k in range(3):
            found[k, 0], found[k, 1] = ((k, 0), (k, half))
        return (block, near, far, corner_top, corner_low), [found[slot] for slot in slots()]
    bit = 1
    while bit < count:
        block = jnp.concatenate((block, flip(block, "seq", bit)), axis=0)
        bit *= 2
    return (block,), [(0, i * half) for i in range(2 * count)]


def partial_layout(tokens):
    count = lax.axis_size("seq")
    if count == 4:
        return [(0, 2, bf16), (2, 4, bf16), (4, 8, f32)]
    return [(0, 2 * count, f32)]


def scatter_seq(partials, half, beside=()):
    if len(partials) == 3:
        near, far, rest = partials
        near = flip(near, "seq", 1)
        far = flip(far, "seq", 2)
        rest = after(rest, *beside)
        across = (rest[2 * half : 3 * half] + near[half:].astype(f32)).astype(bf16)
        along = (rest[3 * half :] + far[half:].astype(f32)).astype(bf16)
        return (rest, near, far, flip(across, "seq", 2), flip(along, "seq", 1))
    (total,) = partials
    bit = lax.axis_size("seq") // 2
    while bit:
        middle = total.shape[0] // 2
        total = total[:middle] + flip(total[middle:].astype(bf16), "seq", bit).astype(f32)
        bit //= 2
    return (total,)


def swap_seq(pieces):
    return lax.all_to_all(pieces, "seq", split_axis=0, concat_axis=0, tiled=True)


def gather_dp(block):
    return lax.all_gather(block, "dp", axis=0, tiled=True)


def scatter_dp(mine):
    groups = [list(range(c, lax.axis_size("dp"), 2)) for c in range(2)]
    return lax.psum_scatter(
        mine, "dp", scatter_dimension=0, axis_index_groups=groups, tiled=True
    )


def row_route():
    count, ranks = (lax.axis_size("dp"), lax.axis_size("seq"))
    return [(b, (b % count) * ranks + b // count) for b in range(count * ranks)]


def after(value, *others):
    return lax.optimization_barrier((value,) + others)[0]


def block(*shape, at=None):
    return pl.BlockSpec(shape, at or (lambda *_: (0,) * len(shape)))


def column_blocks(width, interleave):
    size = LANES if interleave else width
    return [(j * size, size) for j in range(width // size)]


def pieces_kernel(interleave, *refs):
    weights, out_ref = (refs[:-1], refs[-1])
    blocks = column_blocks(weights[0].shape[1], interleave)
    at = 0
    for start, size in blocks:
        for ref in weights:
            out_ref[0, :, at : at + size] = ref[:, start : start + size]
            at += size


def column_pieces(weights, interleave=False):
    ranks = lax.axis_size("seq")
    rows, width = (weights[0].shape[0], weights[0].shape[1] // ranks)
    if width % LANES:
        parts = [jnp.moveaxis(w.reshape(rows, ranks, width), 1, 0) for w in weights]
        return jnp.concatenate(parts, axis=2)
    total = width * len(weights)
    return pl.pallas_call(
        functools.partial(pieces_kernel, interleave),
        grid=(ranks,),
        in_specs=[block(rows, width, at=lambda r: (0, r)) for _ in weights],
        out_specs=block(1, rows, total, at=lambda r: (r, 0, 0)),
        out_shape=jax.ShapeDtypeStruct((ranks, rows, total), bf16),
        compiler_params=vmem,
        cost_estimate=cost(0, 4 * rows * total * ranks),
        name="column_pieces",
    )(*weights)


def return_kernel(interleave, count, *refs):
    pieces_ref, weights, grads, (gain_ref,) = (
        refs[0],
        refs[1 : 1 + count],
        refs[1 + count : 1 + 2 * count],
        refs[1 + 2 * count :],
    )

    @pl.when(pl.program_id(0) == 0)
    def _():
        gain_ref[...] = jnp.zeros_like(gain_ref)

    at = 0
    total = jnp.zeros(gain_ref.shape, f32)
    for start, size in column_blocks(weights[0].shape[1], interleave):
        for weight_ref, grad_ref in zip(weights, grads):
            grad = pieces_ref[0, :, at : at + size].astype(f32)
            grad_ref[:, start : start + size] = grad
            weight = weight_ref[:, start : start + size].astype(f32)
            total += jnp.sum(weight * grad, axis=1, keepdims=True)
            at += size
    gain_ref[...] += total


def return_columns(mine, weights, interleave=False):
    ranks = lax.axis_size("seq")
    rows, width = (weights[0].shape[0], weights[0].shape[1] // ranks)
    total = width * len(weights)
    pieces = swap_seq(mine.reshape(ranks, rows, total))
    if width % LANES:
        grads = [
            jnp.moveaxis(pieces[:, :, i * width : (i + 1) * width], 0, 1)
            .reshape(rows, ranks * width)
            .astype(f32)
            for i in range(len(weights))
        ]
        return grads, sum(jnp.sum(w.astype(f32) * g, axis=1) for w, g in zip(weights, grads))
    columns = block(rows, width, at=lambda r: (0, r))
    *grads, sums = pl.pallas_call(
        functools.partial(return_kernel, interleave, len(weights)),
        grid=(ranks,),
        in_specs=[block(1, rows, total, at=lambda r: (r, 0, 0))] + [columns] * len(weights),
        out_specs=[columns] * len(weights) + [block(rows, 1)],
        out_shape=[jax.ShapeDtypeStruct(w.shape, f32) for w in weights]
        + [jax.ShapeDtypeStruct((rows, 1), f32)],
        compiler_params=vmem,
        cost_estimate=cost(0, 8 * rows * total * ranks),
        name="return_columns",
    )(pieces, *weights)
    return grads, sums[:, 0]


def product(left, right, left_dim, right_dim, precision=highest):
    return lax.dot_general(
        left,
        right,
        (((left_dim,), (right_dim,)), ((), ())),
        precision=precision,
        preferred_element_type=f32,
    )


def chunk_parts(chunk, seg_ref, seg_col_ref, seg_row_ref, pre_ref, bound_ref):
    size, wide = pre_ref.shape
    width = wide // 3
    first = chunk * size
    prior = seg_ref[jnp.maximum(first - 1, 0)]
    last = seg_ref[first + size - 1]
    seg_col = seg_col_ref[...]
    at = lax.broadcasted_iota(jnp.int32, (size, size), 0)
    of = lax.broadcasted_iota(jnp.int32, (size, size), 1)
    seen = (seg_col == seg_row_ref[...]) & (at >= of)
    linked = (seg_col == prior).astype(f32)
    tail = (seg_col == last).astype(f32)
    linked_last = (prior == last).astype(f32)
    query_pre = pre_ref[:, 0:width]
    forget_pre = pre_ref[:, width : 2 * width]
    value = pre_ref[:, 2 * width : 3 * width]
    forget_sig = jax.nn.sigmoid(-forget_pre)
    key = bound_ref[...] * forget_sig
    query_sig = jax.nn.sigmoid(query_pre)
    lower = (at >= of).astype(f32)
    cumul = product(lower, jnp.log1p(-key), 1, 0)
    grow = jnp.exp(cumul)
    shrink = jnp.exp(-cumul)
    end = grow[size - 1 :, :]
    query_d = query_pre * query_sig * grow
    key_d = key * shrink
    key_t = key_d * end * tail
    keep = end * linked_last
    return locals()


def forward_kernel(seg_ref, slot_ref, seg_col_ref, seg_row_ref, pre_ref, bound_ref, mixed_ref, states_ref, state_ref):
    step = pl.program_id(0)
    heads = mixed_ref.shape[1] // HEAD_FEATURES

    @pl.when(step == 0)
    def _():
        state_ref[...] = jnp.zeros_like(state_ref)

    p = chunk_parts(step, seg_ref, seg_col_ref, seg_row_ref, pre_ref, bound_ref)
    for h in range(heads):
        cols = slice(h * HEAD_FEATURES, (h + 1) * HEAD_FEATURES)
        query_d, key_d, value = p["query_d"][:, cols], p["key_d"][:, cols], p["value"][:, cols]
        state = state_ref[h]
        states_ref[0, h] = state
        scores = jnp.where(p["seen"], product(query_d, key_d, 1, 1), 0.0)
        mixed = product(scores, value, 1, 0) + product(query_d * p["linked"], state, 1, 1)
        mixed_ref[:, cols] = mixed
        state_ref[h] = state * p["keep"][:, cols] + product(value, p["key_t"][:, cols], 0, 0)


def backward_kernel(seg_ref, slot_ref, seg_col_ref, seg_row_ref, pre_ref, bound_ref, outgate_pre_ref, mixed_ref, gated_grad_ref, states_ref, grads_ref, logit_ref, back_ref, through_ref):
    step = pl.program_id(0)
    chunk = pl.num_programs(0) - 1 - step
    width = mixed_ref.shape[1]
    heads = width // HEAD_FEATURES

    @pl.when(step == 0)
    def _():
        back_ref[...] = jnp.zeros_like(back_ref)
        through_ref[...] = jnp.zeros_like(through_ref)
        logit_ref[...] = jnp.zeros_like(logit_ref)

    p = chunk_parts(chunk, seg_ref, seg_col_ref, seg_row_ref, pre_ref, bound_ref)
    query_pre, query_sig = p["query_pre"], p["query_sig"]
    upper = (p["at"] <= p["of"]).astype(f32)
    for h in range(heads):
        cols = slice(h * HEAD_FEATURES, (h + 1) * HEAD_FEATURES)
        query_d, key_d, key_t, value = (p[k][:, cols] for k in ("query_d", "key_d", "key_t", "value"))
        grow, shrink, end, keep, key = (p[k][:, cols] for k in ("grow", "shrink", "end", "keep", "key"))
        state = states_ref[0, h]
        back = back_ref[h]
        mixed = mixed_ref[:, cols]
        factor = lax.rsqrt(jnp.mean(mixed * mixed, axis=-1, keepdims=True) + eps_group)
        normed = mixed * factor
        gated_grad = gated_grad_ref[:, cols]
        gate = outgate_pre_ref[:, cols]
        gate_sig = jax.nn.sigmoid(gate)
        outgate_grad = gated_grad * normed * (gate_sig * (1.0 + gate * (1.0 - gate_sig)))
        weighted = gated_grad * (gate * gate_sig)
        mixed_grad = factor * (
            weighted - normed * jnp.mean(weighted * normed, axis=-1, keepdims=True)
        )
        scores = jnp.where(p["seen"], product(query_d, key_d, 1, 1), 0.0)
        scores_grad = jnp.where(p["seen"], product(mixed_grad, value, 1, 1), 0.0)
        value_grad = product(scores, mixed_grad, 0, 0) + product(key_t, back, 1, 1)
        query_d_grad = product(scores_grad, key_d, 1, 0) + p["linked"] * product(mixed_grad, state, 1, 0)
        key_d_grad = product(scores_grad, query_d, 0, 0)
        key_t_grad = product(value, back, 1, 0)
        key_grad = key_d_grad * shrink + (p["tail"] * end * shrink) * key_t_grad
        change = query_d * query_d_grad - key_d * key_d_grad - key_t * key_t_grad
        through = product(upper, change, 1, 0) + through_ref[:, cols]
        key_total = key_grad - through / (1.0 - key)
        new_back = back * keep + product(mixed_grad, query_d * p["linked"], 0, 0)
        back_ref[h] = new_back
        through_ref[:, cols] = jnp.sum(new_back * state, axis=0, keepdims=True)
        sig = query_sig[:, cols]
        query_grad = query_d_grad * grow * (sig * (1.0 + query_pre[:, cols] * (1.0 - sig)))
        weighted_key = key_total * key
        forget_grad = -weighted_key * (1.0 - p["forget_sig"][:, cols])
        logit_ref[:, cols] += jnp.sum(weighted_key, axis=0, keepdims=True)
        for part, grad in enumerate((query_grad, forget_grad, value_grad, outgate_grad)):
            lo = part * width + h * HEAD_FEATURES
            grads_ref[:, lo : lo + HEAD_FEATURES] = grad.astype(bf16)


def recurrence_forward(segments, table, pre, bound):
    tokens, wide = pre.shape
    steps = table.shape[0]
    size, width = (tokens // steps, wide // 4)
    heads = width // HEAD_FEATURES
    return pl.pallas_call(
        forward_kernel,
        grid_spec=pltpu.PrefetchScalarGridSpec(
            num_scalar_prefetch=2,
            grid=(steps,),
            in_specs=[
                pl.BlockSpec((size, 1), lambda i, s, t: (i, 0)),
                pl.BlockSpec((1, size), lambda i, s, t: (0, i)),
                pl.BlockSpec((size, 3 * width), lambda i, s, t: (t[i], 0)),
                pl.BlockSpec((1, width), lambda i, s, t: (0, 0)),
            ],
            out_specs=[
                pl.BlockSpec((size, width), lambda i, s, t: (t[i], 0)),
                pl.BlockSpec((1, heads, HEAD_FEATURES, HEAD_FEATURES), lambda i, s, t: (i, 0, 0, 0)),
            ],
            scratch_shapes=[pltpu.VMEM((heads, HEAD_FEATURES, HEAD_FEATURES), f32)],
        ),
        out_shape=[
            jax.ShapeDtypeStruct((tokens, width), f32),
            jax.ShapeDtypeStruct((steps, heads, HEAD_FEATURES, HEAD_FEATURES), f32),
        ],
        compiler_params=vmem,
        cost_estimate=cost(320 * tokens * width * HEAD_FEATURES),
        name="recurrence_forward",
    )(segments, table, segments[:, None], segments[None, :], pre, bound)


def recurrence_backward(segments, table, pre, bound, mixed, gated_grad, states):
    tokens, wide = pre.shape
    steps = table.shape[0]
    size, width = (tokens // steps, wide // 4)
    heads = width // HEAD_FEATURES
    tokens_block = pl.BlockSpec((size, width), lambda i, s, t: (t[steps - 1 - i], 0))
    return pl.pallas_call(
        backward_kernel,
        grid_spec=pltpu.PrefetchScalarGridSpec(
            num_scalar_prefetch=2,
            grid=(steps,),
            in_specs=[
                pl.BlockSpec((size, 1), lambda i, s, t: (steps - 1 - i, 0)),
                pl.BlockSpec((1, size), lambda i, s, t: (0, steps - 1 - i)),
                pl.BlockSpec((size, 3 * width), lambda i, s, t: (t[steps - 1 - i], 0)),
                pl.BlockSpec((1, width), lambda i, s, t: (0, 0)),
                pl.BlockSpec((size, width), lambda i, s, t: (t[steps - 1 - i], 3)),
                tokens_block,
                tokens_block,
                pl.BlockSpec(
                    (1, heads, HEAD_FEATURES, HEAD_FEATURES),
                    lambda i, s, t: (steps - 1 - i, 0, 0, 0),
                ),
            ],
            out_specs=[
                pl.BlockSpec((size, 4 * width), lambda i, s, t: (t[steps - 1 - i], 0)),
                pl.BlockSpec((1, width), lambda i, s, t: (0, 0)),
            ],
            scratch_shapes=[
                pltpu.VMEM((heads, HEAD_FEATURES, HEAD_FEATURES), f32),
                pltpu.VMEM((1, width), f32),
            ],
        ),
        out_shape=[
            jax.ShapeDtypeStruct((tokens, 4 * width), bf16),
            jax.ShapeDtypeStruct((1, width), f32),
        ],
        compiler_params=vmem,
        cost_estimate=cost(620 * tokens * width * HEAD_FEATURES),
        name="recurrence_backward",
    )(segments, table, segments[:, None], segments[None, :], pre, bound, pre, mixed, gated_grad, states)


def matmul(left, right, left_dim=1, right_dim=0):
    return lax.dot_general(
        left, right, (((left_dim,), (right_dim,)), ((), ())), preferred_element_type=f32
    )


def rms_factor(value):
    return lax.rsqrt(jnp.mean(value * value, axis=-1, keepdims=True) + eps_model)


def rms_back(grad_unit, unit, factor):
    return factor * (grad_unit - unit * jnp.mean(grad_unit * unit, axis=-1, keepdims=True))


def product_kernel(left_dim, *refs):
    left_ref, right_ref, *added, out_ref = refs
    total = matmul(left_ref[...], right_ref[...], left_dim, 0)
    for ref in added:
        total += ref[...].astype(f32)
    out_ref[...] = total.astype(out_ref.dtype)


def dense(left, right, dtype, left_dim=1, added=None, parts=2):
    height, width = (left.shape[1 - left_dim], right.shape[1])
    size = width // parts if (width // parts) % LANES == 0 else width
    columns = block(height, size, at=lambda j: (0, j))
    extra = [] if added is None else [added]
    return pl.pallas_call(
        functools.partial(product_kernel, left_dim),
        grid=(width // size,),
        in_specs=[block(*left.shape), block(right.shape[0], size, at=lambda j: (0, j))]
        + [columns] * len(extra),
        out_specs=columns,
        out_shape=jax.ShapeDtypeStruct((height, width), dtype),
        compiler_params=vmem,
        cost_estimate=cost(3 * left.shape[0] * left.shape[1] * width),
        name="dense",
    )(left, right, *extra)


def store_halves(core, value, rows, row_block, mine_ref, theirs_ref):
    for z in range(value.shape[1] // (2 * row_block)):
        even = value[:, 2 * z * row_block : (2 * z + 1) * row_block]
        odd = value[:, (2 * z + 1) * row_block : (2 * z + 2) * row_block]
        to = slice(z * row_block, (z + 1) * row_block)

        @pl.when(core == 0)
        def _():
            mine_ref[rows, to] = even
            theirs_ref[rows, to] = odd

        @pl.when(core == 1)
        def _():
            mine_ref[rows, to] = odd
            theirs_ref[rows, to] = even


def assemble_kernel(places, half, row_block, normed, core_ref, *refs):
    outs = 3 if normed else 1
    pieces, gain_ref, all_ref = (refs[: len(refs) - 1 - outs], refs[-1 - outs], refs[-outs])
    for slot, (piece, row) in enumerate(places):
        rows = slice(slot * half, (slot + 1) * half)
        value = pieces[piece][row : row + half, :]
        if normed:
            wide = value.astype(f32)
            value = (wide * rms_factor(wide) * gain_ref[...]).astype(bf16)
        all_ref[rows, :] = value
        if normed:
            store_halves(core_ref[0], value, rows, row_block, *refs[-2:])


def assemble(gathered, core, row_block, gain=None):
    pieces, places = gathered
    half = pieces[0].shape[0] // 2 if len(pieces) > 1 else pieces[0].shape[0] // len(places)
    tokens, width = (half * len(places), pieces[0].shape[1])
    normed = gain is not None
    gain = gain if normed else jnp.zeros((1, width), f32)
    shapes = [(tokens, width), (tokens, width // 2), (tokens, width // 2)][: 3 if normed else 1]
    return pl.pallas_call(
        functools.partial(assemble_kernel, places, half, row_block, normed),
        grid_spec=pltpu.PrefetchScalarGridSpec(
            num_scalar_prefetch=1,
            grid=(1,),
            in_specs=[block(*piece.shape) for piece in pieces] + [block(1, width)],
            out_specs=[block(*shape) for shape in shapes],
        ),
        out_shape=[jax.ShapeDtypeStruct(shape, bf16) for shape in shapes],
        compiler_params=vmem,
        cost_estimate=cost(0, 12 * tokens * width),
        name="assemble",
    )(core, *pieces, gain)


def store_partials(value, layout, half, refs):
    for (first, last, dtype), ref in zip(layout, refs):
        ref[...] = value[first * half : last * half, :].astype(dtype)


def partial_specs(layout, half, width, columns):
    specs = [block((b - a) * half, columns, at=lambda j: (0, j)) for a, b, _ in layout]
    shapes = [jax.ShapeDtypeStruct(((b - a) * half, width), dtype) for a, b, dtype in layout]
    return specs, shapes


def partial_kernel(layout, half, cuts, left_ref, *refs):
    weights, outs = (refs[: len(cuts)], refs[len(cuts) :])
    total = None
    for (first, last), ref in zip(cuts, weights):
        term = matmul(left_ref[:, first:last], ref[...], 1, 1)
        total = term if total is None else total + term
    store_partials(total, layout, half, outs)


def ordered_kernel(half, places_ref, left_ref, weight_ref, out_ref):
    total = matmul(left_ref[...], weight_ref[...], 1, 1).astype(bf16)
    for slot in range(left_ref.shape[0] // half):
        to = pl.multiple_of(places_ref[slot] * half, half)
        out_ref[pl.ds(to, half), :] = total[slot * half : (slot + 1) * half, :]


def exchanged_product(left, weight, places, half, columns=256):
    tokens, depth = left.shape
    width = weight.shape[0]
    ranks = lax.axis_size("seq")
    partial = pl.pallas_call(
        functools.partial(ordered_kernel, half),
        grid_spec=pltpu.PrefetchScalarGridSpec(
            num_scalar_prefetch=1,
            grid=(width // columns,),
            in_specs=[block(tokens, depth), block(columns, depth, at=lambda j, p: (j, 0))],
            out_specs=block(tokens, columns, at=lambda j, p: (0, j)),
        ),
        out_shape=jax.ShapeDtypeStruct((tokens, width), bf16),
        compiler_params=vmem,
        cost_estimate=cost(3 * tokens * depth * width),
        name="exchanged_product",
    )(places, left, weight)
    return partial, swap_seq(partial.reshape(ranks, 2 * half, width))


def partial_product(left, weights, widths, half, columns=256):
    tokens, depth = left.shape
    width = weights[0].shape[0]
    layout = partial_layout(tokens)
    specs, shapes = partial_specs(layout, half, width, columns)
    cuts = [(sum(widths[:i]), sum(widths[: i + 1])) for i in range(len(widths))]
    return pl.pallas_call(
        functools.partial(partial_kernel, layout, half, cuts),
        grid=(width // columns,),
        in_specs=[block(tokens, depth)]
        + [block(columns, size, at=lambda j: (j, 0)) for size in widths],
        out_specs=specs,
        out_shape=shapes,
        compiler_params=vmem,
        cost_estimate=cost(3 * tokens * depth * width),
        name="partial_product",
    )(left, *weights)


def gate_out_kernel(layout, half, mixed_ref, outgate_pre_ref, out_ref, gated_ref, *outs):
    @pl.when(pl.program_id(0) == 0)
    def _():
        for h in range(mixed_ref.shape[1] // HEAD_FEATURES):
            cols = slice(h * HEAD_FEATURES, (h + 1) * HEAD_FEATURES)
            mixed, gate = mixed_ref[:, cols], outgate_pre_ref[:, cols]
            factor = lax.rsqrt(jnp.mean(mixed * mixed, axis=-1, keepdims=True) + eps_group)
            gated_ref[:, cols] = (mixed * factor * (gate * jax.nn.sigmoid(gate))).astype(bf16)

    store_partials(matmul(gated_ref[...], out_ref[...]), layout, half, outs)


def gate_out(mixed, pre, out_rows, half):
    tokens, my_width = mixed.shape
    width = out_rows.shape[1]
    layout = partial_layout(tokens)
    specs, shapes = partial_specs(layout, half, width, my_width)
    gated, *partials = pl.pallas_call(
        functools.partial(gate_out_kernel, layout, half),
        grid=(width // my_width,),
        in_specs=[
            block(tokens, my_width),
            block(tokens, my_width, at=lambda j: (0, 3)),
            block(my_width, my_width, at=lambda j: (0, j)),
        ],
        out_specs=[block(tokens, my_width)] + specs,
        out_shape=[jax.ShapeDtypeStruct((tokens, my_width), bf16)] + shapes,
        compiler_params=vmem,
        cost_estimate=cost(3 * tokens * my_width * width, 16 * tokens * width),
        name="gate_out",
    )(mixed, pre, out_rows)
    return gated, partials


def gated_grad_kernel(places, half, *refs):
    *pieces, out_ref, all_ref, grad_ref = refs
    for slot, (piece, row) in enumerate(places):
        all_ref[slot * half : (slot + 1) * half, :] = pieces[piece][row : row + half, :]
    grad_ref[...] = matmul(all_ref[...], out_ref[...], 1, 1)


def gated_gradient(gathered, out_rows, half):
    pieces, places = gathered
    my_width, width = out_rows.shape
    tokens = half * len(places)
    return pl.pallas_call(
        functools.partial(gated_grad_kernel, places, half),
        grid=(1,),
        in_specs=[block(*piece.shape) for piece in pieces] + [block(my_width, width)],
        out_specs=[block(tokens, width), block(tokens, my_width)],
        out_shape=[
            jax.ShapeDtypeStruct((tokens, width), bf16),
            jax.ShapeDtypeStruct((tokens, my_width), f32),
        ],
        compiler_params=vmem,
        cost_estimate=cost(3 * tokens * width * my_width),
        name="gated_gradient",
    )(*pieces, out_rows)


def ffn_forward_kernel(places, half, *refs):
    *pieces, weight_ref, both_ref, hidden_ref, all_ref = refs

    @pl.when(pl.program_id(0) == 0)
    def _():
        for slot, (piece, row) in enumerate(places):
            rows = slice(slot * half, (slot + 1) * half)
            all_ref[rows, :] = pieces[piece][row : row + half, :]

    both = matmul(all_ref[...], weight_ref[...])
    both_ref[...] = both
    gate, up = (both[:, :LANES], both[:, LANES:])
    hidden_ref[...] = (gate * jax.nn.sigmoid(gate) * up).astype(bf16)


def ffn_forward(gathered, ffn_cols, half):
    pieces, places = gathered
    width, total = ffn_cols.shape
    tokens = half * len(places)
    if (total // 2) % LANES:
        (rows,) = pieces
        both = matmul(rows, ffn_cols)
        gate, up = (both[:, : total // 2], both[:, total // 2 :])
        return both, (jax.nn.silu(gate) * up).astype(bf16), rows
    return pl.pallas_call(
        functools.partial(ffn_forward_kernel, places, half),
        grid=(total // (2 * LANES),),
        in_specs=[block(*piece.shape) for piece in pieces]
        + [block(width, 2 * LANES, at=lambda j: (0, j))],
        out_specs=[
            block(tokens, 2 * LANES, at=lambda j: (0, j)),
            block(tokens, LANES, at=lambda j: (0, j)),
            block(tokens, width),
        ],
        out_shape=[
            jax.ShapeDtypeStruct((tokens, total), f32),
            jax.ShapeDtypeStruct((tokens, total // 2), bf16),
            jax.ShapeDtypeStruct((tokens, width), bf16),
        ],
        compiler_params=vmem,
        cost_estimate=cost(3 * tokens * width * total),
        name="ffn_forward",
    )(*pieces, ffn_cols)


def ffn_backward_kernel(cotangent_ref, weight_ref, both_ref, grads_ref):
    hidden_grad = matmul(cotangent_ref[...], weight_ref[...])
    for j in range(hidden_grad.shape[1] // LANES):
        grad = hidden_grad[:, j * LANES : (j + 1) * LANES]
        gate = both_ref[:, 2 * j * LANES : (2 * j + 1) * LANES]
        up = both_ref[:, (2 * j + 1) * LANES : (2 * j + 2) * LANES]
        sig = jax.nn.sigmoid(gate)
        slope = sig * (1.0 + gate * (1.0 - sig))
        grads_ref[:, 2 * j * LANES : (2 * j + 1) * LANES] = (grad * up * slope).astype(bf16)
        grads_ref[:, (2 * j + 1) * LANES : (2 * j + 2) * LANES] = (grad * (gate * sig)).astype(bf16)


def ffn_backward(cotangent_all, down_cols, both):
    tokens, width = cotangent_all.shape
    mine = down_cols.shape[1]
    if mine % LANES:
        gate, up = (both[:, :mine], both[:, mine:])
        hidden_grad = matmul(cotangent_all, down_cols)
        sig = jax.nn.sigmoid(gate)
        gate_grad = hidden_grad * up * (sig * (1.0 + gate * (1.0 - sig)))
        up_grad = hidden_grad * (gate * sig)
        return jnp.concatenate((gate_grad, up_grad), axis=1).astype(bf16)
    size = 2 * LANES
    return pl.pallas_call(
        ffn_backward_kernel,
        grid=(pl.cdiv(mine, size),),
        in_specs=[
            block(tokens, width),
            block(width, size, at=lambda j: (0, j)),
            block(tokens, 2 * size, at=lambda j: (0, j)),
        ],
        out_specs=block(tokens, 2 * size, at=lambda j: (0, j)),
        out_shape=jax.ShapeDtypeStruct((tokens, 2 * mine), bf16),
        compiler_params=vmem,
        cost_estimate=cost(4 * tokens * width * mine),
        name="ffn_backward",
    )(cotangent_all, down_cols, both)


def add_up(parts):
    if len(parts) == 1 and len(parts[0].shape) == 3:
        return jnp.sum(parts[0][...].astype(f32), axis=0)
    if len(parts) == 1:
        return parts[0][...]
    rest, near, far, across, along = parts
    top = near[...].astype(f32) + across[...].astype(f32)
    low = far[...].astype(f32) + along[...].astype(f32)
    return rest[...] + jnp.where(pl.program_id(0) == 0, top, low)


def combine_kernel(post, count, given, *refs):
    parts, values, outs = (refs[:count], refs[count : count + given], refs[count + given :])
    results = post(add_up(parts), *(ref[...].astype(f32) for ref in values))
    for result, ref in zip(results, outs):
        ref[...] = result.astype(ref.dtype)


def combine(post, parts, values, dtypes, half):
    width = parts[0].shape[-1]
    mine = block(half, width, at=lambda h: (h, 0))
    fixed = block(half, width)
    part_specs = [mine] if len(parts) == 1 else [mine] + [fixed] * 4
    if parts[0].ndim == 3:
        part_specs = [block(parts[0].shape[0], half, width, at=lambda h: (0, h, 0))]
    value_specs = [block(1, width) if v.shape[0] == 1 else mine for v in values]
    return pl.pallas_call(
        functools.partial(combine_kernel, post, len(parts), len(values)),
        grid=(2,),
        in_specs=part_specs + value_specs,
        out_specs=[mine] * len(dtypes),
        out_shape=[jax.ShapeDtypeStruct((2 * half, width), dtype) for dtype in dtypes],
        compiler_params=vmem,
        cost_estimate=cost(0, 60 * half * width),
        name="combine",
    )(*parts, *values)


def residual(branch, inputs, gain):
    resid = inputs + branch
    return resid, resid * rms_factor(resid) * gain


def residual_back(mid_grad, cotangent, resid, gain):
    factor = rms_factor(resid)
    grad = cotangent + rms_back(mid_grad * gain, resid * factor, factor)
    return grad, grad


def input_back(in_grad, resid_grad, inputs, gain):
    factor = rms_factor(inputs)
    return (resid_grad + rms_back(in_grad * gain, inputs * factor, factor),)


def local(
    layer_input,
    segment_ids,
    mix_gain,
    bound_logit,
    query_weight,
    forget_weight,
    input_weight,
    output_gate_weight,
    output_weight,
    ffn_gain,
    ffn_gate_weight,
    ffn_up_weight,
    ffn_down_weight,
    output_cotangent,
):
    rows, length, width = layer_input.shape
    ranks, rank = (lax.axis_size("seq"), lax.axis_index("seq"))
    count = lax.axis_size("dp")
    my_width = width // ranks
    tokens = rows * length
    half = tokens // 2
    my_rows = mix_gain.shape[0]
    rank_rows = my_rows * ranks
    x_low = layer_input.reshape(tokens, width)
    cotangent_low = output_cotangent.reshape(tokens, width)
    core = (lax.axis_index("dp") & 1).reshape(1)

    mix_weights = [query_weight, forget_weight, input_weight, output_gate_weight]
    mix_pieces = swap_seq(column_pieces(mix_weights))
    mix_cols = gather_dp(mix_pieces.reshape(rank_rows, 4 * my_width))
    ffn_width = 2 * ffn_gate_weight.shape[1] // ranks
    ffn_pieces = column_pieces([after(ffn_gate_weight, mix_pieces), ffn_up_weight], True)
    down_pieces = column_pieces([ffn_down_weight])
    ffn_pieces = swap_seq(jnp.concatenate((ffn_pieces, down_pieces), axis=2))
    x_pieces, places = gather_seq(after(x_low, ffn_pieces))
    vectors = jnp.stack((mix_gain, bound_logit, ffn_gain), axis=1)
    vectors = gather_small(gather_small(vectors, "seq"), "dp").astype(f32)
    gain_in, logit, gain_mid = (vectors[:, 0], vectors[:, 1], vectors[:, 2])
    gain_in, gain_mid = (gain_in[None, :], gain_mid[None, :])
    segments = gather_small(segment_ids[0], "seq")
    table = slot_table()
    bound = jax.nn.sigmoid(-lax.dynamic_slice_in_dim(logit, rank * my_width, my_width))[None, :]
    normed_in, in_mine, in_theirs = assemble(
        (x_pieces, places), core, rank_rows, after(gain_in, segments, bound)
    )
    out_piece = lax.ppermute(output_weight, ("dp", "seq"), row_route())
    out_rows = gather_dp(after(out_piece, normed_in))
    ffn_cols = gather_dp(after(ffn_pieces[:, :, :ffn_width].reshape(rank_rows, ffn_width), out_piece))
    down_pieces = ffn_pieces[:, :, ffn_width:].reshape(rank_rows, ffn_width // 2)

    pre = dense(normed_in, mix_cols, f32, parts=4)
    down_cols = gather_dp(after(down_pieces, pre))
    mixed, states = recurrence_forward(segments, table, pre, bound)
    gated, partials = gate_out(mixed, pre, out_rows, half)
    cotangent = gather_seq(after(cotangent_low, normed_in))
    branch_parts = scatter_seq(partials, half)
    (cotangent_all,) = assemble(cotangent, core, rank_rows)
    resid, normed_low = combine(
        residual, branch_parts, (after(x_low, cotangent_all), gain_mid), (f32, bf16), half
    )
    normed_mid = gather_seq(normed_low)

    both, hidden, mid_all = ffn_forward(normed_mid, ffn_cols, half)

    down_sum = dense(cotangent_all, hidden, bf16, 0)
    down_mine = lax.psum_scatter(down_sum, "dp", scatter_dimension=0, tiled=True)
    cotangent_all = after(cotangent_all, down_sum)
    ffn_right = ffn_backward(cotangent_all, down_cols, both)
    mid_partials = partial_product(ffn_right, [ffn_cols], [ffn_cols.shape[1]], half)
    ffn_sum = dense(mid_all, after(ffn_right, mid_partials[0]), bf16, 0)
    mid_parts = scatter_seq(mid_partials, half, beside=(ffn_sum, down_mine))
    ffn_mine = lax.psum_scatter(after(ffn_sum, *mid_parts[:3]), "dp", scatter_dimension=0, tiled=True)

    resid_grad, branch_own = combine(
        residual_back, mid_parts, (cotangent_low, resid, gain_mid), (f32, bf16), half
    )
    branch, places = gather_seq(branch_own)
    row_place = row_places()
    out_partial, out_parts = exchanged_product(after(hidden, branch_own), down_cols, row_place, half)
    branch = (after(branch[0], out_partial),) + branch[1:]
    branch_low, gated_grad = gated_gradient((branch, places), out_rows, half)
    mix_right, logit_part = recurrence_backward(segments, table, pre, bound, mixed, gated_grad, states)
    (ffn_down_weight_grad,), _ = return_columns(after(down_mine, branch_low), [ffn_down_weight])
    mix_theirs = dense(in_theirs, after(mix_right, ffn_down_weight_grad, out_parts), bf16, 0)
    out_sum = dense(gated, after(branch_low, mix_theirs), bf16, 0)
    mix_theirs = flip(mix_theirs, "dp", 1)
    mix_sum = dense(in_mine, after(mix_right, out_sum), bf16, 0, mix_theirs)
    mix_mine = scatter_dp(mix_sum)
    out_mine = lax.psum_scatter(after(out_sum, mix_sum), "dp", scatter_dimension=0, tiled=True)
    (ffn_gate_weight_grad, ffn_up_weight_grad), ffn_sums = return_columns(
        after(ffn_mine, mix_sum), [ffn_gate_weight, ffn_up_weight], True
    )
    (block_output,) = combine(
        lambda total, resid: (resid + total,), (out_parts,), (after(resid, mix_sum),), (bf16,), half
    )
    _, in_parts = exchanged_product(after(mix_right, mix_sum, ffn_sums), mix_cols, row_place, half)

    output_weight_grad = lax.ppermute(
        out_mine, ("dp", "seq"), [(b, a) for a, b in row_route()]
    ).astype(f32)
    logit_sum = gather_small(sum_small(-logit_part[0] * (1.0 - bound[0]), "dp"), "seq")
    at = (lax.axis_index("dp") * ranks + rank) * my_rows
    bound_logit_grad = lax.dynamic_slice_in_dim(logit_sum, at, my_rows)
    (input_grad,) = combine(
        input_back, (in_parts,), (after(resid_grad, bound_logit_grad), x_low, gain_in), (f32,), half
    )
    mix_mine = after(mix_mine, input_grad, block_output)
    mix_grads, mix_sums = return_columns(mix_mine, mix_weights)
    query_weight_grad, forget_weight_grad, input_weight_grad, output_gate_weight_grad = mix_grads
    mix_gain_grad = mix_sums / mix_gain.astype(f32)
    ffn_gain_grad = ffn_sums / ffn_gain.astype(f32)
    return (
        block_output.reshape(rows, length, width),
        input_grad.reshape(rows, length, width),
        mix_gain_grad,
        bound_logit_grad,
        query_weight_grad,
        forget_weight_grad,
        input_weight_grad,
        output_gate_weight_grad,
        output_weight_grad,
        ffn_gain_grad,
        ffn_gate_weight_grad,
        ffn_up_weight_grad,
        ffn_down_weight_grad,
    )


def solution(mesh):
    by_token = P("dp", "seq", None)
    vector = P(("dp", "seq"))
    matrix = P(("dp", "seq"), None)
    return jax.shard_map(
        local,
        mesh=mesh,
        in_specs=(by_token, P("dp", "seq"), vector, vector)
        + (matrix,) * 5
        + (vector,)
        + (matrix,) * 3
        + (by_token,),
        out_specs=(by_token, by_token, vector, vector) + (matrix,) * 5 + (vector,) + (matrix,) * 3,
        check_vma=False,
    )
```

```python
import functools

import jax
import jax.numpy as jnp
from jax import lax
from jax.experimental import pallas as pl
from jax.experimental.pallas import tpu as pltpu
from jax.sharding import PartitionSpec as P

HEAD_FEATURES = 128
LANES = 128

eps_model = 1e-06
eps_group = 1e-05
highest = lax.Precision.HIGHEST
f32 = jnp.float32
bf16 = jnp.bfloat16

vmem = pltpu.CompilerParams(vmem_limit_bytes=48 * 1024 * 1024)


def cost(flops, moved=0):
    return pl.CostEstimate(flops=flops, bytes_accessed=moved, transcendentals=0)


def flip(block, axis, bits):
    return lax.ppermute(block, axis, [(i, i ^ bits) for i in range(lax.axis_size(axis))])


def gather_small(block, axis):
    count, mine = (lax.axis_size(axis), lax.axis_index(axis))
    bit = 1
    while bit < count:
        other = flip(block, axis, bit)
        upper = (mine & bit) != 0
        block = jnp.concatenate(
            (jnp.where(upper, other, block), jnp.where(upper, block, other)), axis=0
        )
        bit *= 2
    return block


def sum_small(block, axis):
    others = [flip(block, axis, bits) for bits in range(1, lax.axis_size(axis))]
    return functools.reduce(jnp.add, others, block)


def slots():
    if lax.axis_size("seq") == 4:
        return [(1, 0), (3, 0), (2, 1), (3, 1), (0, 0), (0, 1), (2, 0), (1, 1)]
    return [(k, h) for k in range(lax.axis_size("seq")) for h in range(2)]


def slot_table():
    place = {slot: i for i, slot in enumerate(slots())}
    count = lax.axis_size("seq")
    table = jnp.array([[place[k, h] for h in range(2)] for k in range(count)], jnp.int32)
    return table[jnp.arange(count) ^ lax.axis_index("seq")].reshape(2 * count)


def row_places():
    k, h = (jnp.array(bits, jnp.int32) for bits in zip(*slots()))
    return (k ^ lax.axis_index("seq")) * 2 + h


def gather_seq(block, second=()):
    count = lax.axis_size("seq")
    half = block.shape[0] // 2
    if count == 4:
        near = flip(block, "seq", 1)
        far = flip(block, "seq", 2)
        corner_top = flip(after(near[:half], *second), "seq", 2)
        corner_low = flip(after(far[half:], *second), "seq", 1)
        found = {(3, 0): (3, 0), (3, 1): (4, 0)}
        for k in range(3):
            found[k, 0], found[k, 1] = ((k, 0), (k, half))
        return (block, near, far, corner_top, corner_low), [found[slot] for slot in slots()]
    bit = 1
    while bit < count:
        block = jnp.concatenate((block, flip(block, "seq", bit)), axis=0)
        bit *= 2
    return (block,), [(0, i * half) for i in range(2 * count)]


def partial_layout(tokens):
    count = lax.axis_size("seq")
    if count == 4:
        return [(0, 2, bf16), (2, 4, bf16), (4, 8, f32)]
    return [(0, 2 * count, f32)]


def scatter_seq(partials, half, beside=()):
    if len(partials) == 3:
        near, far, rest = partials
        near = flip(near, "seq", 1)
        far = flip(far, "seq", 2)
        rest = after(rest, *beside)
        across = (rest[2 * half : 3 * half] + near[half:].astype(f32)).astype(bf16)
        along = (rest[3 * half :] + far[half:].astype(f32)).astype(bf16)
        return (rest, near, far, flip(across, "seq", 2), flip(along, "seq", 1))
    (total,) = partials
    bit = lax.axis_size("seq") // 2
    while bit:
        middle = total.shape[0] // 2
        total = total[:middle] + flip(total[middle:].astype(bf16), "seq", bit).astype(f32)
        bit //= 2
    return (total,)


def swap_seq(pieces):
    return lax.all_to_all(pieces, "seq", split_axis=0, concat_axis=0, tiled=True)


def gather_dp(block):
    return lax.all_gather(block, "dp", axis=0, tiled=True)


def scatter_dp(mine):
    groups = [list(range(c, lax.axis_size("dp"), 2)) for c in range(2)]
    return lax.psum_scatter(
        mine, "dp", scatter_dimension=0, axis_index_groups=groups, tiled=True
    )


def row_route():
    count, ranks = (lax.axis_size("dp"), lax.axis_size("seq"))
    return [(b, (b % count) * ranks + b // count) for b in range(count * ranks)]


def after(value, *others):
    return lax.optimization_barrier((value,) + others)[0]


def block(*shape, at=None):
    return pl.BlockSpec(shape, at or (lambda *_: (0,) * len(shape)))


def column_blocks(width, interleave):
    size = LANES if interleave else width
    return [(j * size, size) for j in range(width // size)]


def pieces_kernel(interleave, *refs):
    weights, out_ref = (refs[:-1], refs[-1])
    blocks = column_blocks(weights[0].shape[1], interleave)
    at = 0
    for start, size in blocks:
        for ref in weights:
            out_ref[0, :, at : at + size] = ref[:, start : start + size]
            at += size


def column_pieces(weights, interleave=False):
    ranks = lax.axis_size("seq")
    rows, width = (weights[0].shape[0], weights[0].shape[1] // ranks)
    if width % LANES:
        parts = [jnp.moveaxis(w.reshape(rows, ranks, width), 1, 0) for w in weights]
        return jnp.concatenate(parts, axis=2)
    total = width * len(weights)
    return pl.pallas_call(
        functools.partial(pieces_kernel, interleave),
        grid=(ranks,),
        in_specs=[block(rows, width, at=lambda r: (0, r)) for _ in weights],
        out_specs=block(1, rows, total, at=lambda r: (r, 0, 0)),
        out_shape=jax.ShapeDtypeStruct((ranks, rows, total), bf16),
        compiler_params=vmem,
        cost_estimate=cost(0, 4 * rows * total * ranks),
        name="column_pieces",
    )(*weights)


def return_kernel(interleave, count, *refs):
    pieces_ref, weights, grads, (gain_ref,) = (
        refs[0],
        refs[1 : 1 + count],
        refs[1 + count : 1 + 2 * count],
        refs[1 + 2 * count :],
    )

    @pl.when(pl.program_id(0) == 0)
    def _():
        gain_ref[...] = jnp.zeros_like(gain_ref)

    at = 0
    total = jnp.zeros(gain_ref.shape, f32)
    for start, size in column_blocks(weights[0].shape[1], interleave):
        for weight_ref, grad_ref in zip(weights, grads):
            grad = pieces_ref[0, :, at : at + size].astype(f32)
            grad_ref[:, start : start + size] = grad
            weight = weight_ref[:, start : start + size].astype(f32)
            total += jnp.sum(weight * grad, axis=1, keepdims=True)
            at += size
    gain_ref[...] += total


def swap_columns(mine):
    ranks = lax.axis_size("seq")
    return swap_seq(mine.reshape(ranks, mine.shape[0] // ranks, mine.shape[1]))


def return_columns(pieces, weights, interleave=False):
    ranks, rows, total = pieces.shape
    width = weights[0].shape[1] // ranks
    if width % LANES:
        grads = [
            jnp.moveaxis(pieces[:, :, i * width : (i + 1) * width], 0, 1)
            .reshape(rows, ranks * width)
            .astype(f32)
            for i in range(len(weights))
        ]
        return grads, sum(jnp.sum(w.astype(f32) * g, axis=1) for w, g in zip(weights, grads))
    columns = block(rows, width, at=lambda r: (0, r))
    *grads, sums = pl.pallas_call(
        functools.partial(return_kernel, interleave, len(weights)),
        grid=(ranks,),
        in_specs=[block(1, rows, total, at=lambda r: (r, 0, 0))] + [columns] * len(weights),
        out_specs=[columns] * len(weights) + [block(rows, 1)],
        out_shape=[jax.ShapeDtypeStruct(w.shape, f32) for w in weights]
        + [jax.ShapeDtypeStruct((rows, 1), f32)],
        compiler_params=vmem,
        cost_estimate=cost(0, 8 * rows * total * ranks),
        name="return_columns",
    )(pieces, *weights)
    return grads, sums[:, 0]


def exact_product(left, right, left_dim, right_dim):
    return lax.dot_general(
        left,
        right,
        (((left_dim,), (right_dim,)), ((), ())),
        precision=highest,
        preferred_element_type=f32,
    )


def product(left, right, left_dim, right_dim):
    left_high, right_high = (left.astype(bf16), right.astype(bf16))
    left_low = (left - left_high.astype(f32)).astype(bf16)
    right_low = (right - right_high.astype(f32)).astype(bf16)
    return (
        matmul(left_high, right_low, left_dim, right_dim)
        + matmul(left_low, right_high, left_dim, right_dim)
        + matmul(left_high, right_high, left_dim, right_dim)
    )


def chunk_parts(chunk, seg_ref, seg_col_ref, seg_row_ref, pre_ref, bound_ref):
    size, wide = pre_ref.shape
    width = wide // 3
    first = chunk * size
    prior = seg_ref[jnp.maximum(first - 1, 0)]
    last = seg_ref[first + size - 1]
    seg_col = seg_col_ref[...]
    at = lax.broadcasted_iota(jnp.int32, (size, size), 0)
    of = lax.broadcasted_iota(jnp.int32, (size, size), 1)
    seen = (seg_col == seg_row_ref[...]) & (at >= of)
    linked = (seg_col == prior).astype(f32)
    tail = (seg_col == last).astype(f32)
    linked_last = (prior == last).astype(f32)
    query_pre = pre_ref[:, 0:width]
    forget_pre = pre_ref[:, width : 2 * width]
    value = pre_ref[:, 2 * width : 3 * width]
    forget_sig = jax.nn.sigmoid(-forget_pre)
    key = bound_ref[...] * forget_sig
    query_sig = jax.nn.sigmoid(query_pre)
    lower = (at >= of).astype(f32)
    cumul = exact_product(lower, jnp.log1p(-key), 1, 0)
    grow = jnp.exp(cumul)
    shrink = jnp.exp(-cumul)
    end = grow[size - 1 :, :]
    query_d = query_pre * query_sig * grow
    key_d = key * shrink
    key_t = key_d * end * tail
    keep = end * linked_last
    return locals()


def forward_kernel(seg_ref, slot_ref, seg_col_ref, seg_row_ref, pre_ref, bound_ref, mixed_ref, states_ref, state_ref):
    step = pl.program_id(0)
    heads = mixed_ref.shape[1] // HEAD_FEATURES

    @pl.when(step == 0)
    def _():
        state_ref[...] = jnp.zeros_like(state_ref)

    p = chunk_parts(step, seg_ref, seg_col_ref, seg_row_ref, pre_ref, bound_ref)
    for h in range(heads):
        cols = slice(h * HEAD_FEATURES, (h + 1) * HEAD_FEATURES)
        query_d, key_d, value = p["query_d"][:, cols], p["key_d"][:, cols], p["value"][:, cols]
        state = state_ref[h]
        states_ref[0, h] = state
        scores = jnp.where(p["seen"], product(query_d, key_d, 1, 1), 0.0)
        mixed = product(scores, value, 1, 0) + product(query_d * p["linked"], state, 1, 1)
        mixed_ref[:, cols] = mixed
        state_ref[h] = state * p["keep"][:, cols] + product(value, p["key_t"][:, cols], 0, 0)


def backward_kernel(seg_ref, slot_ref, seg_col_ref, seg_row_ref, pre_ref, bound_ref, outgate_pre_ref, mixed_ref, gated_grad_ref, states_ref, grads_ref, logit_ref, back_ref, through_ref):
    step = pl.program_id(0)
    chunk = pl.num_programs(0) - 1 - step
    width = mixed_ref.shape[1]
    heads = width // HEAD_FEATURES

    @pl.when(step == 0)
    def _():
        back_ref[...] = jnp.zeros_like(back_ref)
        through_ref[...] = jnp.zeros_like(through_ref)
        logit_ref[...] = jnp.zeros_like(logit_ref)

    p = chunk_parts(chunk, seg_ref, seg_col_ref, seg_row_ref, pre_ref, bound_ref)
    query_pre, query_sig = p["query_pre"], p["query_sig"]
    upper = (p["at"] <= p["of"]).astype(f32)
    for h in range(heads):
        cols = slice(h * HEAD_FEATURES, (h + 1) * HEAD_FEATURES)
        query_d, key_d, key_t, value = (p[k][:, cols] for k in ("query_d", "key_d", "key_t", "value"))
        grow, shrink, end, keep, key = (p[k][:, cols] for k in ("grow", "shrink", "end", "keep", "key"))
        state = states_ref[0, h]
        back = back_ref[h]
        mixed = mixed_ref[:, cols]
        factor = lax.rsqrt(jnp.mean(mixed * mixed, axis=-1, keepdims=True) + eps_group)
        normed = mixed * factor
        gated_grad = gated_grad_ref[:, cols]
        gate = outgate_pre_ref[:, cols]
        gate_sig = jax.nn.sigmoid(gate)
        outgate_grad = gated_grad * normed * (gate_sig * (1.0 + gate * (1.0 - gate_sig)))
        weighted = gated_grad * (gate * gate_sig)
        mixed_grad = factor * (
            weighted - normed * jnp.mean(weighted * normed, axis=-1, keepdims=True)
        )
        scores = jnp.where(p["seen"], product(query_d, key_d, 1, 1), 0.0)
        scores_grad = jnp.where(p["seen"], product(mixed_grad, value, 1, 1), 0.0)
        value_grad = product(scores, mixed_grad, 0, 0) + product(key_t, back, 1, 1)
        query_d_grad = product(scores_grad, key_d, 1, 0) + p["linked"] * product(mixed_grad, state, 1, 0)
        key_d_grad = product(scores_grad, query_d, 0, 0)
        key_t_grad = product(value, back, 1, 0)
        key_grad = key_d_grad * shrink + (p["tail"] * end * shrink) * key_t_grad
        change = query_d * query_d_grad - key_d * key_d_grad - key_t * key_t_grad
        through = exact_product(upper, change, 1, 0) + through_ref[:, cols]
        key_total = key_grad - through / (1.0 - key)
        new_back = back * keep + product(mixed_grad, query_d * p["linked"], 0, 0)
        back_ref[h] = new_back
        through_ref[:, cols] = jnp.sum(new_back * state, axis=0, keepdims=True)
        sig = query_sig[:, cols]
        query_grad = query_d_grad * grow * (sig * (1.0 + query_pre[:, cols] * (1.0 - sig)))
        weighted_key = key_total * key
        forget_grad = -weighted_key * (1.0 - p["forget_sig"][:, cols])
        logit_ref[:, cols] += jnp.sum(weighted_key, axis=0, keepdims=True)
        for part, grad in enumerate((query_grad, forget_grad, value_grad, outgate_grad)):
            lo = part * width + h * HEAD_FEATURES
            grads_ref[:, lo : lo + HEAD_FEATURES] = grad.astype(bf16)


def recurrence_forward(segments, table, pre, bound):
    tokens, wide = pre.shape
    steps = table.shape[0]
    size, width = (tokens // steps, wide // 4)
    heads = width // HEAD_FEATURES
    return pl.pallas_call(
        forward_kernel,
        grid_spec=pltpu.PrefetchScalarGridSpec(
            num_scalar_prefetch=2,
            grid=(steps,),
            in_specs=[
                pl.BlockSpec((size, 1), lambda i, s, t: (i, 0)),
                pl.BlockSpec((1, size), lambda i, s, t: (0, i)),
                pl.BlockSpec((size, 3 * width), lambda i, s, t: (t[i], 0)),
                pl.BlockSpec((1, width), lambda i, s, t: (0, 0)),
            ],
            out_specs=[
                pl.BlockSpec((size, width), lambda i, s, t: (t[i], 0)),
                pl.BlockSpec((1, heads, HEAD_FEATURES, HEAD_FEATURES), lambda i, s, t: (i, 0, 0, 0)),
            ],
            scratch_shapes=[pltpu.VMEM((heads, HEAD_FEATURES, HEAD_FEATURES), f32)],
        ),
        out_shape=[
            jax.ShapeDtypeStruct((tokens, width), f32),
            jax.ShapeDtypeStruct((steps, heads, HEAD_FEATURES, HEAD_FEATURES), f32),
        ],
        compiler_params=vmem,
        cost_estimate=cost(320 * tokens * width * HEAD_FEATURES),
        name="recurrence_forward",
    )(segments, table, segments[:, None], segments[None, :], pre, bound)


def recurrence_backward(segments, table, pre, bound, mixed, gated_grad, states):
    tokens, wide = pre.shape
    steps = table.shape[0]
    size, width = (tokens // steps, wide // 4)
    heads = width // HEAD_FEATURES
    tokens_block = pl.BlockSpec((size, width), lambda i, s, t: (t[steps - 1 - i], 0))
    return pl.pallas_call(
        backward_kernel,
        grid_spec=pltpu.PrefetchScalarGridSpec(
            num_scalar_prefetch=2,
            grid=(steps,),
            in_specs=[
                pl.BlockSpec((size, 1), lambda i, s, t: (steps - 1 - i, 0)),
                pl.BlockSpec((1, size), lambda i, s, t: (0, steps - 1 - i)),
                pl.BlockSpec((size, 3 * width), lambda i, s, t: (t[steps - 1 - i], 0)),
                pl.BlockSpec((1, width), lambda i, s, t: (0, 0)),
                pl.BlockSpec((size, width), lambda i, s, t: (t[steps - 1 - i], 3)),
                tokens_block,
                tokens_block,
                pl.BlockSpec(
                    (1, heads, HEAD_FEATURES, HEAD_FEATURES),
                    lambda i, s, t: (steps - 1 - i, 0, 0, 0),
                ),
            ],
            out_specs=[
                pl.BlockSpec((size, 4 * width), lambda i, s, t: (t[steps - 1 - i], 0)),
                pl.BlockSpec((1, width), lambda i, s, t: (0, 0)),
            ],
            scratch_shapes=[
                pltpu.VMEM((heads, HEAD_FEATURES, HEAD_FEATURES), f32),
                pltpu.VMEM((1, width), f32),
            ],
        ),
        out_shape=[
            jax.ShapeDtypeStruct((tokens, 4 * width), bf16),
            jax.ShapeDtypeStruct((1, width), f32),
        ],
        compiler_params=vmem,
        cost_estimate=cost(620 * tokens * width * HEAD_FEATURES),
        name="recurrence_backward",
    )(segments, table, segments[:, None], segments[None, :], pre, bound, pre, mixed, gated_grad, states)


def matmul(left, right, left_dim=1, right_dim=0):
    return lax.dot_general(
        left, right, (((left_dim,), (right_dim,)), ((), ())), preferred_element_type=f32
    )


def rms_factor(value):
    return lax.rsqrt(jnp.mean(value * value, axis=-1, keepdims=True) + eps_model)


def rms_back(grad_unit, unit, factor):
    return factor * (grad_unit - unit * jnp.mean(grad_unit * unit, axis=-1, keepdims=True))


def product_kernel(left_dim, *refs):
    left_ref, right_ref, *added, out_ref = refs
    total = matmul(left_ref[...], right_ref[...], left_dim, 0)
    for ref in added:
        total += ref[...].astype(f32)
    out_ref[...] = total.astype(out_ref.dtype)


def dense(left, right, dtype, left_dim=1, added=None, parts=2):
    height, width = (left.shape[1 - left_dim], right.shape[1])
    size = width // parts if (width // parts) % LANES == 0 else width
    columns = block(height, size, at=lambda j: (0, j))
    extra = [] if added is None else [added]
    return pl.pallas_call(
        functools.partial(product_kernel, left_dim),
        grid=(width // size,),
        in_specs=[block(*left.shape), block(right.shape[0], size, at=lambda j: (0, j))]
        + [columns] * len(extra),
        out_specs=columns,
        out_shape=jax.ShapeDtypeStruct((height, width), dtype),
        compiler_params=vmem,
        cost_estimate=cost(3 * left.shape[0] * left.shape[1] * width),
        name="dense",
    )(left, right, *extra)


def mixer_sums_kernel(count, rows, core_ref, left_ref, right_ref, theirs_ref, out_ref, out_theirs_ref, total_ref):
    step = pl.program_id(0)

    @pl.when(step < count)
    def _():
        total = matmul(left_ref[...], right_ref[...], 0, 0) + theirs_ref[...].astype(f32)
        total_ref[...] = total.astype(bf16)

    @pl.when(step == count)
    def _():
        width = total_ref.shape[1]
        for z in range(out_ref.shape[0]):
            both = (out_ref[z, 0].astype(f32) + out_theirs_ref[z].astype(f32)).astype(bf16)
            ranks = both.shape[1] // width
            for j in range(ranks):
                at = (z * ranks + j) * rows
                total_ref[at : at + rows, :] = both[:, j * width : (j + 1) * width]


def mixer_sums(left, right, theirs, out_sum, out_theirs, core):
    tokens, height = left.shape
    lines, cores, rows, width = out_sum.shape
    size = right.shape[1] // 4
    columns = block(height, size, at=lambda j, c: (0, jnp.minimum(j, 3)))
    return pl.pallas_call(
        functools.partial(mixer_sums_kernel, 4, rows),
        grid_spec=pltpu.PrefetchScalarGridSpec(
            num_scalar_prefetch=1,
            grid=(5,),
            in_specs=[
                block(tokens, height),
                block(tokens, size, at=lambda j, c: (0, jnp.minimum(j, 3))),
                columns,
                block(lines, 1, rows, width, at=lambda j, c: (0, c[0], 0, 0)),
                block(lines, rows, width),
            ],
            out_specs=block(height, size, at=lambda j, c: (0, j)),
        ),
        out_shape=jax.ShapeDtypeStruct((height, 5 * size), bf16),
        compiler_params=vmem,
        cost_estimate=cost(3 * tokens * height * 4 * size),
        name="mixer_sums",
    )(core, left, right, theirs, out_sum, out_theirs)


def store_halves(core, value, rows, row_block, mine_ref, theirs_ref):
    for z in range(value.shape[1] // (2 * row_block)):
        even = value[:, 2 * z * row_block : (2 * z + 1) * row_block]
        odd = value[:, (2 * z + 1) * row_block : (2 * z + 2) * row_block]
        to = slice(z * row_block, (z + 1) * row_block)

        @pl.when(core == 0)
        def _():
            mine_ref[rows, to] = even
            theirs_ref[rows, to] = odd

        @pl.when(core == 1)
        def _():
            mine_ref[rows, to] = odd
            theirs_ref[rows, to] = even


def assemble_kernel(places, half, row_block, normed, core_ref, *refs):
    *pieces, gain_ref, all_ref, mine_ref, theirs_ref = refs
    for slot, (piece, row) in enumerate(places):
        rows = slice(slot * half, (slot + 1) * half)
        value = pieces[piece][row : row + half, :]
        if normed:
            wide = value.astype(f32)
            value = (wide * rms_factor(wide) * gain_ref[...]).astype(bf16)
        all_ref[rows, :] = value
        store_halves(core_ref[0], value, rows, row_block, mine_ref, theirs_ref)


def assemble(gathered, core, row_block, gain=None):
    pieces, places = gathered
    half = pieces[0].shape[0] // 2 if len(pieces) > 1 else pieces[0].shape[0] // len(places)
    tokens, width = (half * len(places), pieces[0].shape[1])
    normed = gain is not None
    gain = gain if normed else jnp.zeros((1, width), f32)
    shapes = [(tokens, width), (tokens, width // 2), (tokens, width // 2)]
    return pl.pallas_call(
        functools.partial(assemble_kernel, places, half, row_block, normed),
        grid_spec=pltpu.PrefetchScalarGridSpec(
            num_scalar_prefetch=1,
            grid=(1,),
            in_specs=[block(*piece.shape) for piece in pieces] + [block(1, width)],
            out_specs=[block(*shape) for shape in shapes],
        ),
        out_shape=[jax.ShapeDtypeStruct(shape, bf16) for shape in shapes],
        compiler_params=vmem,
        cost_estimate=cost(0, 12 * tokens * width),
        name="assemble",
    )(core, *pieces, gain)


def store_partials(value, layout, half, refs):
    for (first, last, dtype), ref in zip(layout, refs):
        ref[...] = value[first * half : last * half, :].astype(dtype)


def partial_specs(layout, half, width, columns):
    specs = [block((b - a) * half, columns, at=lambda j: (0, j)) for a, b, _ in layout]
    shapes = [jax.ShapeDtypeStruct(((b - a) * half, width), dtype) for a, b, dtype in layout]
    return specs, shapes


def partial_kernel(layout, half, cuts, left_ref, *refs):
    weights, outs = (refs[: len(cuts)], refs[len(cuts) :])
    total = None
    for (first, last), ref in zip(cuts, weights):
        term = matmul(left_ref[:, first:last], ref[...], 1, 1)
        total = term if total is None else total + term
    store_partials(total, layout, half, outs)


def ordered_kernel(half, places_ref, left_ref, weight_ref, out_ref):
    total = matmul(left_ref[...], weight_ref[...], 1, 1).astype(bf16)
    for slot in range(left_ref.shape[0] // half):
        to = pl.multiple_of(places_ref[slot] * half, half)
        out_ref[pl.ds(to, half), :] = total[slot * half : (slot + 1) * half, :]


def exchanged_product(left, weight, places, half, columns=256):
    tokens, depth = left.shape
    width = weight.shape[0]
    ranks = lax.axis_size("seq")
    partial = pl.pallas_call(
        functools.partial(ordered_kernel, half),
        grid_spec=pltpu.PrefetchScalarGridSpec(
            num_scalar_prefetch=1,
            grid=(width // columns,),
            in_specs=[block(tokens, depth), block(columns, depth, at=lambda j, p: (j, 0))],
            out_specs=block(tokens, columns, at=lambda j, p: (0, j)),
        ),
        out_shape=jax.ShapeDtypeStruct((tokens, width), bf16),
        compiler_params=vmem,
        cost_estimate=cost(3 * tokens * depth * width),
        name="exchanged_product",
    )(places, left, weight)
    return partial.reshape(ranks, 2 * half, width)


def partial_product(left, weights, widths, half, columns=256):
    tokens, depth = left.shape
    width = weights[0].shape[0]
    layout = partial_layout(tokens)
    specs, shapes = partial_specs(layout, half, width, columns)
    cuts = [(sum(widths[:i]), sum(widths[: i + 1])) for i in range(len(widths))]
    return pl.pallas_call(
        functools.partial(partial_kernel, layout, half, cuts),
        grid=(width // columns,),
        in_specs=[block(tokens, depth)]
        + [block(columns, size, at=lambda j: (j, 0)) for size in widths],
        out_specs=specs,
        out_shape=shapes,
        compiler_params=vmem,
        cost_estimate=cost(3 * tokens * depth * width),
        name="partial_product",
    )(left, *weights)


def gate_out_kernel(layout, half, mixed_ref, outgate_pre_ref, out_ref, gated_ref, *outs):
    @pl.when(pl.program_id(0) == 0)
    def _():
        for h in range(mixed_ref.shape[1] // HEAD_FEATURES):
            cols = slice(h * HEAD_FEATURES, (h + 1) * HEAD_FEATURES)
            mixed, gate = mixed_ref[:, cols], outgate_pre_ref[:, cols]
            factor = lax.rsqrt(jnp.mean(mixed * mixed, axis=-1, keepdims=True) + eps_group)
            gated_ref[:, cols] = (mixed * factor * (gate * jax.nn.sigmoid(gate))).astype(bf16)

    store_partials(matmul(gated_ref[...], out_ref[...]), layout, half, outs)


def gate_out(mixed, pre, out_rows, half):
    tokens, my_width = mixed.shape
    width = out_rows.shape[1]
    layout = partial_layout(tokens)
    specs, shapes = partial_specs(layout, half, width, my_width)
    gated, *partials = pl.pallas_call(
        functools.partial(gate_out_kernel, layout, half),
        grid=(width // my_width,),
        in_specs=[
            block(tokens, my_width),
            block(tokens, my_width, at=lambda j: (0, 3)),
            block(my_width, my_width, at=lambda j: (0, j)),
        ],
        out_specs=[block(tokens, my_width)] + specs,
        out_shape=[jax.ShapeDtypeStruct((tokens, my_width), bf16)] + shapes,
        compiler_params=vmem,
        cost_estimate=cost(3 * tokens * my_width * width, 16 * tokens * width),
        name="gate_out",
    )(mixed, pre, out_rows)
    return gated, partials


def gated_grad_kernel(places, half, *refs):
    *pieces, out_ref, all_ref, grad_ref = refs
    for slot, (piece, row) in enumerate(places):
        all_ref[slot * half : (slot + 1) * half, :] = pieces[piece][row : row + half, :]
    grad_ref[...] = matmul(all_ref[...], out_ref[...], 1, 1)


def gated_gradient(gathered, out_rows, half):
    pieces, places = gathered
    my_width, width = out_rows.shape
    tokens = half * len(places)
    return pl.pallas_call(
        functools.partial(gated_grad_kernel, places, half),
        grid=(1,),
        in_specs=[block(*piece.shape) for piece in pieces] + [block(my_width, width)],
        out_specs=[block(tokens, width), block(tokens, my_width)],
        out_shape=[
            jax.ShapeDtypeStruct((tokens, width), bf16),
            jax.ShapeDtypeStruct((tokens, my_width), f32),
        ],
        compiler_params=vmem,
        cost_estimate=cost(3 * tokens * width * my_width),
        name="gated_gradient",
    )(*pieces, out_rows)


def ffn_forward_kernel(places, half, *refs):
    *pieces, weight_ref, both_ref, hidden_ref, all_ref = refs

    @pl.when(pl.program_id(0) == 0)
    def _():
        for slot, (piece, row) in enumerate(places):
            rows = slice(slot * half, (slot + 1) * half)
            all_ref[rows, :] = pieces[piece][row : row + half, :]

    both = matmul(all_ref[...], weight_ref[...])
    both_ref[...] = both
    gate, up = (both[:, :LANES], both[:, LANES:])
    hidden_ref[...] = (gate * jax.nn.sigmoid(gate) * up).astype(bf16)


def ffn_forward(gathered, ffn_cols, half):
    pieces, places = gathered
    width, total = ffn_cols.shape
    tokens = half * len(places)
    if (total // 2) % LANES:
        (rows,) = pieces
        both = matmul(rows, ffn_cols)
        gate, up = (both[:, : total // 2], both[:, total // 2 :])
        return both, (jax.nn.silu(gate) * up).astype(bf16), rows
    return pl.pallas_call(
        functools.partial(ffn_forward_kernel, places, half),
        grid=(total // (2 * LANES),),
        in_specs=[block(*piece.shape) for piece in pieces]
        + [block(width, 2 * LANES, at=lambda j: (0, j))],
        out_specs=[
            block(tokens, 2 * LANES, at=lambda j: (0, j)),
            block(tokens, LANES, at=lambda j: (0, j)),
            block(tokens, width),
        ],
        out_shape=[
            jax.ShapeDtypeStruct((tokens, total), f32),
            jax.ShapeDtypeStruct((tokens, total // 2), bf16),
            jax.ShapeDtypeStruct((tokens, width), bf16),
        ],
        compiler_params=vmem,
        cost_estimate=cost(3 * tokens * width * total),
        name="ffn_forward",
    )(*pieces, ffn_cols)


def ffn_backward_kernel(cotangent_ref, weight_ref, both_ref, grads_ref):
    hidden_grad = matmul(cotangent_ref[...], weight_ref[...])
    for j in range(hidden_grad.shape[1] // LANES):
        grad = hidden_grad[:, j * LANES : (j + 1) * LANES]
        gate = both_ref[:, 2 * j * LANES : (2 * j + 1) * LANES]
        up = both_ref[:, (2 * j + 1) * LANES : (2 * j + 2) * LANES]
        sig = jax.nn.sigmoid(gate)
        slope = sig * (1.0 + gate * (1.0 - sig))
        grads_ref[:, 2 * j * LANES : (2 * j + 1) * LANES] = (grad * up * slope).astype(bf16)
        grads_ref[:, (2 * j + 1) * LANES : (2 * j + 2) * LANES] = (grad * (gate * sig)).astype(bf16)


def ffn_backward(cotangent_all, down_cols, both):
    tokens, width = cotangent_all.shape
    mine = down_cols.shape[1]
    if mine % LANES:
        gate, up = (both[:, :mine], both[:, mine:])
        hidden_grad = matmul(cotangent_all, down_cols)
        sig = jax.nn.sigmoid(gate)
        gate_grad = hidden_grad * up * (sig * (1.0 + gate * (1.0 - sig)))
        up_grad = hidden_grad * (gate * sig)
        return jnp.concatenate((gate_grad, up_grad), axis=1).astype(bf16)
    size = 2 * LANES
    return pl.pallas_call(
        ffn_backward_kernel,
        grid=(pl.cdiv(mine, size),),
        in_specs=[
            block(tokens, width),
            block(width, size, at=lambda j: (0, j)),
            block(tokens, 2 * size, at=lambda j: (0, j)),
        ],
        out_specs=block(tokens, 2 * size, at=lambda j: (0, j)),
        out_shape=jax.ShapeDtypeStruct((tokens, 2 * mine), bf16),
        compiler_params=vmem,
        cost_estimate=cost(4 * tokens * width * mine),
        name="ffn_backward",
    )(cotangent_all, down_cols, both)


def add_up(parts):
    if len(parts) == 1 and len(parts[0].shape) == 3:
        return jnp.sum(parts[0][...].astype(f32), axis=0)
    if len(parts) == 1:
        return parts[0][...]
    rest, near, far, across, along = parts
    top = near[...].astype(f32) + across[...].astype(f32)
    low = far[...].astype(f32) + along[...].astype(f32)
    return rest[...] + jnp.where(pl.program_id(0) == 0, top, low)


def combine_kernel(post, count, given, *refs):
    parts, values, outs = (refs[:count], refs[count : count + given], refs[count + given :])
    results = post(add_up(parts), *(ref[...].astype(f32) for ref in values))
    for result, ref in zip(results, outs):
        ref[...] = result.astype(ref.dtype)


def combine(post, parts, values, dtypes, half):
    width = parts[0].shape[-1]
    mine = block(half, width, at=lambda h: (h, 0))
    fixed = block(half, width)
    part_specs = [mine] if len(parts) == 1 else [mine] + [fixed] * 4
    if parts[0].ndim == 3:
        part_specs = [block(parts[0].shape[0], half, width, at=lambda h: (0, h, 0))]
    value_specs = [block(1, width) if v.shape[0] == 1 else mine for v in values]
    return pl.pallas_call(
        functools.partial(combine_kernel, post, len(parts), len(values)),
        grid=(2,),
        in_specs=part_specs + value_specs,
        out_specs=[mine] * len(dtypes),
        out_shape=[jax.ShapeDtypeStruct((2 * half, width), dtype) for dtype in dtypes],
        compiler_params=vmem,
        cost_estimate=cost(0, 60 * half * width),
        name="combine",
    )(*parts, *values)


def residual(branch, inputs, gain):
    resid = inputs + branch
    return resid, resid * rms_factor(resid) * gain


def residual_back(mid_grad, cotangent, resid, gain):
    factor = rms_factor(resid)
    grad = cotangent + rms_back(mid_grad * gain, resid * factor, factor)
    return grad, grad


def input_back(in_grad, resid_grad, inputs, gain):
    factor = rms_factor(inputs)
    return (resid_grad + rms_back(in_grad * gain, inputs * factor, factor),)


def local(
    layer_input,
    segment_ids,
    mix_gain,
    bound_logit,
    query_weight,
    forget_weight,
    input_weight,
    output_gate_weight,
    output_weight,
    ffn_gain,
    ffn_gate_weight,
    ffn_up_weight,
    ffn_down_weight,
    output_cotangent,
):
    rows, length, width = layer_input.shape
    ranks, rank = (lax.axis_size("seq"), lax.axis_index("seq"))
    count = lax.axis_size("dp")
    my_width = width // ranks
    tokens = rows * length
    half = tokens // 2
    my_rows = mix_gain.shape[0]
    rank_rows = my_rows * ranks
    x_low = layer_input.reshape(tokens, width)
    cotangent_low = output_cotangent.reshape(tokens, width)
    core = (lax.axis_index("dp") & 1).reshape(1)

    mix_weights = [query_weight, forget_weight, input_weight, output_gate_weight]
    mix_pieces = swap_seq(column_pieces(mix_weights))
    mix_cols = gather_dp(mix_pieces.reshape(rank_rows, 4 * my_width))
    ffn_width = 2 * ffn_gate_weight.shape[1] // ranks
    ffn_pieces = column_pieces([after(ffn_gate_weight, mix_pieces), ffn_up_weight], True)
    down_pieces = column_pieces([ffn_down_weight])
    ffn_pieces = swap_seq(jnp.concatenate((ffn_pieces, down_pieces), axis=2))
    x_pieces, places = gather_seq(after(x_low, ffn_pieces))
    vectors = jnp.stack((mix_gain, bound_logit, ffn_gain), axis=1)
    vectors = gather_small(gather_small(vectors, "seq"), "dp").astype(f32)
    gain_in, logit, gain_mid = (vectors[:, 0], vectors[:, 1], vectors[:, 2])
    gain_in, gain_mid = (gain_in[None, :], gain_mid[None, :])
    segments = gather_small(segment_ids[0], "seq")
    table = slot_table()
    bound = jax.nn.sigmoid(-lax.dynamic_slice_in_dim(logit, rank * my_width, my_width))[None, :]
    normed_in, in_mine, in_theirs = assemble(
        (x_pieces, places), core, rank_rows, after(gain_in, segments, bound)
    )
    out_piece = lax.ppermute(output_weight, ("dp", "seq"), row_route())
    out_rows = gather_dp(after(out_piece, normed_in))
    ffn_cols = gather_dp(after(ffn_pieces[:, :, :ffn_width].reshape(rank_rows, ffn_width), out_piece))
    down_pieces = ffn_pieces[:, :, ffn_width:].reshape(rank_rows, ffn_width // 2)

    pre = dense(normed_in, mix_cols, f32, parts=4)
    down_cols = gather_dp(after(down_pieces, pre))
    mixed, states = recurrence_forward(segments, table, pre, bound)
    gated, partials = gate_out(mixed, pre, out_rows, half)
    cotangent = gather_seq(after(cotangent_low, normed_in))
    branch_parts = scatter_seq(partials, half)
    cotangent_all, cotangent_mine, cotangent_theirs = assemble(cotangent, core, rank_rows)
    resid, normed_low = combine(
        residual, branch_parts, (after(x_low, cotangent_all), gain_mid), (f32, bf16), half
    )
    normed_mid = gather_seq(normed_low)

    both, hidden, mid_all = ffn_forward(normed_mid, ffn_cols, half)

    down_theirs = flip(dense(cotangent_theirs, hidden, bf16, 0), "dp", 1)
    down_sum = dense(cotangent_mine, hidden, bf16, 0, down_theirs)
    down_mine = scatter_dp(down_sum)
    cotangent_all = after(cotangent_all, down_sum)
    ffn_right = ffn_backward(cotangent_all, down_cols, both)
    mid_partials = partial_product(ffn_right, [ffn_cols], [ffn_cols.shape[1]], half)
    ffn_sum = dense(mid_all, after(ffn_right, mid_partials[0]), bf16, 0)
    mid_parts = scatter_seq(mid_partials, half, beside=(ffn_sum, down_mine))
    ffn_mine = lax.psum_scatter(after(ffn_sum, *mid_parts[:3]), "dp", scatter_dimension=0, tiled=True)

    resid_grad, branch_own = combine(
        residual_back, mid_parts, (cotangent_low, resid, gain_mid), (f32, bf16), half
    )
    branch, places = gather_seq(branch_own)
    row_place = row_places()
    out_partial = exchanged_product(after(hidden, branch_own), down_cols, row_place, half)
    branch = (after(branch[0], out_partial),) + branch[1:]
    branch_low, gated_grad = gated_gradient((branch, places), out_rows, half)
    out_parts = swap_seq(after(out_partial, branch_low))
    mix_right, logit_part = recurrence_backward(segments, table, pre, bound, mixed, gated_grad, states)
    mix_theirs = dense(in_theirs, mix_right, bf16, 0)
    out_sum = dense(gated, after(branch_low, mix_theirs, out_parts), bf16, 0)
    out_sum = out_sum.reshape(count // 2, 2, my_rows, width)
    out_theirs = flip(lax.dynamic_index_in_dim(out_sum, 1 - core[0], 1, keepdims=False), "dp", 1)
    mix_sum = mixer_sums(in_mine, mix_right, flip(mix_theirs, "dp", 1), out_sum, out_theirs, core)
    mix_mine = scatter_dp(mix_sum)
    down_back = swap_columns(after(down_mine, mix_sum))
    ffn_back = swap_columns(after(ffn_mine, down_back))
    in_partial = exchanged_product(after(mix_right, mix_sum), mix_cols, row_place, half)
    in_parts = swap_seq(after(in_partial, ffn_back))
    (block_output,) = combine(
        lambda total, resid: (resid + total,), (out_parts,), (after(resid, in_partial),), (bf16,), half
    )
    (ffn_gate_weight_grad, ffn_up_weight_grad), ffn_sums = return_columns(
        after(ffn_back, in_partial), [ffn_gate_weight, ffn_up_weight], True
    )
    (input_grad,) = combine(input_back, (in_parts,), (resid_grad, x_low, gain_in), (f32,), half)
    (ffn_down_weight_grad,), _ = return_columns(after(down_back, in_partial), [ffn_down_weight])

    logit_sum = gather_small(sum_small(-after(logit_part, in_partial)[0] * (1.0 - bound[0]), "dp"), "seq")
    at = (lax.axis_index("dp") * ranks + rank) * my_rows
    bound_logit_grad = lax.dynamic_slice_in_dim(logit_sum, at, my_rows)
    mix_mine = after(mix_mine, in_parts)
    mix_grads, mix_sums = return_columns(swap_columns(mix_mine[:, : 4 * my_width]), mix_weights)
    out_mine = mix_mine[:, 4 * my_width :].reshape(ranks, my_rows, my_width)
    out_mine = lax.ppermute(out_mine, ("dp", "seq"), [(b, a) for a, b in row_route()])
    output_weight_grad = jnp.moveaxis(out_mine, 0, 1).reshape(my_rows, width).astype(f32)
    query_weight_grad, forget_weight_grad, input_weight_grad, output_gate_weight_grad = mix_grads
    mix_gain_grad = mix_sums / mix_gain.astype(f32)
    ffn_gain_grad = ffn_sums / ffn_gain.astype(f32)
    return (
        block_output.reshape(rows, length, width),
        input_grad.reshape(rows, length, width),
        mix_gain_grad,
        bound_logit_grad,
        query_weight_grad,
        forget_weight_grad,
        input_weight_grad,
        output_gate_weight_grad,
        output_weight_grad,
        ffn_gain_grad,
        ffn_gate_weight_grad,
        ffn_up_weight_grad,
        ffn_down_weight_grad,
    )


def solution(mesh):
    by_token = P("dp", "seq", None)
    vector = P(("dp", "seq"))
    matrix = P(("dp", "seq"), None)
    return jax.shard_map(
        local,
        mesh=mesh,
        in_specs=(by_token, P("dp", "seq"), vector, vector)
        + (matrix,) * 5
        + (vector,)
        + (matrix,) * 3
        + (by_token,),
        out_specs=(by_token, by_token, vector, vector) + (matrix,) * 5 + (vector,) + (matrix,) * 3,
        check_vma=False,
    )
```

```python
import functools

import jax
import jax.numpy as jnp
from jax import lax
from jax.experimental import pallas as pl
from jax.experimental.pallas import tpu as pltpu
from jax.sharding import PartitionSpec as P

HEAD_FEATURES = 128
LANES = 128

eps_model = 1e-06
eps_group = 1e-05
f32 = jnp.float32
bf16 = jnp.bfloat16

vmem = pltpu.CompilerParams(vmem_limit_bytes=48 * 1024 * 1024)


def cost(flops, moved=0):
    return pl.CostEstimate(flops=flops, bytes_accessed=moved, transcendentals=0)


def flip(block, axis, bits):
    return lax.ppermute(block, axis, [(i, i ^ bits) for i in range(lax.axis_size(axis))])


def gather_small(block, axis):
    count, mine = (lax.axis_size(axis), lax.axis_index(axis))
    bit = 1
    while bit < count:
        other = flip(block, axis, bit)
        upper = (mine & bit) != 0
        block = jnp.concatenate(
            (jnp.where(upper, other, block), jnp.where(upper, block, other)), axis=0
        )
        bit *= 2
    return block


def sum_small(block, axis):
    others = [flip(block, axis, bits) for bits in range(1, lax.axis_size(axis))]
    return functools.reduce(jnp.add, others, block)


def slots():
    if lax.axis_size("seq") == 4:
        return [(1, 0), (3, 0), (2, 1), (3, 1), (0, 0), (0, 1), (2, 0), (1, 1)]
    return [(k, h) for k in range(lax.axis_size("seq")) for h in range(2)]


def slot_table():
    place = {slot: i for i, slot in enumerate(slots())}
    count = lax.axis_size("seq")
    table = jnp.array([[place[k, h] for h in range(2)] for k in range(count)], jnp.int32)
    return table[jnp.arange(count) ^ lax.axis_index("seq")].reshape(2 * count)


def row_places():
    k, h = (jnp.array(bits, jnp.int32) for bits in zip(*slots()))
    return (k ^ lax.axis_index("seq")) * 2 + h


def gather_seq(block, second=()):
    count = lax.axis_size("seq")
    half = block.shape[0] // 2
    if count == 4:
        near = flip(block, "seq", 1)
        far = flip(block, "seq", 2)
        corner_top = flip(after(near[:half], *second), "seq", 2)
        corner_low = flip(after(far[half:], *second), "seq", 1)
        found = {(3, 0): (3, 0), (3, 1): (4, 0)}
        for k in range(3):
            found[k, 0], found[k, 1] = ((k, 0), (k, half))
        return (block, near, far, corner_top, corner_low), [found[slot] for slot in slots()]
    bit = 1
    while bit < count:
        block = jnp.concatenate((block, flip(block, "seq", bit)), axis=0)
        bit *= 2
    return (block,), [(0, i * half) for i in range(2 * count)]


def partial_layout(tokens):
    count = lax.axis_size("seq")
    if count == 4:
        return [(0, 2, bf16), (2, 4, bf16), (4, 8, f32)]
    return [(0, 2 * count, f32)]


def scatter_seq(partials, half, beside=()):
    if len(partials) == 3:
        near, far, rest = partials
        near = flip(near, "seq", 1)
        far = flip(far, "seq", 2)
        rest = after(rest, *beside)
        across = (rest[2 * half : 3 * half] + near[half:].astype(f32)).astype(bf16)
        along = (rest[3 * half :] + far[half:].astype(f32)).astype(bf16)
        return (rest, near, far, flip(across, "seq", 2), flip(along, "seq", 1))
    (total,) = partials
    bit = lax.axis_size("seq") // 2
    while bit:
        middle = total.shape[0] // 2
        total = total[:middle] + flip(total[middle:].astype(bf16), "seq", bit).astype(f32)
        bit //= 2
    return (total,)


def swap_seq(pieces):
    return lax.all_to_all(pieces, "seq", split_axis=0, concat_axis=0, tiled=True)


def gather_dp(block):
    return lax.all_gather(block, "dp", axis=0, tiled=True)


def scatter_dp(mine):
    groups = [list(range(c, lax.axis_size("dp"), 2)) for c in range(2)]
    return lax.psum_scatter(
        mine, "dp", scatter_dimension=0, axis_index_groups=groups, tiled=True
    )


def row_route():
    count, ranks = (lax.axis_size("dp"), lax.axis_size("seq"))
    return [(b, (b % count) * ranks + b // count) for b in range(count * ranks)]


def after(value, *others):
    return lax.optimization_barrier((value,) + others)[0]


def block(*shape, at=None):
    return pl.BlockSpec(shape, at or (lambda *_: (0,) * len(shape)))


def column_blocks(width, interleave):
    size = LANES if interleave else width
    return [(j * size, size) for j in range(width // size)]


def pieces_kernel(interleave, *refs):
    weights, out_ref = (refs[:-1], refs[-1])
    blocks = column_blocks(weights[0].shape[1], interleave)
    at = 0
    for start, size in blocks:
        for ref in weights:
            out_ref[0, :, at : at + size] = ref[:, start : start + size]
            at += size


def column_pieces(weights, interleave=False):
    ranks = lax.axis_size("seq")
    rows, width = (weights[0].shape[0], weights[0].shape[1] // ranks)
    if width % LANES:
        parts = [jnp.moveaxis(w.reshape(rows, ranks, width), 1, 0) for w in weights]
        return jnp.concatenate(parts, axis=2)
    total = width * len(weights)
    return pl.pallas_call(
        functools.partial(pieces_kernel, interleave),
        grid=(ranks,),
        in_specs=[block(rows, width, at=lambda r: (0, r)) for _ in weights],
        out_specs=block(1, rows, total, at=lambda r: (r, 0, 0)),
        out_shape=jax.ShapeDtypeStruct((ranks, rows, total), bf16),
        compiler_params=vmem,
        cost_estimate=cost(0, 4 * rows * total * ranks),
        name="column_pieces",
    )(*weights)


def return_kernel(interleave, count, *refs):
    pieces_ref, weights, grads, (gain_ref,) = (
        refs[0],
        refs[1 : 1 + count],
        refs[1 + count : 1 + 2 * count],
        refs[1 + 2 * count :],
    )

    @pl.when(pl.program_id(0) == 0)
    def _():
        gain_ref[...] = jnp.zeros_like(gain_ref)

    at = 0
    total = jnp.zeros(gain_ref.shape, f32)
    for start, size in column_blocks(weights[0].shape[1], interleave):
        for weight_ref, grad_ref in zip(weights, grads):
            grad = pieces_ref[0, :, at : at + size].astype(f32)
            grad_ref[:, start : start + size] = grad
            weight = weight_ref[:, start : start + size].astype(f32)
            total += jnp.sum(weight * grad, axis=1, keepdims=True)
            at += size
    gain_ref[...] += total


def swap_columns(mine):
    ranks = lax.axis_size("seq")
    return swap_seq(mine.reshape(ranks, mine.shape[0] // ranks, mine.shape[1]))


def return_columns(pieces, weights, interleave=False):
    ranks, rows, total = pieces.shape
    width = weights[0].shape[1] // ranks
    if width % LANES:
        grads = [
            jnp.moveaxis(pieces[:, :, i * width : (i + 1) * width], 0, 1)
            .reshape(rows, ranks * width)
            .astype(f32)
            for i in range(len(weights))
        ]
        return grads, sum(jnp.sum(w.astype(f32) * g, axis=1) for w, g in zip(weights, grads))
    columns = block(rows, width, at=lambda r: (0, r))
    *grads, sums = pl.pallas_call(
        functools.partial(return_kernel, interleave, len(weights)),
        grid=(ranks,),
        in_specs=[block(1, rows, total, at=lambda r: (r, 0, 0))] + [columns] * len(weights),
        out_specs=[columns] * len(weights) + [block(rows, 1)],
        out_shape=[jax.ShapeDtypeStruct(w.shape, f32) for w in weights]
        + [jax.ShapeDtypeStruct((rows, 1), f32)],
        compiler_params=vmem,
        cost_estimate=cost(0, 8 * rows * total * ranks),
        name="return_columns",
    )(pieces, *weights)
    return grads, sums[:, 0]


def sums(mask, terms):
    high = terms.astype(bf16)
    low = (terms - high.astype(f32)).astype(bf16)
    ones = mask.astype(bf16)
    return matmul(ones, low) + matmul(ones, high)


def product(left, right, left_dim, right_dim):
    left_high, right_high = (left.astype(bf16), right.astype(bf16))
    left_low = (left - left_high.astype(f32)).astype(bf16)
    right_low = (right - right_high.astype(f32)).astype(bf16)
    return (
        matmul(left_high, right_low, left_dim, right_dim)
        + matmul(left_low, right_high, left_dim, right_dim)
        + matmul(left_high, right_high, left_dim, right_dim)
    )


def chunk_parts(chunk, seg_ref, seg_col_ref, seg_row_ref, pre_ref, bound_ref):
    size, wide = pre_ref.shape
    width = wide // 3
    first = chunk * size
    prior = seg_ref[jnp.maximum(first - 1, 0)]
    last = seg_ref[first + size - 1]
    seg_col = seg_col_ref[...]
    at = lax.broadcasted_iota(jnp.int32, (size, size), 0)
    of = lax.broadcasted_iota(jnp.int32, (size, size), 1)
    seen = (seg_col == seg_row_ref[...]) & (at >= of)
    linked = (seg_col == prior).astype(f32)
    tail = (seg_col == last).astype(f32)
    linked_last = (prior == last).astype(f32)
    query_pre = pre_ref[:, 0:width]
    forget_pre = pre_ref[:, width : 2 * width]
    value = pre_ref[:, 2 * width : 3 * width]
    forget_sig = jax.nn.sigmoid(-forget_pre)
    key = bound_ref[...] * forget_sig
    query_sig = jax.nn.sigmoid(query_pre)
    lower = (at >= of).astype(f32)
    cumul = sums(lower, jnp.log1p(-key))
    grow = jnp.exp(cumul)
    shrink = jnp.exp(-cumul)
    end = grow[size - 1 :, :]
    query_d = query_pre * query_sig * grow
    key_d = key * shrink
    key_t = key_d * end * tail
    keep = end * linked_last
    return locals()


def forward_kernel(seg_ref, slot_ref, seg_col_ref, seg_row_ref, pre_ref, bound_ref, mixed_ref, states_ref, state_ref):
    step = pl.program_id(0)
    heads = mixed_ref.shape[1] // HEAD_FEATURES

    @pl.when(step == 0)
    def _():
        state_ref[...] = jnp.zeros_like(state_ref)

    p = chunk_parts(step, seg_ref, seg_col_ref, seg_row_ref, pre_ref, bound_ref)
    for h in range(heads):
        cols = slice(h * HEAD_FEATURES, (h + 1) * HEAD_FEATURES)
        query_d, key_d, value = p["query_d"][:, cols], p["key_d"][:, cols], p["value"][:, cols]
        state = state_ref[h]
        states_ref[0, h] = state
        scores = jnp.where(p["seen"], product(query_d, key_d, 1, 1), 0.0)
        mixed = product(scores, value, 1, 0) + product(query_d * p["linked"], state, 1, 1)
        mixed_ref[:, cols] = mixed
        state_ref[h] = state * p["keep"][:, cols] + product(value, p["key_t"][:, cols], 0, 0)


def backward_kernel(seg_ref, slot_ref, seg_col_ref, seg_row_ref, pre_ref, bound_ref, outgate_pre_ref, mixed_ref, gated_grad_ref, states_ref, grads_ref, logit_ref, back_ref, through_ref):
    step = pl.program_id(0)
    chunk = pl.num_programs(0) - 1 - step
    width = mixed_ref.shape[1]
    heads = width // HEAD_FEATURES

    @pl.when(step == 0)
    def _():
        back_ref[...] = jnp.zeros_like(back_ref)
        through_ref[...] = jnp.zeros_like(through_ref)
        logit_ref[...] = jnp.zeros_like(logit_ref)

    p = chunk_parts(chunk, seg_ref, seg_col_ref, seg_row_ref, pre_ref, bound_ref)
    query_pre, query_sig = p["query_pre"], p["query_sig"]
    upper = (p["at"] <= p["of"]).astype(f32)
    for h in range(heads):
        cols = slice(h * HEAD_FEATURES, (h + 1) * HEAD_FEATURES)
        query_d, key_d, key_t, value = (p[k][:, cols] for k in ("query_d", "key_d", "key_t", "value"))
        grow, shrink, end, keep, key = (p[k][:, cols] for k in ("grow", "shrink", "end", "keep", "key"))
        state = states_ref[0, h]
        back = back_ref[h]
        mixed = mixed_ref[:, cols]
        factor = lax.rsqrt(jnp.mean(mixed * mixed, axis=-1, keepdims=True) + eps_group)
        normed = mixed * factor
        gated_grad = gated_grad_ref[:, cols]
        gate = outgate_pre_ref[:, cols]
        gate_sig = jax.nn.sigmoid(gate)
        outgate_grad = gated_grad * normed * (gate_sig * (1.0 + gate * (1.0 - gate_sig)))
        weighted = gated_grad * (gate * gate_sig)
        mixed_grad = factor * (
            weighted - normed * jnp.mean(weighted * normed, axis=-1, keepdims=True)
        )
        scores = jnp.where(p["seen"], product(query_d, key_d, 1, 1), 0.0)
        scores_grad = jnp.where(p["seen"], product(mixed_grad, value, 1, 1), 0.0)
        value_grad = product(scores, mixed_grad, 0, 0) + product(key_t, back, 1, 1)
        query_d_grad = product(scores_grad, key_d, 1, 0) + p["linked"] * product(mixed_grad, state, 1, 0)
        key_d_grad = product(scores_grad, query_d, 0, 0)
        key_t_grad = product(value, back, 1, 0)
        key_grad = key_d_grad * shrink + (p["tail"] * end * shrink) * key_t_grad
        change = query_d * query_d_grad - key_d * key_d_grad - key_t * key_t_grad
        through = sums(upper, change) + through_ref[:, cols]
        key_total = key_grad - through / (1.0 - key)
        new_back = back * keep + product(mixed_grad, query_d * p["linked"], 0, 0)
        back_ref[h] = new_back
        through_ref[:, cols] = jnp.sum(new_back * state, axis=0, keepdims=True)
        sig = query_sig[:, cols]
        query_grad = query_d_grad * grow * (sig * (1.0 + query_pre[:, cols] * (1.0 - sig)))
        weighted_key = key_total * key
        forget_grad = -weighted_key * (1.0 - p["forget_sig"][:, cols])
        logit_ref[:, cols] += jnp.sum(weighted_key, axis=0, keepdims=True)
        for part, grad in enumerate((query_grad, forget_grad, value_grad, outgate_grad)):
            lo = part * width + h * HEAD_FEATURES
            grads_ref[:, lo : lo + HEAD_FEATURES] = grad.astype(bf16)


def recurrence_forward(segments, table, pre, bound):
    tokens, wide = pre.shape
    steps = table.shape[0]
    size, width = (tokens // steps, wide // 4)
    heads = width // HEAD_FEATURES
    return pl.pallas_call(
        forward_kernel,
        grid_spec=pltpu.PrefetchScalarGridSpec(
            num_scalar_prefetch=2,
            grid=(steps,),
            in_specs=[
                pl.BlockSpec((size, 1), lambda i, s, t: (i, 0)),
                pl.BlockSpec((1, size), lambda i, s, t: (0, i)),
                pl.BlockSpec((size, 3 * width), lambda i, s, t: (t[i], 0)),
                pl.BlockSpec((1, width), lambda i, s, t: (0, 0)),
            ],
            out_specs=[
                pl.BlockSpec((size, width), lambda i, s, t: (t[i], 0)),
                pl.BlockSpec((1, heads, HEAD_FEATURES, HEAD_FEATURES), lambda i, s, t: (i, 0, 0, 0)),
            ],
            scratch_shapes=[pltpu.VMEM((heads, HEAD_FEATURES, HEAD_FEATURES), f32)],
        ),
        out_shape=[
            jax.ShapeDtypeStruct((tokens, width), f32),
            jax.ShapeDtypeStruct((steps, heads, HEAD_FEATURES, HEAD_FEATURES), f32),
        ],
        compiler_params=vmem,
        cost_estimate=cost(320 * tokens * width * HEAD_FEATURES),
        name="recurrence_forward",
    )(segments, table, segments[:, None], segments[None, :], pre, bound)


def recurrence_backward(segments, table, pre, bound, mixed, gated_grad, states):
    tokens, wide = pre.shape
    steps = table.shape[0]
    size, width = (tokens // steps, wide // 4)
    heads = width // HEAD_FEATURES
    tokens_block = pl.BlockSpec((size, width), lambda i, s, t: (t[steps - 1 - i], 0))
    return pl.pallas_call(
        backward_kernel,
        grid_spec=pltpu.PrefetchScalarGridSpec(
            num_scalar_prefetch=2,
            grid=(steps,),
            in_specs=[
                pl.BlockSpec((size, 1), lambda i, s, t: (steps - 1 - i, 0)),
                pl.BlockSpec((1, size), lambda i, s, t: (0, steps - 1 - i)),
                pl.BlockSpec((size, 3 * width), lambda i, s, t: (t[steps - 1 - i], 0)),
                pl.BlockSpec((1, width), lambda i, s, t: (0, 0)),
                pl.BlockSpec((size, width), lambda i, s, t: (t[steps - 1 - i], 3)),
                tokens_block,
                tokens_block,
                pl.BlockSpec(
                    (1, heads, HEAD_FEATURES, HEAD_FEATURES),
                    lambda i, s, t: (steps - 1 - i, 0, 0, 0),
                ),
            ],
            out_specs=[
                pl.BlockSpec((size, 4 * width), lambda i, s, t: (t[steps - 1 - i], 0)),
                pl.BlockSpec((1, width), lambda i, s, t: (0, 0)),
            ],
            scratch_shapes=[
                pltpu.VMEM((heads, HEAD_FEATURES, HEAD_FEATURES), f32),
                pltpu.VMEM((1, width), f32),
            ],
        ),
        out_shape=[
            jax.ShapeDtypeStruct((tokens, 4 * width), bf16),
            jax.ShapeDtypeStruct((1, width), f32),
        ],
        compiler_params=vmem,
        cost_estimate=cost(620 * tokens * width * HEAD_FEATURES),
        name="recurrence_backward",
    )(segments, table, segments[:, None], segments[None, :], pre, bound, pre, mixed, gated_grad, states)


def matmul(left, right, left_dim=1, right_dim=0):
    return lax.dot_general(
        left, right, (((left_dim,), (right_dim,)), ((), ())), preferred_element_type=f32
    )


def rms_factor(value):
    return lax.rsqrt(jnp.mean(value * value, axis=-1, keepdims=True) + eps_model)


def rms_back(grad_unit, unit, factor):
    return factor * (grad_unit - unit * jnp.mean(grad_unit * unit, axis=-1, keepdims=True))


def product_kernel(left_dim, *refs):
    left_ref, right_ref, *added, out_ref = refs
    total = matmul(left_ref[...], right_ref[...], left_dim, 0)
    for ref in added:
        total += ref[...].astype(f32)
    out_ref[...] = total.astype(out_ref.dtype)


def dense(left, right, dtype, left_dim=1, added=None, parts=2):
    height, width = (left.shape[1 - left_dim], right.shape[1])
    size = width // parts if (width // parts) % LANES == 0 else width
    columns = block(height, size, at=lambda j: (0, j))
    extra = [] if added is None else [added]
    return pl.pallas_call(
        functools.partial(product_kernel, left_dim),
        grid=(width // size,),
        in_specs=[block(*left.shape), block(right.shape[0], size, at=lambda j: (0, j))]
        + [columns] * len(extra),
        out_specs=columns,
        out_shape=jax.ShapeDtypeStruct((height, width), dtype),
        compiler_params=vmem,
        cost_estimate=cost(3 * left.shape[0] * left.shape[1] * width),
        name="dense",
    )(left, right, *extra)


def mixer_sums_kernel(count, rows, core_ref, left_ref, right_ref, theirs_ref, out_ref, out_theirs_ref, total_ref):
    step = pl.program_id(0)

    @pl.when(step < count)
    def _():
        total = matmul(left_ref[...], right_ref[...], 0, 0) + theirs_ref[...].astype(f32)
        total_ref[...] = total.astype(bf16)

    @pl.when(step == count)
    def _():
        width = total_ref.shape[1]
        for z in range(out_ref.shape[0]):
            both = (out_ref[z, 0].astype(f32) + out_theirs_ref[z].astype(f32)).astype(bf16)
            ranks = both.shape[1] // width
            for j in range(ranks):
                at = (z * ranks + j) * rows
                total_ref[at : at + rows, :] = both[:, j * width : (j + 1) * width]


def mixer_sums(left, right, theirs, out_sum, out_theirs, core):
    tokens, height = left.shape
    lines, cores, rows, width = out_sum.shape
    size = right.shape[1] // 4
    columns = block(height, size, at=lambda j, c: (0, jnp.minimum(j, 3)))
    return pl.pallas_call(
        functools.partial(mixer_sums_kernel, 4, rows),
        grid_spec=pltpu.PrefetchScalarGridSpec(
            num_scalar_prefetch=1,
            grid=(5,),
            in_specs=[
                block(tokens, height),
                block(tokens, size, at=lambda j, c: (0, jnp.minimum(j, 3))),
                columns,
                block(lines, 1, rows, width, at=lambda j, c: (0, c[0], 0, 0)),
                block(lines, rows, width),
            ],
            out_specs=block(height, size, at=lambda j, c: (0, j)),
        ),
        out_shape=jax.ShapeDtypeStruct((height, 5 * size), bf16),
        compiler_params=vmem,
        cost_estimate=cost(3 * tokens * height * 4 * size),
        name="mixer_sums",
    )(core, left, right, theirs, out_sum, out_theirs)


def store_halves(core, value, rows, row_block, mine_ref, theirs_ref):
    for z in range(value.shape[1] // (2 * row_block)):
        even = value[:, 2 * z * row_block : (2 * z + 1) * row_block]
        odd = value[:, (2 * z + 1) * row_block : (2 * z + 2) * row_block]
        to = slice(z * row_block, (z + 1) * row_block)

        @pl.when(core == 0)
        def _():
            mine_ref[rows, to] = even
            theirs_ref[rows, to] = odd

        @pl.when(core == 1)
        def _():
            mine_ref[rows, to] = odd
            theirs_ref[rows, to] = even


def assemble_kernel(places, half, row_block, normed, core_ref, *refs):
    *pieces, gain_ref, all_ref, mine_ref, theirs_ref = refs
    for slot, (piece, row) in enumerate(places):
        rows = slice(slot * half, (slot + 1) * half)
        value = pieces[piece][row : row + half, :]
        if normed:
            wide = value.astype(f32)
            value = (wide * rms_factor(wide) * gain_ref[...]).astype(bf16)
        all_ref[rows, :] = value
        store_halves(core_ref[0], value, rows, row_block, mine_ref, theirs_ref)


def assemble(gathered, core, row_block, gain=None):
    pieces, places = gathered
    half = pieces[0].shape[0] // 2 if len(pieces) > 1 else pieces[0].shape[0] // len(places)
    tokens, width = (half * len(places), pieces[0].shape[1])
    normed = gain is not None
    gain = gain if normed else jnp.zeros((1, width), f32)
    shapes = [(tokens, width), (tokens, width // 2), (tokens, width // 2)]
    return pl.pallas_call(
        functools.partial(assemble_kernel, places, half, row_block, normed),
        grid_spec=pltpu.PrefetchScalarGridSpec(
            num_scalar_prefetch=1,
            grid=(1,),
            in_specs=[block(*piece.shape) for piece in pieces] + [block(1, width)],
            out_specs=[block(*shape) for shape in shapes],
        ),
        out_shape=[jax.ShapeDtypeStruct(shape, bf16) for shape in shapes],
        compiler_params=vmem,
        cost_estimate=cost(0, 12 * tokens * width),
        name="assemble",
    )(core, *pieces, gain)


def store_partials(value, layout, half, refs):
    for (first, last, dtype), ref in zip(layout, refs):
        ref[...] = value[first * half : last * half, :].astype(dtype)


def partial_specs(layout, half, width, columns):
    specs = [block((b - a) * half, columns, at=lambda j: (0, j)) for a, b, _ in layout]
    shapes = [jax.ShapeDtypeStruct(((b - a) * half, width), dtype) for a, b, dtype in layout]
    return specs, shapes


def partial_kernel(layout, half, cuts, left_ref, *refs):
    weights, outs = (refs[: len(cuts)], refs[len(cuts) :])
    total = None
    for (first, last), ref in zip(cuts, weights):
        term = matmul(left_ref[:, first:last], ref[...], 1, 1)
        total = term if total is None else total + term
    store_partials(total, layout, half, outs)


def ordered_kernel(half, places_ref, left_ref, weight_ref, out_ref):
    total = matmul(left_ref[...], weight_ref[...], 1, 1).astype(bf16)
    for slot in range(left_ref.shape[0] // half):
        to = pl.multiple_of(places_ref[slot] * half, half)
        out_ref[pl.ds(to, half), :] = total[slot * half : (slot + 1) * half, :]


def exchanged_product(left, weight, places, half, columns=256):
    tokens, depth = left.shape
    width = weight.shape[0]
    ranks = lax.axis_size("seq")
    partial = pl.pallas_call(
        functools.partial(ordered_kernel, half),
        grid_spec=pltpu.PrefetchScalarGridSpec(
            num_scalar_prefetch=1,
            grid=(width // columns,),
            in_specs=[block(tokens, depth), block(columns, depth, at=lambda j, p: (j, 0))],
            out_specs=block(tokens, columns, at=lambda j, p: (0, j)),
        ),
        out_shape=jax.ShapeDtypeStruct((tokens, width), bf16),
        compiler_params=vmem,
        cost_estimate=cost(3 * tokens * depth * width),
        name="exchanged_product",
    )(places, left, weight)
    return partial.reshape(ranks, 2 * half, width)


def partial_product(left, weights, widths, half, columns=256):
    tokens, depth = left.shape
    width = weights[0].shape[0]
    layout = partial_layout(tokens)
    specs, shapes = partial_specs(layout, half, width, columns)
    cuts = [(sum(widths[:i]), sum(widths[: i + 1])) for i in range(len(widths))]
    return pl.pallas_call(
        functools.partial(partial_kernel, layout, half, cuts),
        grid=(width // columns,),
        in_specs=[block(tokens, depth)]
        + [block(columns, size, at=lambda j: (j, 0)) for size in widths],
        out_specs=specs,
        out_shape=shapes,
        compiler_params=vmem,
        cost_estimate=cost(3 * tokens * depth * width),
        name="partial_product",
    )(left, *weights)


def gate_out_kernel(layout, half, mixed_ref, outgate_pre_ref, out_ref, gated_ref, *outs):
    @pl.when(pl.program_id(0) == 0)
    def _():
        for h in range(mixed_ref.shape[1] // HEAD_FEATURES):
            cols = slice(h * HEAD_FEATURES, (h + 1) * HEAD_FEATURES)
            mixed, gate = mixed_ref[:, cols], outgate_pre_ref[:, cols]
            factor = lax.rsqrt(jnp.mean(mixed * mixed, axis=-1, keepdims=True) + eps_group)
            gated_ref[:, cols] = (mixed * factor * (gate * jax.nn.sigmoid(gate))).astype(bf16)

    store_partials(matmul(gated_ref[...], out_ref[...]), layout, half, outs)


def gate_out(mixed, pre, out_rows, half):
    tokens, my_width = mixed.shape
    width = out_rows.shape[1]
    layout = partial_layout(tokens)
    specs, shapes = partial_specs(layout, half, width, my_width)
    gated, *partials = pl.pallas_call(
        functools.partial(gate_out_kernel, layout, half),
        grid=(width // my_width,),
        in_specs=[
            block(tokens, my_width),
            block(tokens, my_width, at=lambda j: (0, 3)),
            block(my_width, my_width, at=lambda j: (0, j)),
        ],
        out_specs=[block(tokens, my_width)] + specs,
        out_shape=[jax.ShapeDtypeStruct((tokens, my_width), bf16)] + shapes,
        compiler_params=vmem,
        cost_estimate=cost(3 * tokens * my_width * width, 16 * tokens * width),
        name="gate_out",
    )(mixed, pre, out_rows)
    return gated, partials


def gated_grad_kernel(places, half, *refs):
    *pieces, out_ref, all_ref, grad_ref = refs
    for slot, (piece, row) in enumerate(places):
        all_ref[slot * half : (slot + 1) * half, :] = pieces[piece][row : row + half, :]
    grad_ref[...] = matmul(all_ref[...], out_ref[...], 1, 1)


def gated_gradient(gathered, out_rows, half):
    pieces, places = gathered
    my_width, width = out_rows.shape
    tokens = half * len(places)
    return pl.pallas_call(
        functools.partial(gated_grad_kernel, places, half),
        grid=(1,),
        in_specs=[block(*piece.shape) for piece in pieces] + [block(*out_rows.shape)],
        out_specs=[block(tokens, width), block(tokens, my_width)],
        out_shape=[
            jax.ShapeDtypeStruct((tokens, width), bf16),
            jax.ShapeDtypeStruct((tokens, my_width), f32),
        ],
        compiler_params=vmem,
        cost_estimate=cost(3 * tokens * width * my_width),
        name="gated_gradient",
    )(*pieces, out_rows)


def ffn_forward_kernel(places, half, *refs):
    *pieces, weight_ref, both_ref, hidden_ref, all_ref = refs

    @pl.when(pl.program_id(0) == 0)
    def _():
        for slot, (piece, row) in enumerate(places):
            rows = slice(slot * half, (slot + 1) * half)
            all_ref[rows, :] = pieces[piece][row : row + half, :]

    both = matmul(all_ref[...], weight_ref[...])
    both_ref[...] = both
    gate, up = (both[:, :LANES], both[:, LANES:])
    hidden_ref[...] = (gate * jax.nn.sigmoid(gate) * up).astype(bf16)


def ffn_forward(gathered, ffn_cols, half):
    pieces, places = gathered
    width, total = ffn_cols.shape
    tokens = half * len(places)
    if (total // 2) % LANES:
        (rows,) = pieces
        both = matmul(rows, ffn_cols)
        gate, up = (both[:, : total // 2], both[:, total // 2 :])
        return both, (jax.nn.silu(gate) * up).astype(bf16), rows
    return pl.pallas_call(
        functools.partial(ffn_forward_kernel, places, half),
        grid=(total // (2 * LANES),),
        in_specs=[block(*piece.shape) for piece in pieces]
        + [block(width, 2 * LANES, at=lambda j: (0, j))],
        out_specs=[
            block(tokens, 2 * LANES, at=lambda j: (0, j)),
            block(tokens, LANES, at=lambda j: (0, j)),
            block(tokens, width),
        ],
        out_shape=[
            jax.ShapeDtypeStruct((tokens, total), f32),
            jax.ShapeDtypeStruct((tokens, total // 2), bf16),
            jax.ShapeDtypeStruct((tokens, width), bf16),
        ],
        compiler_params=vmem,
        cost_estimate=cost(3 * tokens * width * total),
        name="ffn_forward",
    )(*pieces, ffn_cols)


def ffn_backward_kernel(cotangent_ref, weight_ref, both_ref, grads_ref):
    hidden_grad = matmul(cotangent_ref[...], weight_ref[...])
    for j in range(hidden_grad.shape[1] // LANES):
        grad = hidden_grad[:, j * LANES : (j + 1) * LANES]
        gate = both_ref[:, 2 * j * LANES : (2 * j + 1) * LANES]
        up = both_ref[:, (2 * j + 1) * LANES : (2 * j + 2) * LANES]
        sig = jax.nn.sigmoid(gate)
        slope = sig * (1.0 + gate * (1.0 - sig))
        grads_ref[:, 2 * j * LANES : (2 * j + 1) * LANES] = (grad * up * slope).astype(bf16)
        grads_ref[:, (2 * j + 1) * LANES : (2 * j + 2) * LANES] = (grad * (gate * sig)).astype(bf16)


def ffn_backward(cotangent_all, down_cols, both):
    tokens, width = cotangent_all.shape
    mine = down_cols.shape[1]
    if mine % LANES:
        gate, up = (both[:, :mine], both[:, mine:])
        hidden_grad = matmul(cotangent_all, down_cols)
        sig = jax.nn.sigmoid(gate)
        gate_grad = hidden_grad * up * (sig * (1.0 + gate * (1.0 - sig)))
        up_grad = hidden_grad * (gate * sig)
        return jnp.concatenate((gate_grad, up_grad), axis=1).astype(bf16)
    size = 2 * LANES
    return pl.pallas_call(
        ffn_backward_kernel,
        grid=(pl.cdiv(mine, size),),
        in_specs=[
            block(tokens, width),
            block(width, size, at=lambda j: (0, j)),
            block(tokens, 2 * size, at=lambda j: (0, j)),
        ],
        out_specs=block(tokens, 2 * size, at=lambda j: (0, j)),
        out_shape=jax.ShapeDtypeStruct((tokens, 2 * mine), bf16),
        compiler_params=vmem,
        cost_estimate=cost(4 * tokens * width * mine),
        name="ffn_backward",
    )(cotangent_all, down_cols, both)


def add_up(parts):
    if len(parts) == 1 and len(parts[0].shape) == 3:
        return jnp.sum(parts[0][...].astype(f32), axis=0)
    if len(parts) == 1:
        return parts[0][...]
    rest, near, far, across, along = parts
    top = near[...].astype(f32) + across[...].astype(f32)
    low = far[...].astype(f32) + along[...].astype(f32)
    return rest[...] + jnp.where(pl.program_id(0) == 0, top, low)


def combine_kernel(post, count, given, *refs):
    parts, values, outs = (refs[:count], refs[count : count + given], refs[count + given :])
    results = post(add_up(parts), *(ref[...].astype(f32) for ref in values))
    for result, ref in zip(results, outs):
        ref[...] = result.astype(ref.dtype)


def combine(post, parts, values, dtypes, half):
    width = parts[0].shape[-1]
    mine = block(half, width, at=lambda h: (h, 0))
    fixed = block(half, width)
    part_specs = [mine] if len(parts) == 1 else [mine] + [fixed] * 4
    if parts[0].ndim == 3:
        part_specs = [block(parts[0].shape[0], half, width, at=lambda h: (0, h, 0))]
    value_specs = [block(1, width) if v.shape[0] == 1 else mine for v in values]
    return pl.pallas_call(
        functools.partial(combine_kernel, post, len(parts), len(values)),
        grid=(2,),
        in_specs=part_specs + value_specs,
        out_specs=[mine] * len(dtypes),
        out_shape=[jax.ShapeDtypeStruct((2 * half, width), dtype) for dtype in dtypes],
        compiler_params=vmem,
        cost_estimate=cost(0, 60 * half * width),
        name="combine",
    )(*parts, *values)


def residual(branch, inputs, gain):
    resid = inputs + branch
    return resid, resid * rms_factor(resid) * gain


def residual_back(mid_grad, cotangent, resid, gain):
    factor = rms_factor(resid)
    grad = cotangent + rms_back(mid_grad * gain, resid * factor, factor)
    return grad, grad


def input_back(in_grad, resid_grad, inputs, gain):
    factor = rms_factor(inputs)
    return (resid_grad + rms_back(in_grad * gain, inputs * factor, factor),)


def local(
    layer_input,
    segment_ids,
    mix_gain,
    bound_logit,
    query_weight,
    forget_weight,
    input_weight,
    output_gate_weight,
    output_weight,
    ffn_gain,
    ffn_gate_weight,
    ffn_up_weight,
    ffn_down_weight,
    output_cotangent,
):
    rows, length, width = layer_input.shape
    ranks, rank = (lax.axis_size("seq"), lax.axis_index("seq"))
    count = lax.axis_size("dp")
    my_width = width // ranks
    tokens = rows * length
    half = tokens // 2
    my_rows = mix_gain.shape[0]
    rank_rows = my_rows * ranks
    x_low = layer_input.reshape(tokens, width)
    cotangent_low = output_cotangent.reshape(tokens, width)
    core = (lax.axis_index("dp") & 1).reshape(1)

    mix_weights = [query_weight, forget_weight, input_weight, output_gate_weight]
    mix_pieces = swap_seq(column_pieces(mix_weights))
    mix_cols = gather_dp(mix_pieces.reshape(rank_rows, 4 * my_width))
    out_rows = gather_dp(lax.ppermute(output_weight, ("dp", "seq"), row_route()))
    x_pieces, places = gather_seq(after(x_low, mix_pieces))
    vectors = jnp.stack((mix_gain, bound_logit, ffn_gain), axis=1)
    vectors = gather_small(gather_small(vectors, "seq"), "dp")
    segments = gather_small(segment_ids[0], "seq")
    vectors = vectors.astype(f32)
    gain_in, logit, gain_mid = (vectors[:, 0], vectors[:, 1], vectors[:, 2])
    gain_in, gain_mid = (gain_in[None, :], gain_mid[None, :])
    table = slot_table()
    bound = jax.nn.sigmoid(-lax.dynamic_slice_in_dim(logit, rank * my_width, my_width))[None, :]
    normed_in, in_mine, in_theirs = assemble(
        (x_pieces, places), core, rank_rows, after(gain_in, segments, bound)
    )
    ffn_pieces = swap_seq(column_pieces([after(ffn_gate_weight, normed_in, out_rows), ffn_up_weight], True))
    ffn_cols = gather_dp(ffn_pieces.reshape(rank_rows, ffn_pieces.shape[2]))
    down_pieces = swap_seq(column_pieces([after(ffn_down_weight, ffn_pieces)]))
    down_cols = gather_dp(down_pieces.reshape(rank_rows, down_pieces.shape[2]))

    pre = dense(after(normed_in, down_pieces), mix_cols, f32, parts=4)
    mixed, states = recurrence_forward(segments, table, pre, bound)
    cotangent = gather_seq(after(cotangent_low, down_pieces))
    gated, partials = gate_out(after(mixed, *cotangent[0][:3]), pre, out_rows, half)
    branch_parts = scatter_seq(partials, half)
    cotangent_all, cotangent_mine, cotangent_theirs = assemble(cotangent, core, rank_rows)
    resid, normed_low = combine(
        residual, branch_parts, (after(x_low, cotangent_all), gain_mid), (f32, bf16), half
    )
    normed_mid = gather_seq(normed_low)

    both, hidden, mid_all = ffn_forward(normed_mid, ffn_cols, half)

    down_theirs = flip(dense(cotangent_theirs, hidden, bf16, 0), "dp", 1)
    down_sum = dense(cotangent_mine, hidden, bf16, 0, down_theirs)
    down_mine = scatter_dp(down_sum)
    cotangent_all = after(cotangent_all, down_sum)
    ffn_right = ffn_backward(cotangent_all, down_cols, both)
    mid_partials = partial_product(ffn_right, [ffn_cols], [ffn_cols.shape[1]], half)
    ffn_sum = dense(mid_all, after(ffn_right, mid_partials[0]), bf16, 0)
    mid_parts = scatter_seq(mid_partials, half, beside=(ffn_sum, down_mine))
    ffn_mine = lax.psum_scatter(after(ffn_sum, *mid_parts[:3]), "dp", scatter_dimension=0, tiled=True)

    resid_grad, branch_own = combine(
        residual_back, mid_parts, (cotangent_low, resid, gain_mid), (f32, bf16), half
    )
    branch, places = gather_seq(branch_own)
    row_place = row_places()
    out_partial = exchanged_product(after(hidden, branch_own), down_cols, row_place, half)
    branch = (after(branch[0], out_partial),) + branch[1:]
    branch_low, gated_grad = gated_gradient((branch, places), out_rows, half)
    out_parts = swap_seq(after(out_partial, branch_low))
    mix_right, logit_part = recurrence_backward(segments, table, pre, bound, mixed, gated_grad, states)
    mix_theirs = dense(in_theirs, mix_right, bf16, 0)
    out_sum = dense(gated, after(branch_low, mix_theirs, out_parts), bf16, 0)
    out_sum = out_sum.reshape(count // 2, 2, my_rows, width)
    out_theirs = flip(lax.dynamic_index_in_dim(out_sum, 1 - core[0], 1, keepdims=False), "dp", 1)
    mix_sum = mixer_sums(in_mine, mix_right, flip(mix_theirs, "dp", 1), out_sum, out_theirs, core)
    mix_mine = scatter_dp(mix_sum)
    down_back = swap_columns(after(down_mine, mix_sum))
    ffn_back = swap_columns(after(ffn_mine, down_back))
    in_partial = exchanged_product(after(mix_right, mix_sum), mix_cols, row_place, half)
    in_parts = swap_seq(after(in_partial, ffn_back))
    (block_output,) = combine(
        lambda total, resid: (resid + total,), (out_parts,), (after(resid, in_partial),), (bf16,), half
    )
    (ffn_gate_weight_grad, ffn_up_weight_grad), ffn_sums = return_columns(
        after(ffn_back, in_partial), [ffn_gate_weight, ffn_up_weight], True
    )
    (input_grad,) = combine(input_back, (in_parts,), (resid_grad, x_low, gain_in), (f32,), half)
    (ffn_down_weight_grad,), _ = return_columns(after(down_back, in_partial), [ffn_down_weight])

    logit_sum = gather_small(sum_small(-after(logit_part, in_partial)[0] * (1.0 - bound[0]), "dp"), "seq")
    at = (lax.axis_index("dp") * ranks + rank) * my_rows
    bound_logit_grad = lax.dynamic_slice_in_dim(logit_sum, at, my_rows)
    mix_mine = after(mix_mine, in_parts)
    mix_grads, mix_sums = return_columns(swap_columns(mix_mine[:, : 4 * my_width]), mix_weights)
    out_mine = mix_mine[:, 4 * my_width :].reshape(ranks, my_rows, my_width)
    out_mine = lax.ppermute(out_mine, ("dp", "seq"), [(b, a) for a, b in row_route()])
    output_weight_grad = jnp.moveaxis(out_mine, 0, 1).reshape(my_rows, width).astype(f32)
    query_weight_grad, forget_weight_grad, input_weight_grad, output_gate_weight_grad = mix_grads
    mix_gain_grad = mix_sums / mix_gain.astype(f32)
    ffn_gain_grad = ffn_sums / ffn_gain.astype(f32)
    return (
        block_output.reshape(rows, length, width),
        input_grad.reshape(rows, length, width),
        mix_gain_grad,
        bound_logit_grad,
        query_weight_grad,
        forget_weight_grad,
        input_weight_grad,
        output_gate_weight_grad,
        output_weight_grad,
        ffn_gain_grad,
        ffn_gate_weight_grad,
        ffn_up_weight_grad,
        ffn_down_weight_grad,
    )


def solution(mesh):
    by_token = P("dp", "seq", None)
    vector = P(("dp", "seq"))
    matrix = P(("dp", "seq"), None)
    return jax.shard_map(
        local,
        mesh=mesh,
        in_specs=(by_token, P("dp", "seq"), vector, vector)
        + (matrix,) * 5
        + (vector,)
        + (matrix,) * 3
        + (by_token,),
        out_specs=(by_token, by_token, vector, vector) + (matrix,) * 5 + (vector,) + (matrix,) * 3,
        check_vma=False,
    )
```

```python
import functools

import jax
import jax.numpy as jnp
from jax import lax
from jax.experimental import pallas as pl
from jax.experimental.pallas import tpu as pltpu
from jax.sharding import PartitionSpec as P

HEAD_FEATURES = 128
LANES = 128

eps_model = 1e-06
eps_group = 1e-05
f32 = jnp.float32
bf16 = jnp.bfloat16

vmem = pltpu.CompilerParams(vmem_limit_bytes=48 * 1024 * 1024)


def cost(flops, moved=0):
    return pl.CostEstimate(flops=flops, bytes_accessed=moved, transcendentals=0)


def flip(block, axis, bits):
    return lax.ppermute(block, axis, [(i, i ^ bits) for i in range(lax.axis_size(axis))])


def gather_small(block, axis):
    count, mine = (lax.axis_size(axis), lax.axis_index(axis))
    bit = 1
    while bit < count:
        other = flip(block, axis, bit)
        upper = (mine & bit) != 0
        block = jnp.concatenate(
            (jnp.where(upper, other, block), jnp.where(upper, block, other)), axis=0
        )
        bit *= 2
    return block


def sum_small(block, axis):
    others = [flip(block, axis, bits) for bits in range(1, lax.axis_size(axis))]
    return functools.reduce(jnp.add, others, block)


def slots():
    if lax.axis_size("seq") == 4:
        return [(1, 0), (3, 0), (2, 1), (3, 1), (0, 0), (0, 1), (2, 0), (1, 1)]
    return [(k, h) for k in range(lax.axis_size("seq")) for h in range(2)]


def slot_table():
    place = {slot: i for i, slot in enumerate(slots())}
    count = lax.axis_size("seq")
    table = jnp.array([[place[k, h] for h in range(2)] for k in range(count)], jnp.int32)
    return table[jnp.arange(count) ^ lax.axis_index("seq")].reshape(2 * count)


def row_places():
    k, h = (jnp.array(bits, jnp.int32) for bits in zip(*slots()))
    return (k ^ lax.axis_index("seq")) * 2 + h


def gather_seq(block, second=()):
    count = lax.axis_size("seq")
    half = block.shape[0] // 2
    if count == 4:
        near = flip(block, "seq", 1)
        far = flip(block, "seq", 2)
        corner_top = flip(after(near[:half], *second), "seq", 2)
        corner_low = flip(after(far[half:], *second), "seq", 1)
        found = {(3, 0): (3, 0), (3, 1): (4, 0)}
        for k in range(3):
            found[k, 0], found[k, 1] = ((k, 0), (k, half))
        return (block, near, far, corner_top, corner_low), [found[slot] for slot in slots()]
    bit = 1
    while bit < count:
        block = jnp.concatenate((block, flip(block, "seq", bit)), axis=0)
        bit *= 2
    return (block,), [(0, i * half) for i in range(2 * count)]


def partial_layout(tokens):
    count = lax.axis_size("seq")
    if count == 4:
        return [(0, 2, bf16), (2, 4, bf16), (4, 8, f32)]
    return [(0, 2 * count, f32)]


def scatter_seq(partials, half, beside=()):
    if len(partials) == 3:
        near, far, rest = partials
        near = flip(near, "seq", 1)
        far = flip(far, "seq", 2)
        rest = after(rest, *beside)
        across = (rest[2 * half : 3 * half] + near[half:].astype(f32)).astype(bf16)
        along = (rest[3 * half :] + far[half:].astype(f32)).astype(bf16)
        return (rest, near, far, flip(across, "seq", 2), flip(along, "seq", 1))
    (total,) = partials
    bit = lax.axis_size("seq") // 2
    while bit:
        middle = total.shape[0] // 2
        total = total[:middle] + flip(total[middle:].astype(bf16), "seq", bit).astype(f32)
        bit //= 2
    return (total,)


def swap_seq(pieces):
    return lax.all_to_all(pieces, "seq", split_axis=0, concat_axis=0, tiled=True)


def gather_dp(block):
    return lax.all_gather(block, "dp", axis=0, tiled=True)


def scatter_dp(mine):
    groups = [list(range(c, lax.axis_size("dp"), 2)) for c in range(2)]
    return lax.psum_scatter(
        mine, "dp", scatter_dimension=0, axis_index_groups=groups, tiled=True
    )


def row_route():
    count, ranks = (lax.axis_size("dp"), lax.axis_size("seq"))
    return [(b, (b % count) * ranks + b // count) for b in range(count * ranks)]


def after(value, *others):
    return lax.optimization_barrier((value,) + others)[0]


def block(*shape, at=None):
    return pl.BlockSpec(shape, at or (lambda *_: (0,) * len(shape)))


def column_blocks(width, interleave):
    size = LANES if interleave else width
    return [(j * size, size) for j in range(width // size)]


def pieces_kernel(interleave, *refs):
    weights, out_ref = (refs[:-1], refs[-1])
    blocks = column_blocks(weights[0].shape[1], interleave)
    at = 0
    for start, size in blocks:
        for ref in weights:
            out_ref[0, :, at : at + size] = ref[:, start : start + size]
            at += size


def column_pieces(weights, interleave=False):
    ranks = lax.axis_size("seq")
    rows, width = (weights[0].shape[0], weights[0].shape[1] // ranks)
    if width % LANES:
        parts = [jnp.moveaxis(w.reshape(rows, ranks, width), 1, 0) for w in weights]
        return jnp.concatenate(parts, axis=2)
    total = width * len(weights)
    return pl.pallas_call(
        functools.partial(pieces_kernel, interleave),
        grid=(ranks,),
        in_specs=[block(rows, width, at=lambda r: (0, r)) for _ in weights],
        out_specs=block(1, rows, total, at=lambda r: (r, 0, 0)),
        out_shape=jax.ShapeDtypeStruct((ranks, rows, total), bf16),
        compiler_params=vmem,
        cost_estimate=cost(0, 4 * rows * total * ranks),
        name="column_pieces",
    )(*weights)


def return_kernel(interleave, count, *refs):
    pieces_ref, weights, grads, (gain_ref,) = (
        refs[0],
        refs[1 : 1 + count],
        refs[1 + count : 1 + 2 * count],
        refs[1 + 2 * count :],
    )

    @pl.when(pl.program_id(0) == 0)
    def _():
        gain_ref[...] = jnp.zeros_like(gain_ref)

    at = 0
    total = jnp.zeros(gain_ref.shape, f32)
    for start, size in column_blocks(weights[0].shape[1], interleave):
        for weight_ref, grad_ref in zip(weights, grads):
            grad = pieces_ref[0, :, at : at + size].astype(f32)
            grad_ref[:, start : start + size] = grad
            weight = weight_ref[:, start : start + size].astype(f32)
            total += jnp.sum(weight * grad, axis=1, keepdims=True)
            at += size
    gain_ref[...] += total


def swap_columns(mine):
    ranks = lax.axis_size("seq")
    return swap_seq(mine.reshape(ranks, mine.shape[0] // ranks, mine.shape[1]))


def return_columns(pieces, weights, interleave=False):
    ranks, rows, total = pieces.shape
    width = weights[0].shape[1] // ranks
    if width % LANES:
        grads = [
            jnp.moveaxis(pieces[:, :, i * width : (i + 1) * width], 0, 1)
            .reshape(rows, ranks * width)
            .astype(f32)
            for i in range(len(weights))
        ]
        return grads, sum(jnp.sum(w.astype(f32) * g, axis=1) for w, g in zip(weights, grads))
    columns = block(rows, width, at=lambda r: (0, r))
    *grads, sums = pl.pallas_call(
        functools.partial(return_kernel, interleave, len(weights)),
        grid=(ranks,),
        in_specs=[block(1, rows, total, at=lambda r: (r, 0, 0))] + [columns] * len(weights),
        out_specs=[columns] * len(weights) + [block(rows, 1)],
        out_shape=[jax.ShapeDtypeStruct(w.shape, f32) for w in weights]
        + [jax.ShapeDtypeStruct((rows, 1), f32)],
        compiler_params=vmem,
        cost_estimate=cost(0, 8 * rows * total * ranks),
        name="return_columns",
    )(pieces, *weights)
    return grads, sums[:, 0]


def sums(mask, terms):
    high = terms.astype(bf16)
    low = (terms - high.astype(f32)).astype(bf16)
    ones = mask.astype(bf16)
    return matmul(ones, low) + matmul(ones, high)


def product(left, right, left_dim, right_dim):
    left_high, right_high = (left.astype(bf16), right.astype(bf16))
    left_low = (left - left_high.astype(f32)).astype(bf16)
    right_low = (right - right_high.astype(f32)).astype(bf16)
    return (
        matmul(left_high, right_low, left_dim, right_dim)
        + matmul(left_low, right_high, left_dim, right_dim)
        + matmul(left_high, right_high, left_dim, right_dim)
    )


def chunk_parts(chunk, seg_ref, seg_col_ref, seg_row_ref, pre_ref, bound_ref):
    size, wide = pre_ref.shape
    width = wide // 3
    first = chunk * size
    prior = seg_ref[jnp.maximum(first - 1, 0)]
    last = seg_ref[first + size - 1]
    seg_col = seg_col_ref[...]
    at = lax.broadcasted_iota(jnp.int32, (size, size), 0)
    of = lax.broadcasted_iota(jnp.int32, (size, size), 1)
    seen = (seg_col == seg_row_ref[...]) & (at >= of)
    linked = (seg_col == prior).astype(f32)
    tail = (seg_col == last).astype(f32)
    linked_last = (prior == last).astype(f32)
    query_pre = pre_ref[:, 0:width]
    forget_pre = pre_ref[:, width : 2 * width]
    value = pre_ref[:, 2 * width : 3 * width]
    forget_sig = jax.nn.sigmoid(-forget_pre)
    key = bound_ref[...] * forget_sig
    query_sig = jax.nn.sigmoid(query_pre)
    lower = (at >= of).astype(f32)
    cumul = sums(lower, jnp.log1p(-key))
    grow = jnp.exp(cumul)
    shrink = jnp.exp(-cumul)
    end = grow[size - 1 :, :]
    query_d = query_pre * query_sig * grow
    key_d = key * shrink
    key_t = key_d * end * tail
    keep = end * linked_last
    return locals()


def forward_kernel(seg_ref, slot_ref, seg_col_ref, seg_row_ref, pre_ref, bound_ref, mixed_ref, states_ref, state_ref):
    step = pl.program_id(0)
    heads = mixed_ref.shape[1] // HEAD_FEATURES

    @pl.when(step == 0)
    def _():
        state_ref[...] = jnp.zeros_like(state_ref)

    p = chunk_parts(step, seg_ref, seg_col_ref, seg_row_ref, pre_ref, bound_ref)
    for h in range(heads):
        cols = slice(h * HEAD_FEATURES, (h + 1) * HEAD_FEATURES)
        query_d, key_d, value = p["query_d"][:, cols], p["key_d"][:, cols], p["value"][:, cols]
        state = state_ref[h]
        states_ref[0, h] = state
        scores = jnp.where(p["seen"], product(query_d, key_d, 1, 1), 0.0)
        mixed = product(scores, value, 1, 0) + product(query_d * p["linked"], state, 1, 1)
        mixed_ref[:, cols] = mixed
        state_ref[h] = state * p["keep"][:, cols] + product(value, p["key_t"][:, cols], 0, 0)


def backward_kernel(seg_ref, slot_ref, seg_col_ref, seg_row_ref, pre_ref, bound_ref, outgate_pre_ref, mixed_ref, gated_grad_ref, states_ref, grads_ref, logit_ref, back_ref, through_ref):
    step = pl.program_id(0)
    chunk = pl.num_programs(0) - 1 - step
    width = mixed_ref.shape[1]
    heads = width // HEAD_FEATURES

    @pl.when(step == 0)
    def _():
        back_ref[...] = jnp.zeros_like(back_ref)
        through_ref[...] = jnp.zeros_like(through_ref)
        logit_ref[...] = jnp.zeros_like(logit_ref)

    p = chunk_parts(chunk, seg_ref, seg_col_ref, seg_row_ref, pre_ref, bound_ref)
    query_pre, query_sig = p["query_pre"], p["query_sig"]
    upper = (p["at"] <= p["of"]).astype(f32)
    for h in range(heads):
        cols = slice(h * HEAD_FEATURES, (h + 1) * HEAD_FEATURES)
        query_d, key_d, key_t, value = (p[k][:, cols] for k in ("query_d", "key_d", "key_t", "value"))
        grow, shrink, end, keep, key = (p[k][:, cols] for k in ("grow", "shrink", "end", "keep", "key"))
        state = states_ref[0, h]
        back = back_ref[h]
        mixed = mixed_ref[:, cols]
        factor = lax.rsqrt(jnp.mean(mixed * mixed, axis=-1, keepdims=True) + eps_group)
        normed = mixed * factor
        gated_grad = gated_grad_ref[:, cols]
        gate = outgate_pre_ref[:, cols]
        gate_sig = jax.nn.sigmoid(gate)
        outgate_grad = gated_grad * normed * (gate_sig * (1.0 + gate * (1.0 - gate_sig)))
        weighted = gated_grad * (gate * gate_sig)
        mixed_grad = factor * (
            weighted - normed * jnp.mean(weighted * normed, axis=-1, keepdims=True)
        )
        scores = jnp.where(p["seen"], product(query_d, key_d, 1, 1), 0.0)
        scores_grad = jnp.where(p["seen"], product(mixed_grad, value, 1, 1), 0.0)
        value_grad = product(scores, mixed_grad, 0, 0) + product(key_t, back, 1, 1)
        query_d_grad = product(scores_grad, key_d, 1, 0) + p["linked"] * product(mixed_grad, state, 1, 0)
        key_d_grad = product(scores_grad, query_d, 0, 0)
        key_t_grad = product(value, back, 1, 0)
        key_grad = key_d_grad * shrink + (p["tail"] * end * shrink) * key_t_grad
        change = query_d * query_d_grad - key_d * key_d_grad - key_t * key_t_grad
        through = sums(upper, change) + through_ref[:, cols]
        key_total = key_grad - through / (1.0 - key)
        new_back = back * keep + product(mixed_grad, query_d * p["linked"], 0, 0)
        back_ref[h] = new_back
        through_ref[:, cols] = jnp.sum(new_back * state, axis=0, keepdims=True)
        sig = query_sig[:, cols]
        query_grad = query_d_grad * grow * (sig * (1.0 + query_pre[:, cols] * (1.0 - sig)))
        weighted_key = key_total * key
        forget_grad = -weighted_key * (1.0 - p["forget_sig"][:, cols])
        logit_ref[:, cols] += jnp.sum(weighted_key, axis=0, keepdims=True)
        for part, grad in enumerate((query_grad, forget_grad, value_grad, outgate_grad)):
            lo = part * width + h * HEAD_FEATURES
            grads_ref[:, lo : lo + HEAD_FEATURES] = grad.astype(bf16)


def recurrence_forward(segments, table, pre, bound):
    tokens, wide = pre.shape
    steps = table.shape[0]
    size, width = (tokens // steps, wide // 4)
    heads = width // HEAD_FEATURES
    return pl.pallas_call(
        forward_kernel,
        grid_spec=pltpu.PrefetchScalarGridSpec(
            num_scalar_prefetch=2,
            grid=(steps,),
            in_specs=[
                pl.BlockSpec((size, 1), lambda i, s, t: (i, 0)),
                pl.BlockSpec((1, size), lambda i, s, t: (0, i)),
                pl.BlockSpec((size, 3 * width), lambda i, s, t: (t[i], 0)),
                pl.BlockSpec((1, width), lambda i, s, t: (0, 0)),
            ],
            out_specs=[
                pl.BlockSpec((size, width), lambda i, s, t: (t[i], 0)),
                pl.BlockSpec((1, heads, HEAD_FEATURES, HEAD_FEATURES), lambda i, s, t: (i, 0, 0, 0)),
            ],
            scratch_shapes=[pltpu.VMEM((heads, HEAD_FEATURES, HEAD_FEATURES), f32)],
        ),
        out_shape=[
            jax.ShapeDtypeStruct((tokens, width), f32),
            jax.ShapeDtypeStruct((steps, heads, HEAD_FEATURES, HEAD_FEATURES), f32),
        ],
        compiler_params=vmem,
        cost_estimate=cost(320 * tokens * width * HEAD_FEATURES),
        name="recurrence_forward",
    )(segments, table, segments[:, None], segments[None, :], pre, bound)


def recurrence_backward(segments, table, pre, bound, mixed, gated_grad, states):
    tokens, wide = pre.shape
    steps = table.shape[0]
    size, width = (tokens // steps, wide // 4)
    heads = width // HEAD_FEATURES
    tokens_block = pl.BlockSpec((size, width), lambda i, s, t: (t[steps - 1 - i], 0))
    return pl.pallas_call(
        backward_kernel,
        grid_spec=pltpu.PrefetchScalarGridSpec(
            num_scalar_prefetch=2,
            grid=(steps,),
            in_specs=[
                pl.BlockSpec((size, 1), lambda i, s, t: (steps - 1 - i, 0)),
                pl.BlockSpec((1, size), lambda i, s, t: (0, steps - 1 - i)),
                pl.BlockSpec((size, 3 * width), lambda i, s, t: (t[steps - 1 - i], 0)),
                pl.BlockSpec((1, width), lambda i, s, t: (0, 0)),
                pl.BlockSpec((size, width), lambda i, s, t: (t[steps - 1 - i], 3)),
                tokens_block,
                tokens_block,
                pl.BlockSpec(
                    (1, heads, HEAD_FEATURES, HEAD_FEATURES),
                    lambda i, s, t: (steps - 1 - i, 0, 0, 0),
                ),
            ],
            out_specs=[
                pl.BlockSpec((size, 4 * width), lambda i, s, t: (t[steps - 1 - i], 0)),
                pl.BlockSpec((1, width), lambda i, s, t: (0, 0)),
            ],
            scratch_shapes=[
                pltpu.VMEM((heads, HEAD_FEATURES, HEAD_FEATURES), f32),
                pltpu.VMEM((1, width), f32),
            ],
        ),
        out_shape=[
            jax.ShapeDtypeStruct((tokens, 4 * width), bf16),
            jax.ShapeDtypeStruct((1, width), f32),
        ],
        compiler_params=vmem,
        cost_estimate=cost(620 * tokens * width * HEAD_FEATURES),
        name="recurrence_backward",
    )(segments, table, segments[:, None], segments[None, :], pre, bound, pre, mixed, gated_grad, states)


def matmul(left, right, left_dim=1, right_dim=0):
    return lax.dot_general(
        left, right, (((left_dim,), (right_dim,)), ((), ())), preferred_element_type=f32
    )


def rms_factor(value):
    return lax.rsqrt(jnp.mean(value * value, axis=-1, keepdims=True) + eps_model)


def rms_back(grad_unit, unit, factor):
    return factor * (grad_unit - unit * jnp.mean(grad_unit * unit, axis=-1, keepdims=True))


def product_kernel(left_dim, *refs):
    left_ref, right_ref, *added, out_ref = refs
    total = matmul(left_ref[...], right_ref[...], left_dim, 0)
    for ref in added:
        total += ref[...].astype(f32)
    out_ref[...] = total.astype(out_ref.dtype)


def dense(left, right, dtype, left_dim=1, added=None, parts=2):
    height, width = (left.shape[1 - left_dim], right.shape[1])
    size = width // parts if (width // parts) % LANES == 0 else width
    columns = block(height, size, at=lambda j: (0, j))
    extra = [] if added is None else [added]
    return pl.pallas_call(
        functools.partial(product_kernel, left_dim),
        grid=(width // size,),
        in_specs=[block(*left.shape), block(right.shape[0], size, at=lambda j: (0, j))]
        + [columns] * len(extra),
        out_specs=columns,
        out_shape=jax.ShapeDtypeStruct((height, width), dtype),
        compiler_params=vmem,
        cost_estimate=cost(3 * left.shape[0] * left.shape[1] * width),
        name="dense",
    )(left, right, *extra)


def mixer_sums_kernel(count, rows, core_ref, left_ref, right_ref, theirs_ref, out_ref, out_theirs_ref, total_ref):
    step = pl.program_id(0)

    @pl.when(step < count)
    def _():
        total = matmul(left_ref[...], right_ref[...], 0, 0) + theirs_ref[...].astype(f32)
        total_ref[...] = total.astype(bf16)

    @pl.when(step == count)
    def _():
        width = total_ref.shape[1]
        for z in range(out_ref.shape[0]):
            both = (out_ref[z, 0].astype(f32) + out_theirs_ref[z].astype(f32)).astype(bf16)
            ranks = both.shape[1] // width
            for j in range(ranks):
                at = (z * ranks + j) * rows
                total_ref[at : at + rows, :] = both[:, j * width : (j + 1) * width]


def mixer_sums(left, right, theirs, out_sum, out_theirs, core):
    tokens, height = left.shape
    lines, cores, rows, width = out_sum.shape
    size = right.shape[1] // 4
    columns = block(height, size, at=lambda j, c: (0, jnp.minimum(j, 3)))
    return pl.pallas_call(
        functools.partial(mixer_sums_kernel, 4, rows),
        grid_spec=pltpu.PrefetchScalarGridSpec(
            num_scalar_prefetch=1,
            grid=(5,),
            in_specs=[
                block(tokens, height),
                block(tokens, size, at=lambda j, c: (0, jnp.minimum(j, 3))),
                columns,
                block(lines, 1, rows, width, at=lambda j, c: (0, c[0], 0, 0)),
                block(lines, rows, width),
            ],
            out_specs=block(height, size, at=lambda j, c: (0, j)),
        ),
        out_shape=jax.ShapeDtypeStruct((height, 5 * size), bf16),
        compiler_params=vmem,
        cost_estimate=cost(3 * tokens * height * 4 * size),
        name="mixer_sums",
    )(core, left, right, theirs, out_sum, out_theirs)


def store_halves(core, value, rows, row_block, mine_ref, theirs_ref):
    for z in range(value.shape[1] // (2 * row_block)):
        even = value[:, 2 * z * row_block : (2 * z + 1) * row_block]
        odd = value[:, (2 * z + 1) * row_block : (2 * z + 2) * row_block]
        to = slice(z * row_block, (z + 1) * row_block)

        @pl.when(core == 0)
        def _():
            mine_ref[rows, to] = even
            theirs_ref[rows, to] = odd

        @pl.when(core == 1)
        def _():
            mine_ref[rows, to] = odd
            theirs_ref[rows, to] = even


def assemble_kernel(places, half, row_block, normed, core_ref, *refs):
    *pieces, gain_ref, all_ref, mine_ref, theirs_ref = refs
    for slot, (piece, row) in enumerate(places):
        rows = slice(slot * half, (slot + 1) * half)
        value = pieces[piece][row : row + half, :]
        if normed:
            wide = value.astype(f32)
            value = (wide * rms_factor(wide) * gain_ref[...]).astype(bf16)
        all_ref[rows, :] = value
        store_halves(core_ref[0], value, rows, row_block, mine_ref, theirs_ref)


def assemble(gathered, core, row_block, gain=None):
    pieces, places = gathered
    half = pieces[0].shape[0] // 2 if len(pieces) > 1 else pieces[0].shape[0] // len(places)
    tokens, width = (half * len(places), pieces[0].shape[1])
    normed = gain is not None
    gain = gain if normed else jnp.zeros((1, width), f32)
    shapes = [(tokens, width), (tokens, width // 2), (tokens, width // 2)]
    return pl.pallas_call(
        functools.partial(assemble_kernel, places, half, row_block, normed),
        grid_spec=pltpu.PrefetchScalarGridSpec(
            num_scalar_prefetch=1,
            grid=(1,),
            in_specs=[block(*piece.shape) for piece in pieces] + [block(1, width)],
            out_specs=[block(*shape) for shape in shapes],
        ),
        out_shape=[jax.ShapeDtypeStruct(shape, bf16) for shape in shapes],
        compiler_params=vmem,
        cost_estimate=cost(0, 12 * tokens * width),
        name="assemble",
    )(core, *pieces, gain)


def store_partials(value, layout, half, refs):
    for (first, last, dtype), ref in zip(layout, refs):
        ref[...] = value[first * half : last * half, :].astype(dtype)


def partial_specs(layout, half, width, columns):
    specs = [block((b - a) * half, columns, at=lambda j: (0, j)) for a, b, _ in layout]
    shapes = [jax.ShapeDtypeStruct(((b - a) * half, width), dtype) for a, b, dtype in layout]
    return specs, shapes


def partial_kernel(layout, half, cuts, left_ref, *refs):
    weights, outs = (refs[: len(cuts)], refs[len(cuts) :])
    total = None
    for (first, last), ref in zip(cuts, weights):
        term = matmul(left_ref[:, first:last], ref[...], 1, 1)
        total = term if total is None else total + term
    store_partials(total, layout, half, outs)


def ordered_kernel(half, places_ref, left_ref, weight_ref, out_ref):
    total = matmul(left_ref[...], weight_ref[...], 1, 1).astype(bf16)
    for slot in range(left_ref.shape[0] // half):
        to = pl.multiple_of(places_ref[slot] * half, half)
        out_ref[pl.ds(to, half), :] = total[slot * half : (slot + 1) * half, :]


def exchanged_product(left, weight, places, half, columns=512):
    tokens, depth = left.shape
    width = weight.shape[0]
    ranks = lax.axis_size("seq")
    partial = pl.pallas_call(
        functools.partial(ordered_kernel, half),
        grid_spec=pltpu.PrefetchScalarGridSpec(
            num_scalar_prefetch=1,
            grid=(width // columns,),
            in_specs=[block(tokens, depth), block(columns, depth, at=lambda j, p: (j, 0))],
            out_specs=block(tokens, columns, at=lambda j, p: (0, j)),
        ),
        out_shape=jax.ShapeDtypeStruct((tokens, width), bf16),
        compiler_params=vmem,
        cost_estimate=cost(3 * tokens * depth * width),
        name="exchanged_product",
    )(places, left, weight)
    return partial.reshape(ranks, 2 * half, width)


def partial_product(left, weights, widths, half, columns=512):
    tokens, depth = left.shape
    width = weights[0].shape[0]
    layout = partial_layout(tokens)
    specs, shapes = partial_specs(layout, half, width, columns)
    cuts = [(sum(widths[:i]), sum(widths[: i + 1])) for i in range(len(widths))]
    return pl.pallas_call(
        functools.partial(partial_kernel, layout, half, cuts),
        grid=(width // columns,),
        in_specs=[block(tokens, depth)]
        + [block(columns, size, at=lambda j: (j, 0)) for size in widths],
        out_specs=specs,
        out_shape=shapes,
        compiler_params=vmem,
        cost_estimate=cost(3 * tokens * depth * width),
        name="partial_product",
    )(left, *weights)


def gate_out_kernel(layout, half, mixed_ref, outgate_pre_ref, out_ref, gated_ref, *outs):
    @pl.when(pl.program_id(0) == 0)
    def _():
        for h in range(mixed_ref.shape[1] // HEAD_FEATURES):
            cols = slice(h * HEAD_FEATURES, (h + 1) * HEAD_FEATURES)
            mixed, gate = mixed_ref[:, cols], outgate_pre_ref[:, cols]
            factor = lax.rsqrt(jnp.mean(mixed * mixed, axis=-1, keepdims=True) + eps_group)
            gated_ref[:, cols] = (mixed * factor * (gate * jax.nn.sigmoid(gate))).astype(bf16)

    store_partials(matmul(gated_ref[...], out_ref[...]), layout, half, outs)


def gate_out(mixed, pre, out_rows, half):
    tokens, my_width = mixed.shape
    width = out_rows.shape[1]
    layout = partial_layout(tokens)
    specs, shapes = partial_specs(layout, half, width, my_width)
    gated, *partials = pl.pallas_call(
        functools.partial(gate_out_kernel, layout, half),
        grid=(width // my_width,),
        in_specs=[
            block(tokens, my_width),
            block(tokens, my_width, at=lambda j: (0, 3)),
            block(my_width, my_width, at=lambda j: (0, j)),
        ],
        out_specs=[block(tokens, my_width)] + specs,
        out_shape=[jax.ShapeDtypeStruct((tokens, my_width), bf16)] + shapes,
        compiler_params=vmem,
        cost_estimate=cost(3 * tokens * my_width * width, 16 * tokens * width),
        name="gate_out",
    )(mixed, pre, out_rows)
    return gated, partials


def gated_grad_kernel(places, half, *refs):
    *pieces, out_ref, all_ref, grad_ref = refs
    for slot, (piece, row) in enumerate(places):
        all_ref[slot * half : (slot + 1) * half, :] = pieces[piece][row : row + half, :]
    grad_ref[...] = matmul(all_ref[...], out_ref[...], 1, 1)


def gated_gradient(gathered, out_rows, half):
    pieces, places = gathered
    my_width, width = out_rows.shape
    tokens = half * len(places)
    return pl.pallas_call(
        functools.partial(gated_grad_kernel, places, half),
        grid=(1,),
        in_specs=[block(*piece.shape) for piece in pieces] + [block(*out_rows.shape)],
        out_specs=[block(tokens, width), block(tokens, my_width)],
        out_shape=[
            jax.ShapeDtypeStruct((tokens, width), bf16),
            jax.ShapeDtypeStruct((tokens, my_width), f32),
        ],
        compiler_params=vmem,
        cost_estimate=cost(3 * tokens * width * my_width),
        name="gated_gradient",
    )(*pieces, out_rows)


def ffn_forward_kernel(places, half, *refs):
    *pieces, weight_ref, both_ref, hidden_ref, all_ref = refs

    @pl.when(pl.program_id(0) == 0)
    def _():
        for slot, (piece, row) in enumerate(places):
            rows = slice(slot * half, (slot + 1) * half)
            all_ref[rows, :] = pieces[piece][row : row + half, :]

    both = matmul(all_ref[...], weight_ref[...])
    both_ref[...] = both
    gate, up = (both[:, :LANES], both[:, LANES:])
    hidden_ref[...] = (gate * jax.nn.sigmoid(gate) * up).astype(bf16)


def ffn_forward(gathered, ffn_cols, half):
    pieces, places = gathered
    width, total = ffn_cols.shape
    tokens = half * len(places)
    if (total // 2) % LANES:
        (rows,) = pieces
        both = matmul(rows, ffn_cols)
        gate, up = (both[:, : total // 2], both[:, total // 2 :])
        return both, (jax.nn.silu(gate) * up).astype(bf16), rows
    return pl.pallas_call(
        functools.partial(ffn_forward_kernel, places, half),
        grid=(total // (2 * LANES),),
        in_specs=[block(*piece.shape) for piece in pieces]
        + [block(width, 2 * LANES, at=lambda j: (0, j))],
        out_specs=[
            block(tokens, 2 * LANES, at=lambda j: (0, j)),
            block(tokens, LANES, at=lambda j: (0, j)),
            block(tokens, width),
        ],
        out_shape=[
            jax.ShapeDtypeStruct((tokens, total), f32),
            jax.ShapeDtypeStruct((tokens, total // 2), bf16),
            jax.ShapeDtypeStruct((tokens, width), bf16),
        ],
        compiler_params=vmem,
        cost_estimate=cost(3 * tokens * width * total),
        name="ffn_forward",
    )(*pieces, ffn_cols)


def ffn_backward_kernel(cotangent_ref, weight_ref, both_ref, grads_ref):
    width = weight_ref.shape[1]
    for first in range(0, width, 2 * LANES):
        last = min(first + 2 * LANES, width)
        hidden_grad = matmul(cotangent_ref[...], weight_ref[:, first:last])
        for at in range(first, last, LANES):
            grad = hidden_grad[:, at - first : at - first + LANES]
            gate = both_ref[:, 2 * at : 2 * at + LANES]
            up = both_ref[:, 2 * at + LANES : 2 * at + 2 * LANES]
            sig = jax.nn.sigmoid(gate)
            slope = sig * (1.0 + gate * (1.0 - sig))
            grads_ref[:, 2 * at : 2 * at + LANES] = (grad * up * slope).astype(bf16)
            grads_ref[:, 2 * at + LANES : 2 * at + 2 * LANES] = (grad * (gate * sig)).astype(bf16)


def ffn_backward(cotangent_all, down_cols, both):
    tokens, width = cotangent_all.shape
    mine = down_cols.shape[1]
    if mine % LANES:
        gate, up = (both[:, :mine], both[:, mine:])
        hidden_grad = matmul(cotangent_all, down_cols)
        sig = jax.nn.sigmoid(gate)
        gate_grad = hidden_grad * up * (sig * (1.0 + gate * (1.0 - sig)))
        up_grad = hidden_grad * (gate * sig)
        return jnp.concatenate((gate_grad, up_grad), axis=1).astype(bf16)
    rows = tokens // 2
    return pl.pallas_call(
        ffn_backward_kernel,
        grid=(2,),
        in_specs=[
            block(rows, width, at=lambda i: (i, 0)),
            block(width, mine),
            block(rows, 2 * mine, at=lambda i: (i, 0)),
        ],
        out_specs=block(rows, 2 * mine, at=lambda i: (i, 0)),
        out_shape=jax.ShapeDtypeStruct((tokens, 2 * mine), bf16),
        compiler_params=vmem,
        cost_estimate=cost(4 * tokens * width * mine),
        name="ffn_backward",
    )(cotangent_all, down_cols, both)


def add_up(parts):
    if len(parts) == 1 and len(parts[0].shape) == 3:
        return jnp.sum(parts[0][...].astype(f32), axis=0)
    if len(parts) == 1:
        return parts[0][...]
    rest, near, far, across, along = parts
    top = near[...].astype(f32) + across[...].astype(f32)
    low = far[...].astype(f32) + along[...].astype(f32)
    return rest[...] + jnp.where(pl.program_id(0) == 0, top, low)


def combine_kernel(post, count, given, *refs):
    parts, values, outs = (refs[:count], refs[count : count + given], refs[count + given :])
    results = post(add_up(parts), *(ref[...].astype(f32) for ref in values))
    for result, ref in zip(results, outs):
        ref[...] = result.astype(ref.dtype)


def combine(post, parts, values, dtypes, half):
    width = parts[0].shape[-1]
    mine = block(half, width, at=lambda h: (h, 0))
    fixed = block(half, width)
    part_specs = [mine] if len(parts) == 1 else [mine] + [fixed] * 4
    if parts[0].ndim == 3:
        part_specs = [block(parts[0].shape[0], half, width, at=lambda h: (0, h, 0))]
    value_specs = [block(1, width) if v.shape[0] == 1 else mine for v in values]
    return pl.pallas_call(
        functools.partial(combine_kernel, post, len(parts), len(values)),
        grid=(2,),
        in_specs=part_specs + value_specs,
        out_specs=[mine] * len(dtypes),
        out_shape=[jax.ShapeDtypeStruct((2 * half, width), dtype) for dtype in dtypes],
        compiler_params=vmem,
        cost_estimate=cost(0, 60 * half * width),
        name="combine",
    )(*parts, *values)


def residual(branch, inputs, gain):
    resid = inputs + branch
    return resid, resid * rms_factor(resid) * gain


def residual_back(mid_grad, cotangent, resid, gain):
    factor = rms_factor(resid)
    grad = cotangent + rms_back(mid_grad * gain, resid * factor, factor)
    return grad, grad


def input_back(in_grad, resid_grad, inputs, gain):
    factor = rms_factor(inputs)
    return (resid_grad + rms_back(in_grad * gain, inputs * factor, factor),)


def local(
    layer_input,
    segment_ids,
    mix_gain,
    bound_logit,
    query_weight,
    forget_weight,
    input_weight,
    output_gate_weight,
    output_weight,
    ffn_gain,
    ffn_gate_weight,
    ffn_up_weight,
    ffn_down_weight,
    output_cotangent,
):
    rows, length, width = layer_input.shape
    ranks, rank = (lax.axis_size("seq"), lax.axis_index("seq"))
    count = lax.axis_size("dp")
    my_width = width // ranks
    tokens = rows * length
    half = tokens // 2
    my_rows = mix_gain.shape[0]
    rank_rows = my_rows * ranks
    x_low = layer_input.reshape(tokens, width)
    cotangent_low = output_cotangent.reshape(tokens, width)
    core = (lax.axis_index("dp") & 1).reshape(1)

    mix_weights = [query_weight, forget_weight, input_weight, output_gate_weight]
    mix_pieces = swap_seq(column_pieces(mix_weights))
    mix_cols = gather_dp(mix_pieces.reshape(rank_rows, 4 * my_width))
    out_rows = gather_dp(lax.ppermute(output_weight, ("dp", "seq"), row_route()))
    x_pieces, places = gather_seq(after(x_low, mix_pieces))
    vectors = jnp.stack((mix_gain, bound_logit, ffn_gain), axis=1)
    vectors = gather_small(gather_small(vectors, "seq"), "dp")
    segments = gather_small(segment_ids[0], "seq")
    vectors = vectors.astype(f32)
    gain_in, logit, gain_mid = (vectors[:, 0], vectors[:, 1], vectors[:, 2])
    gain_in, gain_mid = (gain_in[None, :], gain_mid[None, :])
    table = slot_table()
    bound = jax.nn.sigmoid(-lax.dynamic_slice_in_dim(logit, rank * my_width, my_width))[None, :]
    normed_in, in_mine, in_theirs = assemble(
        (x_pieces, places), core, rank_rows, after(gain_in, segments, bound)
    )
    ffn_pieces = swap_seq(column_pieces([after(ffn_gate_weight, normed_in, out_rows), ffn_up_weight], True))
    ffn_cols = gather_dp(ffn_pieces.reshape(rank_rows, ffn_pieces.shape[2]))
    down_pieces = swap_seq(column_pieces([after(ffn_down_weight, ffn_pieces)]))
    down_cols = gather_dp(down_pieces.reshape(rank_rows, down_pieces.shape[2]))

    pre = dense(after(normed_in, down_pieces), mix_cols, f32, parts=4)
    mixed, states = recurrence_forward(segments, table, pre, bound)
    cotangent = gather_seq(after(cotangent_low, down_pieces))
    gated, partials = gate_out(after(mixed, *cotangent[0][:3]), pre, out_rows, half)
    branch_parts = scatter_seq(partials, half)
    cotangent_all, cotangent_mine, cotangent_theirs = assemble(cotangent, core, rank_rows)
    resid, normed_low = combine(
        residual, branch_parts, (after(x_low, cotangent_all), gain_mid), (f32, bf16), half
    )
    normed_mid = gather_seq(normed_low)

    both, hidden, mid_all = ffn_forward(normed_mid, ffn_cols, half)

    down_theirs = flip(dense(cotangent_theirs, hidden, bf16, 0), "dp", 1)
    down_sum = dense(cotangent_mine, hidden, bf16, 0, down_theirs)
    down_mine = scatter_dp(down_sum)
    cotangent_all = after(cotangent_all, down_sum)
    ffn_right = ffn_backward(cotangent_all, down_cols, both)
    mid_partials = partial_product(ffn_right, [ffn_cols], [ffn_cols.shape[1]], half)
    ffn_sum = dense(mid_all, after(ffn_right, mid_partials[0]), bf16, 0)
    mid_parts = scatter_seq(mid_partials, half, beside=(ffn_sum, down_mine))
    ffn_mine = lax.psum_scatter(after(ffn_sum, *mid_parts[:3]), "dp", scatter_dimension=0, tiled=True)

    resid_grad, branch_own = combine(
        residual_back, mid_parts, (cotangent_low, resid, gain_mid), (f32, bf16), half
    )
    branch, places = gather_seq(branch_own)
    row_place = row_places()
    out_partial = exchanged_product(after(hidden, branch_own), down_cols, row_place, half)
    branch = (after(branch[0], out_partial),) + branch[1:]
    branch_low, gated_grad = gated_gradient((branch, places), out_rows, half)
    out_parts = swap_seq(after(out_partial, branch_low))
    mix_right, logit_part = recurrence_backward(segments, table, pre, bound, mixed, gated_grad, states)
    mix_theirs = dense(in_theirs, mix_right, bf16, 0)
    out_sum = dense(gated, after(branch_low, mix_theirs, out_parts), bf16, 0)
    out_sum = out_sum.reshape(count // 2, 2, my_rows, width)
    out_theirs = flip(lax.dynamic_index_in_dim(out_sum, 1 - core[0], 1, keepdims=False), "dp", 1)
    mix_sum = mixer_sums(in_mine, mix_right, flip(mix_theirs, "dp", 1), out_sum, out_theirs, core)
    mix_mine = scatter_dp(mix_sum)
    down_back = swap_columns(after(down_mine, mix_sum))
    ffn_back = swap_columns(after(ffn_mine, down_back))
    (block_output,) = combine(
        lambda total, resid: (resid + total,), (out_parts,), (after(resid, mix_sum),), (bf16,), half
    )
    in_partial = exchanged_product(after(mix_right, block_output), mix_cols, row_place, half)
    in_parts = swap_seq(after(in_partial, ffn_back))
    (ffn_gate_weight_grad, ffn_up_weight_grad), ffn_sums = return_columns(
        after(ffn_back, in_partial), [ffn_gate_weight, ffn_up_weight], True
    )
    (input_grad,) = combine(input_back, (in_parts,), (resid_grad, x_low, gain_in), (f32,), half)
    (ffn_down_weight_grad,), _ = return_columns(after(down_back, in_partial), [ffn_down_weight])

    logit_sum = gather_small(sum_small(-after(logit_part, in_partial)[0] * (1.0 - bound[0]), "dp"), "seq")
    at = (lax.axis_index("dp") * ranks + rank) * my_rows
    bound_logit_grad = lax.dynamic_slice_in_dim(logit_sum, at, my_rows)
    mix_mine = after(mix_mine, in_parts)
    mix_grads, mix_sums = return_columns(swap_columns(mix_mine[:, : 4 * my_width]), mix_weights)
    out_mine = mix_mine[:, 4 * my_width :].reshape(ranks, my_rows, my_width)
    out_mine = lax.ppermute(out_mine, ("dp", "seq"), [(b, a) for a, b in row_route()])
    output_weight_grad = jnp.moveaxis(out_mine, 0, 1).reshape(my_rows, width).astype(f32)
    query_weight_grad, forget_weight_grad, input_weight_grad, output_gate_weight_grad = mix_grads
    mix_gain_grad = mix_sums / mix_gain.astype(f32)
    ffn_gain_grad = ffn_sums / ffn_gain.astype(f32)
    return (
        block_output.reshape(rows, length, width),
        input_grad.reshape(rows, length, width),
        mix_gain_grad,
        bound_logit_grad,
        query_weight_grad,
        forget_weight_grad,
        input_weight_grad,
        output_gate_weight_grad,
        output_weight_grad,
        ffn_gain_grad,
        ffn_gate_weight_grad,
        ffn_up_weight_grad,
        ffn_down_weight_grad,
    )


def solution(mesh):
    by_token = P("dp", "seq", None)
    vector = P(("dp", "seq"))
    matrix = P(("dp", "seq"), None)
    return jax.shard_map(
        local,
        mesh=mesh,
        in_specs=(by_token, P("dp", "seq"), vector, vector)
        + (matrix,) * 5
        + (vector,)
        + (matrix,) * 3
        + (by_token,),
        out_specs=(by_token, by_token, vector, vector) + (matrix,) * 5 + (vector,) + (matrix,) * 3,
        check_vma=False,
    )
```

```python
import functools

import jax
import jax.numpy as jnp
from jax import lax
from jax.experimental import pallas as pl
from jax.experimental.pallas import tpu as pltpu
from jax.sharding import PartitionSpec as P

HEAD_FEATURES = 128
LANES = 128

eps_model = 1e-06
eps_group = 1e-05
f32 = jnp.float32
bf16 = jnp.bfloat16

vmem = pltpu.CompilerParams(vmem_limit_bytes=48 * 1024 * 1024)


def cost(flops, moved=0):
    return pl.CostEstimate(flops=flops, bytes_accessed=moved, transcendentals=0)


def flip(block, axis, bits):
    return lax.ppermute(block, axis, [(i, i ^ bits) for i in range(lax.axis_size(axis))])


def gather_small(block, axis):
    count, mine = (lax.axis_size(axis), lax.axis_index(axis))
    bit = 1
    while bit < count:
        other = flip(block, axis, bit)
        upper = (mine & bit) != 0
        block = jnp.concatenate(
            (jnp.where(upper, other, block), jnp.where(upper, block, other)), axis=0
        )
        bit *= 2
    return block


def sum_small(block, axis):
    others = [flip(block, axis, bits) for bits in range(1, lax.axis_size(axis))]
    return functools.reduce(jnp.add, others, block)


def slots():
    if lax.axis_size("seq") == 4:
        return [(1, 0), (3, 0), (2, 1), (3, 1), (0, 0), (0, 1), (2, 0), (1, 1)]
    return [(k, h) for k in range(lax.axis_size("seq")) for h in range(2)]


def slot_table():
    place = {slot: i for i, slot in enumerate(slots())}
    count = lax.axis_size("seq")
    table = jnp.array([[place[k, h] for h in range(2)] for k in range(count)], jnp.int32)
    return table[jnp.arange(count) ^ lax.axis_index("seq")].reshape(2 * count)


def row_places():
    k, h = (jnp.array(bits, jnp.int32) for bits in zip(*slots()))
    return (k ^ lax.axis_index("seq")) * 2 + h


def gather_seq(block, second=()):
    count = lax.axis_size("seq")
    half = block.shape[0] // 2
    if count == 4:
        near = flip(block, "seq", 1)
        far = flip(block, "seq", 2)
        corner_top = flip(after(near[:half], *second), "seq", 2)
        corner_low = flip(after(far[half:], *second), "seq", 1)
        found = {(3, 0): (3, 0), (3, 1): (4, 0)}
        for k in range(3):
            found[k, 0], found[k, 1] = ((k, 0), (k, half))
        return (block, near, far, corner_top, corner_low), [found[slot] for slot in slots()]
    bit = 1
    while bit < count:
        block = jnp.concatenate((block, flip(block, "seq", bit)), axis=0)
        bit *= 2
    return (block,), [(0, i * half) for i in range(2 * count)]


def partial_layout(tokens):
    count = lax.axis_size("seq")
    if count == 4:
        return [(0, 2, bf16), (2, 4, bf16), (4, 8, f32)]
    return [(0, 2 * count, f32)]


def scatter_seq(partials, half, beside=()):
    if len(partials) == 3:
        near, far, rest = partials
        near = flip(near, "seq", 1)
        far = flip(far, "seq", 2)
        rest = after(rest, *beside)
        across = (rest[2 * half : 3 * half] + near[half:].astype(f32)).astype(bf16)
        along = (rest[3 * half :] + far[half:].astype(f32)).astype(bf16)
        return (rest, near, far, flip(across, "seq", 2), flip(along, "seq", 1))
    (total,) = partials
    bit = lax.axis_size("seq") // 2
    while bit:
        middle = total.shape[0] // 2
        total = total[:middle] + flip(total[middle:].astype(bf16), "seq", bit).astype(f32)
        bit //= 2
    return (total,)


def swap_seq(pieces):
    return lax.all_to_all(pieces, "seq", split_axis=0, concat_axis=0, tiled=True)


def gather_dp(block):
    return lax.all_gather(block, "dp", axis=0, tiled=True)


def scatter_dp(mine):
    groups = [list(range(c, lax.axis_size("dp"), 2)) for c in range(2)]
    return lax.psum_scatter(
        mine, "dp", scatter_dimension=0, axis_index_groups=groups, tiled=True
    )


def row_route():
    count, ranks = (lax.axis_size("dp"), lax.axis_size("seq"))
    return [(b, (b % count) * ranks + b // count) for b in range(count * ranks)]


def after(value, *others):
    return lax.optimization_barrier((value,) + others)[0]


def block(*shape, at=None):
    return pl.BlockSpec(shape, at or (lambda *_: (0,) * len(shape)))


def column_blocks(width, interleave):
    size = LANES if interleave else width
    return [(j * size, size) for j in range(width // size)]


def pieces_kernel(interleave, *refs):
    weights, out_ref = (refs[:-1], refs[-1])
    blocks = column_blocks(weights[0].shape[1], interleave)
    at = 0
    for start, size in blocks:
        for ref in weights:
            out_ref[0, :, at : at + size] = ref[:, start : start + size]
            at += size


def column_pieces(weights, interleave=False):
    ranks = lax.axis_size("seq")
    rows, width = (weights[0].shape[0], weights[0].shape[1] // ranks)
    if width % LANES:
        parts = [jnp.moveaxis(w.reshape(rows, ranks, width), 1, 0) for w in weights]
        return jnp.concatenate(parts, axis=2)
    total = width * len(weights)
    return pl.pallas_call(
        functools.partial(pieces_kernel, interleave),
        grid=(ranks,),
        in_specs=[block(rows, width, at=lambda r: (0, r)) for _ in weights],
        out_specs=block(1, rows, total, at=lambda r: (r, 0, 0)),
        out_shape=jax.ShapeDtypeStruct((ranks, rows, total), bf16),
        compiler_params=vmem,
        cost_estimate=cost(0, 4 * rows * total * ranks),
        name="column_pieces",
    )(*weights)


def return_kernel(interleave, count, *refs):
    pieces_ref, weights, grads, (gain_ref,) = (
        refs[0],
        refs[1 : 1 + count],
        refs[1 + count : 1 + 2 * count],
        refs[1 + 2 * count :],
    )

    @pl.when(pl.program_id(0) == 0)
    def _():
        gain_ref[...] = jnp.zeros_like(gain_ref)

    at = 0
    total = jnp.zeros(gain_ref.shape, f32)
    for start, size in column_blocks(weights[0].shape[1], interleave):
        for weight_ref, grad_ref in zip(weights, grads):
            grad = pieces_ref[0, :, at : at + size].astype(f32)
            grad_ref[:, start : start + size] = grad
            weight = weight_ref[:, start : start + size].astype(f32)
            total += jnp.sum(weight * grad, axis=1, keepdims=True)
            at += size
    gain_ref[...] += total


def swap_columns(mine):
    ranks = lax.axis_size("seq")
    return swap_seq(mine.reshape(ranks, mine.shape[0] // ranks, mine.shape[1]))


def return_columns(pieces, weights, interleave=False):
    ranks, rows, total = pieces.shape
    width = weights[0].shape[1] // ranks
    if width % LANES:
        grads = [
            jnp.moveaxis(pieces[:, :, i * width : (i + 1) * width], 0, 1)
            .reshape(rows, ranks * width)
            .astype(f32)
            for i in range(len(weights))
        ]
        return grads, sum(jnp.sum(w.astype(f32) * g, axis=1) for w, g in zip(weights, grads))
    columns = block(rows, width, at=lambda r: (0, r))
    *grads, sums = pl.pallas_call(
        functools.partial(return_kernel, interleave, len(weights)),
        grid=(ranks,),
        in_specs=[block(1, rows, total, at=lambda r: (r, 0, 0))] + [columns] * len(weights),
        out_specs=[columns] * len(weights) + [block(rows, 1)],
        out_shape=[jax.ShapeDtypeStruct(w.shape, f32) for w in weights]
        + [jax.ShapeDtypeStruct((rows, 1), f32)],
        compiler_params=vmem,
        cost_estimate=cost(0, 8 * rows * total * ranks),
        name="return_columns",
    )(pieces, *weights)
    return grads, sums[:, 0]


def sums(mask, terms):
    high = terms.astype(bf16)
    low = (terms - high.astype(f32)).astype(bf16)
    ones = mask.astype(bf16)
    return matmul(ones, low) + matmul(ones, high)


def product(left, right, left_dim, right_dim):
    left_high, right_high = (left.astype(bf16), right.astype(bf16))
    left_low = (left - left_high.astype(f32)).astype(bf16)
    right_low = (right - right_high.astype(f32)).astype(bf16)
    return (
        matmul(left_high, right_low, left_dim, right_dim)
        + matmul(left_low, right_high, left_dim, right_dim)
        + matmul(left_high, right_high, left_dim, right_dim)
    )


def chunk_parts(chunk, seg_ref, seg_col_ref, seg_row_ref, pre_ref, bound_ref):
    size, wide = pre_ref.shape
    width = wide // 3
    first = chunk * size
    prior = seg_ref[jnp.maximum(first - 1, 0)]
    last = seg_ref[first + size - 1]
    seg_col = seg_col_ref[...]
    at = lax.broadcasted_iota(jnp.int32, (size, size), 0)
    of = lax.broadcasted_iota(jnp.int32, (size, size), 1)
    seen = (seg_col == seg_row_ref[...]) & (at >= of)
    linked = (seg_col == prior).astype(f32)
    tail = (seg_col == last).astype(f32)
    linked_last = (prior == last).astype(f32)
    query_pre = pre_ref[:, 0:width]
    forget_pre = pre_ref[:, width : 2 * width]
    value = pre_ref[:, 2 * width : 3 * width]
    forget_sig = jax.nn.sigmoid(-forget_pre)
    key = bound_ref[...] * forget_sig
    query_sig = jax.nn.sigmoid(query_pre)
    lower = (at >= of).astype(f32)
    cumul = sums(lower, jnp.log1p(-key))
    grow = jnp.exp(cumul)
    shrink = jnp.exp(-cumul)
    end = grow[size - 1 :, :]
    query_d = query_pre * query_sig * grow
    key_d = key * shrink
    key_t = key_d * end * tail
    keep = end * linked_last
    return locals()


def forward_kernel(seg_ref, slot_ref, seg_col_ref, seg_row_ref, pre_ref, bound_ref, mixed_ref, states_ref, state_ref):
    step = pl.program_id(0)
    heads = mixed_ref.shape[1] // HEAD_FEATURES

    @pl.when(step == 0)
    def _():
        state_ref[...] = jnp.zeros_like(state_ref)

    p = chunk_parts(step, seg_ref, seg_col_ref, seg_row_ref, pre_ref, bound_ref)
    for h in range(heads):
        cols = slice(h * HEAD_FEATURES, (h + 1) * HEAD_FEATURES)
        query_d, key_d, value = p["query_d"][:, cols], p["key_d"][:, cols], p["value"][:, cols]
        state = state_ref[h]
        states_ref[0, h] = state
        scores = jnp.where(p["seen"], product(query_d, key_d, 1, 1), 0.0)
        mixed = product(scores, value, 1, 0) + product(query_d * p["linked"], state, 1, 1)
        mixed_ref[:, cols] = mixed
        state_ref[h] = state * p["keep"][:, cols] + product(value, p["key_t"][:, cols], 0, 0)


def backward_kernel(seg_ref, slot_ref, seg_col_ref, seg_row_ref, pre_ref, bound_ref, outgate_pre_ref, mixed_ref, gated_grad_ref, states_ref, grads_ref, logit_ref, back_ref, through_ref):
    step = pl.program_id(0)
    chunk = pl.num_programs(0) - 1 - step
    width = mixed_ref.shape[1]
    heads = width // HEAD_FEATURES

    @pl.when(step == 0)
    def _():
        back_ref[...] = jnp.zeros_like(back_ref)
        through_ref[...] = jnp.zeros_like(through_ref)
        logit_ref[...] = jnp.zeros_like(logit_ref)

    p = chunk_parts(chunk, seg_ref, seg_col_ref, seg_row_ref, pre_ref, bound_ref)
    query_pre, query_sig = p["query_pre"], p["query_sig"]
    upper = (p["at"] <= p["of"]).astype(f32)
    for h in range(heads):
        cols = slice(h * HEAD_FEATURES, (h + 1) * HEAD_FEATURES)
        query_d, key_d, key_t, value = (p[k][:, cols] for k in ("query_d", "key_d", "key_t", "value"))
        grow, shrink, end, keep, key = (p[k][:, cols] for k in ("grow", "shrink", "end", "keep", "key"))
        state = states_ref[0, h]
        back = back_ref[h]
        mixed = mixed_ref[:, cols]
        factor = lax.rsqrt(jnp.mean(mixed * mixed, axis=-1, keepdims=True) + eps_group)
        normed = mixed * factor
        gated_grad = gated_grad_ref[:, cols]
        gate = outgate_pre_ref[:, cols]
        gate_sig = jax.nn.sigmoid(gate)
        outgate_grad = gated_grad * normed * (gate_sig * (1.0 + gate * (1.0 - gate_sig)))
        weighted = gated_grad * (gate * gate_sig)
        mixed_grad = factor * (
            weighted - normed * jnp.mean(weighted * normed, axis=-1, keepdims=True)
        )
        scores = jnp.where(p["seen"], product(query_d, key_d, 1, 1), 0.0)
        scores_grad = jnp.where(p["seen"], product(mixed_grad, value, 1, 1), 0.0)
        value_grad = product(scores, mixed_grad, 0, 0) + product(key_t, back, 1, 1)
        query_d_grad = product(scores_grad, key_d, 1, 0) + p["linked"] * product(mixed_grad, state, 1, 0)
        key_d_grad = product(scores_grad, query_d, 0, 0)
        key_t_grad = product(value, back, 1, 0)
        key_grad = key_d_grad * shrink + (p["tail"] * end * shrink) * key_t_grad
        change = query_d * query_d_grad - key_d * key_d_grad - key_t * key_t_grad
        through = sums(upper, change) + through_ref[:, cols]
        key_total = key_grad - through / (1.0 - key)
        new_back = back * keep + product(mixed_grad, query_d * p["linked"], 0, 0)
        back_ref[h] = new_back
        through_ref[:, cols] = jnp.sum(new_back * state, axis=0, keepdims=True)
        sig = query_sig[:, cols]
        query_grad = query_d_grad * grow * (sig * (1.0 + query_pre[:, cols] * (1.0 - sig)))
        weighted_key = key_total * key
        forget_grad = -weighted_key * (1.0 - p["forget_sig"][:, cols])
        logit_ref[:, cols] += jnp.sum(weighted_key, axis=0, keepdims=True)
        for part, grad in enumerate((query_grad, forget_grad, value_grad, outgate_grad)):
            lo = part * width + h * HEAD_FEATURES
            grads_ref[:, lo : lo + HEAD_FEATURES] = grad.astype(bf16)


def recurrence_forward(segments, table, pre, bound):
    tokens, wide = pre.shape
    steps = table.shape[0]
    size, width = (tokens // steps, wide // 4)
    heads = width // HEAD_FEATURES
    return pl.pallas_call(
        forward_kernel,
        grid_spec=pltpu.PrefetchScalarGridSpec(
            num_scalar_prefetch=2,
            grid=(steps,),
            in_specs=[
                pl.BlockSpec((size, 1), lambda i, s, t: (i, 0)),
                pl.BlockSpec((1, size), lambda i, s, t: (0, i)),
                pl.BlockSpec((size, 3 * width), lambda i, s, t: (t[i], 0)),
                pl.BlockSpec((1, width), lambda i, s, t: (0, 0)),
            ],
            out_specs=[
                pl.BlockSpec((size, width), lambda i, s, t: (t[i], 0)),
                pl.BlockSpec((1, heads, HEAD_FEATURES, HEAD_FEATURES), lambda i, s, t: (i, 0, 0, 0)),
            ],
            scratch_shapes=[pltpu.VMEM((heads, HEAD_FEATURES, HEAD_FEATURES), f32)],
        ),
        out_shape=[
            jax.ShapeDtypeStruct((tokens, width), f32),
            jax.ShapeDtypeStruct((steps, heads, HEAD_FEATURES, HEAD_FEATURES), f32),
        ],
        compiler_params=vmem,
        cost_estimate=cost(320 * tokens * width * HEAD_FEATURES),
        name="recurrence_forward",
    )(segments, table, segments[:, None], segments[None, :], pre, bound)


def recurrence_backward(segments, table, pre, bound, mixed, gated_grad, states):
    tokens, wide = pre.shape
    steps = table.shape[0]
    size, width = (tokens // steps, wide // 4)
    heads = width // HEAD_FEATURES
    tokens_block = pl.BlockSpec((size, width), lambda i, s, t: (t[steps - 1 - i], 0))
    return pl.pallas_call(
        backward_kernel,
        grid_spec=pltpu.PrefetchScalarGridSpec(
            num_scalar_prefetch=2,
            grid=(steps,),
            in_specs=[
                pl.BlockSpec((size, 1), lambda i, s, t: (steps - 1 - i, 0)),
                pl.BlockSpec((1, size), lambda i, s, t: (0, steps - 1 - i)),
                pl.BlockSpec((size, 3 * width), lambda i, s, t: (t[steps - 1 - i], 0)),
                pl.BlockSpec((1, width), lambda i, s, t: (0, 0)),
                pl.BlockSpec((size, width), lambda i, s, t: (t[steps - 1 - i], 3)),
                tokens_block,
                tokens_block,
                pl.BlockSpec(
                    (1, heads, HEAD_FEATURES, HEAD_FEATURES),
                    lambda i, s, t: (steps - 1 - i, 0, 0, 0),
                ),
            ],
            out_specs=[
                pl.BlockSpec((size, 4 * width), lambda i, s, t: (t[steps - 1 - i], 0)),
                pl.BlockSpec((1, width), lambda i, s, t: (0, 0)),
            ],
            scratch_shapes=[
                pltpu.VMEM((heads, HEAD_FEATURES, HEAD_FEATURES), f32),
                pltpu.VMEM((1, width), f32),
            ],
        ),
        out_shape=[
            jax.ShapeDtypeStruct((tokens, 4 * width), bf16),
            jax.ShapeDtypeStruct((1, width), f32),
        ],
        compiler_params=vmem,
        cost_estimate=cost(620 * tokens * width * HEAD_FEATURES),
        name="recurrence_backward",
    )(segments, table, segments[:, None], segments[None, :], pre, bound, pre, mixed, gated_grad, states)


def matmul(left, right, left_dim=1, right_dim=0):
    return lax.dot_general(
        left, right, (((left_dim,), (right_dim,)), ((), ())), preferred_element_type=f32
    )


def rms_factor(value):
    return lax.rsqrt(jnp.mean(value * value, axis=-1, keepdims=True) + eps_model)


def rms_back(grad_unit, unit, factor):
    return factor * (grad_unit - unit * jnp.mean(grad_unit * unit, axis=-1, keepdims=True))


def product_kernel(left_dim, *refs):
    left_ref, right_ref, *added, out_ref = refs
    total = matmul(left_ref[...], right_ref[...], left_dim, 0)
    for ref in added:
        total += ref[...].astype(f32)
    out_ref[...] = total.astype(out_ref.dtype)


def dense(left, right, dtype, left_dim=1, added=None, parts=2):
    height, width = (left.shape[1 - left_dim], right.shape[1])
    size = width // parts if (width // parts) % LANES == 0 else width
    columns = block(height, size, at=lambda j: (0, j))
    extra = [] if added is None else [added]
    return pl.pallas_call(
        functools.partial(product_kernel, left_dim),
        grid=(width // size,),
        in_specs=[block(*left.shape), block(right.shape[0], size, at=lambda j: (0, j))]
        + [columns] * len(extra),
        out_specs=columns,
        out_shape=jax.ShapeDtypeStruct((height, width), dtype),
        compiler_params=vmem,
        cost_estimate=cost(3 * left.shape[0] * left.shape[1] * width),
        name="dense",
    )(left, right, *extra)


def mixer_sums_kernel(count, rows, core_ref, left_ref, right_ref, theirs_ref, out_ref, out_theirs_ref, total_ref):
    step = pl.program_id(0)

    @pl.when(step < count)
    def _():
        total = matmul(left_ref[...], right_ref[...], 0, 0) + theirs_ref[...].astype(f32)
        total_ref[...] = total.astype(bf16)

    @pl.when(step == count)
    def _():
        width = total_ref.shape[1]
        for z in range(out_ref.shape[0]):
            both = (out_ref[z, 0].astype(f32) + out_theirs_ref[z].astype(f32)).astype(bf16)
            ranks = both.shape[1] // width
            for j in range(ranks):
                at = (z * ranks + j) * rows
                total_ref[at : at + rows, :] = both[:, j * width : (j + 1) * width]


def mixer_sums(left, right, theirs, out_sum, out_theirs, core):
    tokens, height = left.shape
    lines, cores, rows, width = out_sum.shape
    size = right.shape[1] // 4
    columns = block(height, size, at=lambda j, c: (0, jnp.minimum(j, 3)))
    return pl.pallas_call(
        functools.partial(mixer_sums_kernel, 4, rows),
        grid_spec=pltpu.PrefetchScalarGridSpec(
            num_scalar_prefetch=1,
            grid=(5,),
            in_specs=[
                block(tokens, height),
                block(tokens, size, at=lambda j, c: (0, jnp.minimum(j, 3))),
                columns,
                block(lines, 1, rows, width, at=lambda j, c: (0, c[0], 0, 0)),
                block(lines, rows, width),
            ],
            out_specs=block(height, size, at=lambda j, c: (0, j)),
        ),
        out_shape=jax.ShapeDtypeStruct((height, 5 * size), bf16),
        compiler_params=vmem,
        cost_estimate=cost(3 * tokens * height * 4 * size),
        name="mixer_sums",
    )(core, left, right, theirs, out_sum, out_theirs)


def store_halves(core, value, rows, row_block, mine_ref, theirs_ref):
    for z in range(value.shape[1] // (2 * row_block)):
        even = value[:, 2 * z * row_block : (2 * z + 1) * row_block]
        odd = value[:, (2 * z + 1) * row_block : (2 * z + 2) * row_block]
        to = slice(z * row_block, (z + 1) * row_block)

        @pl.when(core == 0)
        def _():
            mine_ref[rows, to] = even
            theirs_ref[rows, to] = odd

        @pl.when(core == 1)
        def _():
            mine_ref[rows, to] = odd
            theirs_ref[rows, to] = even


def assemble_kernel(places, half, row_block, normed, core_ref, *refs):
    *pieces, gain_ref, all_ref, mine_ref, theirs_ref = refs
    for slot, (piece, row) in enumerate(places):
        rows = slice(slot * half, (slot + 1) * half)
        value = pieces[piece][row : row + half, :]
        if normed:
            wide = value.astype(f32)
            value = (wide * rms_factor(wide) * gain_ref[...]).astype(bf16)
        all_ref[rows, :] = value
        store_halves(core_ref[0], value, rows, row_block, mine_ref, theirs_ref)


def assemble(gathered, core, row_block, gain=None):
    pieces, places = gathered
    half = pieces[0].shape[0] // 2 if len(pieces) > 1 else pieces[0].shape[0] // len(places)
    tokens, width = (half * len(places), pieces[0].shape[1])
    normed = gain is not None
    gain = gain if normed else jnp.zeros((1, width), f32)
    shapes = [(tokens, width), (tokens, width // 2), (tokens, width // 2)]
    return pl.pallas_call(
        functools.partial(assemble_kernel, places, half, row_block, normed),
        grid_spec=pltpu.PrefetchScalarGridSpec(
            num_scalar_prefetch=1,
            grid=(1,),
            in_specs=[block(*piece.shape) for piece in pieces] + [block(1, width)],
            out_specs=[block(*shape) for shape in shapes],
        ),
        out_shape=[jax.ShapeDtypeStruct(shape, bf16) for shape in shapes],
        compiler_params=vmem,
        cost_estimate=cost(0, 12 * tokens * width),
        name="assemble",
    )(core, *pieces, gain)


def store_partials(value, layout, half, refs):
    for (first, last, dtype), ref in zip(layout, refs):
        ref[...] = value[first * half : last * half, :].astype(dtype)


def partial_specs(layout, half, width, columns):
    specs = [block((b - a) * half, columns, at=lambda j: (0, j)) for a, b, _ in layout]
    shapes = [jax.ShapeDtypeStruct(((b - a) * half, width), dtype) for a, b, dtype in layout]
    return specs, shapes


def partial_kernel(layout, half, cuts, left_ref, *refs):
    weights, outs = (refs[: len(cuts)], refs[len(cuts) :])
    total = None
    for (first, last), ref in zip(cuts, weights):
        term = matmul(left_ref[:, first:last], ref[...], 1, 1)
        total = term if total is None else total + term
    store_partials(total, layout, half, outs)


def ordered_kernel(half, places_ref, left_ref, weight_ref, out_ref):
    total = matmul(left_ref[...], weight_ref[...], 1, 1).astype(bf16)
    for slot in range(left_ref.shape[0] // half):
        to = pl.multiple_of(places_ref[slot] * half, half)
        out_ref[pl.ds(to, half), :] = total[slot * half : (slot + 1) * half, :]


def exchanged_product(left, weight, places, half, columns=512):
    tokens, depth = left.shape
    width = weight.shape[0]
    ranks = lax.axis_size("seq")
    partial = pl.pallas_call(
        functools.partial(ordered_kernel, half),
        grid_spec=pltpu.PrefetchScalarGridSpec(
            num_scalar_prefetch=1,
            grid=(width // columns,),
            in_specs=[block(tokens, depth), block(columns, depth, at=lambda j, p: (j, 0))],
            out_specs=block(tokens, columns, at=lambda j, p: (0, j)),
        ),
        out_shape=jax.ShapeDtypeStruct((tokens, width), bf16),
        compiler_params=vmem,
        cost_estimate=cost(3 * tokens * depth * width),
        name="exchanged_product",
    )(places, left, weight)
    return partial.reshape(ranks, 2 * half, width)


def partial_product(left, weights, widths, half, columns=512):
    tokens, depth = left.shape
    width = weights[0].shape[0]
    layout = partial_layout(tokens)
    specs, shapes = partial_specs(layout, half, width, columns)
    cuts = [(sum(widths[:i]), sum(widths[: i + 1])) for i in range(len(widths))]
    return pl.pallas_call(
        functools.partial(partial_kernel, layout, half, cuts),
        grid=(width // columns,),
        in_specs=[block(tokens, depth)]
        + [block(columns, size, at=lambda j: (j, 0)) for size in widths],
        out_specs=specs,
        out_shape=shapes,
        compiler_params=vmem,
        cost_estimate=cost(3 * tokens * depth * width),
        name="partial_product",
    )(left, *weights)


def gate_out_kernel(layout, half, mixed_ref, outgate_pre_ref, out_ref, gated_ref, *outs):
    @pl.when(pl.program_id(0) == 0)
    def _():
        for h in range(mixed_ref.shape[1] // HEAD_FEATURES):
            cols = slice(h * HEAD_FEATURES, (h + 1) * HEAD_FEATURES)
            mixed, gate = mixed_ref[:, cols], outgate_pre_ref[:, cols]
            factor = lax.rsqrt(jnp.mean(mixed * mixed, axis=-1, keepdims=True) + eps_group)
            gated_ref[:, cols] = (mixed * factor * (gate * jax.nn.sigmoid(gate))).astype(bf16)

    store_partials(matmul(gated_ref[...], out_ref[...]), layout, half, outs)


def gate_out(mixed, pre, out_rows, half):
    tokens, my_width = mixed.shape
    width = out_rows.shape[1]
    layout = partial_layout(tokens)
    specs, shapes = partial_specs(layout, half, width, my_width)
    gated, *partials = pl.pallas_call(
        functools.partial(gate_out_kernel, layout, half),
        grid=(width // my_width,),
        in_specs=[
            block(tokens, my_width),
            block(tokens, my_width, at=lambda j: (0, 3)),
            block(my_width, my_width, at=lambda j: (0, j)),
        ],
        out_specs=[block(tokens, my_width)] + specs,
        out_shape=[jax.ShapeDtypeStruct((tokens, my_width), bf16)] + shapes,
        compiler_params=vmem,
        cost_estimate=cost(3 * tokens * my_width * width, 16 * tokens * width),
        name="gate_out",
    )(mixed, pre, out_rows)
    return gated, partials


def gated_grad_kernel(places, half, *refs):
    *pieces, out_ref, all_ref, grad_ref = refs
    for slot, (piece, row) in enumerate(places):
        all_ref[slot * half : (slot + 1) * half, :] = pieces[piece][row : row + half, :]
    grad_ref[...] = matmul(all_ref[...], out_ref[...], 1, 1)


def gated_gradient(gathered, out_rows, half):
    pieces, places = gathered
    my_width, width = out_rows.shape
    tokens = half * len(places)
    return pl.pallas_call(
        functools.partial(gated_grad_kernel, places, half),
        grid=(1,),
        in_specs=[block(*piece.shape) for piece in pieces] + [block(*out_rows.shape)],
        out_specs=[block(tokens, width), block(tokens, my_width)],
        out_shape=[
            jax.ShapeDtypeStruct((tokens, width), bf16),
            jax.ShapeDtypeStruct((tokens, my_width), f32),
        ],
        compiler_params=vmem,
        cost_estimate=cost(3 * tokens * width * my_width),
        name="gated_gradient",
    )(*pieces, out_rows)


def ffn_forward_kernel(places, half, *refs):
    *pieces, weight_ref, both_ref, hidden_ref, all_ref = refs

    @pl.when(pl.program_id(0) == 0)
    def _():
        for slot, (piece, row) in enumerate(places):
            rows = slice(slot * half, (slot + 1) * half)
            all_ref[rows, :] = pieces[piece][row : row + half, :]

    both = matmul(all_ref[...], weight_ref[...])
    both_ref[...] = both
    gate, up = (both[:, :LANES], both[:, LANES:])
    hidden_ref[...] = (gate * jax.nn.sigmoid(gate) * up).astype(bf16)


def ffn_forward(gathered, ffn_cols, half):
    pieces, places = gathered
    width, total = ffn_cols.shape
    tokens = half * len(places)
    if (total // 2) % LANES:
        (rows,) = pieces
        both = matmul(rows, ffn_cols)
        gate, up = (both[:, : total // 2], both[:, total // 2 :])
        return both, (jax.nn.silu(gate) * up).astype(bf16), rows
    return pl.pallas_call(
        functools.partial(ffn_forward_kernel, places, half),
        grid=(total // (2 * LANES),),
        in_specs=[block(*piece.shape) for piece in pieces]
        + [block(width, 2 * LANES, at=lambda j: (0, j))],
        out_specs=[
            block(tokens, 2 * LANES, at=lambda j: (0, j)),
            block(tokens, LANES, at=lambda j: (0, j)),
            block(tokens, width),
        ],
        out_shape=[
            jax.ShapeDtypeStruct((tokens, total), f32),
            jax.ShapeDtypeStruct((tokens, total // 2), bf16),
            jax.ShapeDtypeStruct((tokens, width), bf16),
        ],
        compiler_params=vmem,
        cost_estimate=cost(3 * tokens * width * total),
        name="ffn_forward",
    )(*pieces, ffn_cols)


def ffn_backward_kernel(cotangent_ref, weight_ref, both_ref, grads_ref):
    width = weight_ref.shape[1]
    for first in range(0, width, 2 * LANES):
        last = min(first + 2 * LANES, width)
        hidden_grad = matmul(cotangent_ref[...], weight_ref[:, first:last])
        for at in range(first, last, LANES):
            grad = hidden_grad[:, at - first : at - first + LANES]
            gate = both_ref[:, 2 * at : 2 * at + LANES]
            up = both_ref[:, 2 * at + LANES : 2 * at + 2 * LANES]
            sig = jax.nn.sigmoid(gate)
            slope = sig * (1.0 + gate * (1.0 - sig))
            grads_ref[:, 2 * at : 2 * at + LANES] = (grad * up * slope).astype(bf16)
            grads_ref[:, 2 * at + LANES : 2 * at + 2 * LANES] = (grad * (gate * sig)).astype(bf16)


def ffn_backward(cotangent_all, down_cols, both):
    tokens, width = cotangent_all.shape
    mine = down_cols.shape[1]
    if mine % LANES:
        gate, up = (both[:, :mine], both[:, mine:])
        hidden_grad = matmul(cotangent_all, down_cols)
        sig = jax.nn.sigmoid(gate)
        gate_grad = hidden_grad * up * (sig * (1.0 + gate * (1.0 - sig)))
        up_grad = hidden_grad * (gate * sig)
        return jnp.concatenate((gate_grad, up_grad), axis=1).astype(bf16)
    rows = tokens // 2
    return pl.pallas_call(
        ffn_backward_kernel,
        grid=(2,),
        in_specs=[
            block(rows, width, at=lambda i: (i, 0)),
            block(width, mine),
            block(rows, 2 * mine, at=lambda i: (i, 0)),
        ],
        out_specs=block(rows, 2 * mine, at=lambda i: (i, 0)),
        out_shape=jax.ShapeDtypeStruct((tokens, 2 * mine), bf16),
        compiler_params=vmem,
        cost_estimate=cost(4 * tokens * width * mine),
        name="ffn_backward",
    )(cotangent_all, down_cols, both)


def add_up(parts):
    if len(parts) == 1 and len(parts[0].shape) == 3:
        return jnp.sum(parts[0][...].astype(f32), axis=0)
    if len(parts) == 1:
        return parts[0][...]
    rest, near, far, across, along = parts
    top = near[...].astype(f32) + across[...].astype(f32)
    low = far[...].astype(f32) + along[...].astype(f32)
    return rest[...] + jnp.where(pl.program_id(0) == 0, top, low)


def combine_kernel(post, count, given, *refs):
    parts, values, outs = (refs[:count], refs[count : count + given], refs[count + given :])
    results = post(add_up(parts), *(ref[...].astype(f32) for ref in values))
    for result, ref in zip(results, outs):
        ref[...] = result.astype(ref.dtype)


def combine(post, parts, values, dtypes, half):
    width = parts[0].shape[-1]
    mine = block(half, width, at=lambda h: (h, 0))
    fixed = block(half, width)
    part_specs = [mine] if len(parts) == 1 else [mine] + [fixed] * 4
    if parts[0].ndim == 3:
        part_specs = [block(parts[0].shape[0], half, width, at=lambda h: (0, h, 0))]
    value_specs = [block(1, width) if v.shape[0] == 1 else mine for v in values]
    return pl.pallas_call(
        functools.partial(combine_kernel, post, len(parts), len(values)),
        grid=(2,),
        in_specs=part_specs + value_specs,
        out_specs=[mine] * len(dtypes),
        out_shape=[jax.ShapeDtypeStruct((2 * half, width), dtype) for dtype in dtypes],
        compiler_params=vmem,
        cost_estimate=cost(0, 60 * half * width),
        name="combine",
    )(*parts, *values)


def residual(branch, inputs, gain):
    resid = inputs + branch
    return resid, resid * rms_factor(resid) * gain


def residual_back(mid_grad, cotangent, resid, gain):
    factor = rms_factor(resid)
    grad = cotangent + rms_back(mid_grad * gain, resid * factor, factor)
    return grad, grad


def input_back(in_grad, resid_grad, inputs, gain):
    factor = rms_factor(inputs)
    return (resid_grad + rms_back(in_grad * gain, inputs * factor, factor),)


def local(
    layer_input,
    segment_ids,
    mix_gain,
    bound_logit,
    query_weight,
    forget_weight,
    input_weight,
    output_gate_weight,
    output_weight,
    ffn_gain,
    ffn_gate_weight,
    ffn_up_weight,
    ffn_down_weight,
    output_cotangent,
):
    rows, length, width = layer_input.shape
    ranks, rank = (lax.axis_size("seq"), lax.axis_index("seq"))
    count = lax.axis_size("dp")
    my_width = width // ranks
    tokens = rows * length
    half = tokens // 2
    my_rows = mix_gain.shape[0]
    rank_rows = my_rows * ranks
    x_low = layer_input.reshape(tokens, width)
    cotangent_low = output_cotangent.reshape(tokens, width)
    core = (lax.axis_index("dp") & 1).reshape(1)

    mix_weights = [query_weight, forget_weight, input_weight, output_gate_weight]
    mix_pieces = swap_seq(column_pieces(mix_weights))
    mix_cols = gather_dp(mix_pieces.reshape(rank_rows, 4 * my_width))
    out_rows = gather_dp(lax.ppermute(output_weight, ("dp", "seq"), row_route()))
    x_pieces, places = gather_seq(after(x_low, mix_pieces))
    vectors = jnp.stack((mix_gain, bound_logit, ffn_gain), axis=1)
    vectors = gather_small(gather_small(vectors, "seq"), "dp")
    segments = gather_small(segment_ids[0], "seq")
    vectors = vectors.astype(f32)
    gain_in, logit, gain_mid = (vectors[:, 0], vectors[:, 1], vectors[:, 2])
    gain_in, gain_mid = (gain_in[None, :], gain_mid[None, :])
    table = slot_table()
    bound = jax.nn.sigmoid(-lax.dynamic_slice_in_dim(logit, rank * my_width, my_width))[None, :]
    normed_in, in_mine, in_theirs = assemble(
        (x_pieces, places), core, rank_rows, after(gain_in, segments, bound)
    )
    ffn_pieces = swap_seq(column_pieces([after(ffn_gate_weight, normed_in, out_rows), ffn_up_weight], True))
    ffn_cols = gather_dp(ffn_pieces.reshape(rank_rows, ffn_pieces.shape[2]))
    down_pieces = swap_seq(column_pieces([after(ffn_down_weight, ffn_pieces)]))
    down_cols = gather_dp(down_pieces.reshape(rank_rows, down_pieces.shape[2]))

    pre = dense(after(normed_in, down_pieces), mix_cols, f32, parts=2)
    mixed, states = recurrence_forward(segments, table, pre, bound)
    cotangent = gather_seq(after(cotangent_low, down_pieces))
    gated, partials = gate_out(after(mixed, *cotangent[0][:3]), pre, out_rows, half)
    branch_parts = scatter_seq(partials, half)
    cotangent_all, cotangent_mine, cotangent_theirs = assemble(cotangent, core, rank_rows)
    resid, normed_low = combine(
        residual, branch_parts, (after(x_low, cotangent_all), gain_mid), (f32, bf16), half
    )
    normed_mid = gather_seq(normed_low)

    both, hidden, mid_all = ffn_forward(normed_mid, ffn_cols, half)

    down_theirs = flip(dense(cotangent_theirs, hidden, bf16, 0), "dp", 1)
    down_sum = dense(cotangent_mine, hidden, bf16, 0, down_theirs)
    down_mine = scatter_dp(down_sum)
    cotangent_all = after(cotangent_all, down_sum)
    ffn_right = ffn_backward(cotangent_all, down_cols, both)
    mid_partials = partial_product(ffn_right, [ffn_cols], [ffn_cols.shape[1]], half)
    ffn_sum = dense(mid_all, after(ffn_right, mid_partials[0]), bf16, 0)
    mid_parts = scatter_seq(mid_partials, half, beside=(ffn_sum, down_mine))
    ffn_mine = lax.psum_scatter(after(ffn_sum, *mid_parts[:3]), "dp", scatter_dimension=0, tiled=True)

    resid_grad, branch_own = combine(
        residual_back, mid_parts, (cotangent_low, resid, gain_mid), (f32, bf16), half
    )
    branch, places = gather_seq(branch_own)
    row_place = row_places()
    out_partial = exchanged_product(after(hidden, branch_own), down_cols, row_place, half)
    branch = (after(branch[0], out_partial),) + branch[1:]
    branch_low, gated_grad = gated_gradient((branch, places), out_rows, half)
    out_parts = swap_seq(after(out_partial, branch_low))
    mix_right, logit_part = recurrence_backward(segments, table, pre, bound, mixed, gated_grad, states)
    mix_theirs = dense(in_theirs, mix_right, bf16, 0)
    out_sum = dense(gated, after(branch_low, mix_theirs, out_parts), bf16, 0)
    out_sum = out_sum.reshape(count // 2, 2, my_rows, width)
    out_theirs = flip(lax.dynamic_index_in_dim(out_sum, 1 - core[0], 1, keepdims=False), "dp", 1)
    mix_sum = mixer_sums(in_mine, mix_right, flip(mix_theirs, "dp", 1), out_sum, out_theirs, core)
    mix_mine = scatter_dp(mix_sum)
    down_back = swap_columns(after(down_mine, mix_sum))
    ffn_back = swap_columns(after(ffn_mine, down_back))
    (block_output,) = combine(
        lambda total, resid: (resid + total,), (out_parts,), (after(resid, mix_sum),), (bf16,), half
    )
    in_partial = exchanged_product(after(mix_right, block_output), mix_cols, row_place, half)
    in_parts = swap_seq(after(in_partial, ffn_back))
    (ffn_gate_weight_grad, ffn_up_weight_grad), ffn_sums = return_columns(
        after(ffn_back, in_partial), [ffn_gate_weight, ffn_up_weight], True
    )
    (input_grad,) = combine(input_back, (in_parts,), (resid_grad, x_low, gain_in), (f32,), half)
    (ffn_down_weight_grad,), _ = return_columns(after(down_back, in_partial), [ffn_down_weight])

    logit_sum = gather_small(sum_small(-after(logit_part, in_partial)[0] * (1.0 - bound[0]), "dp"), "seq")
    at = (lax.axis_index("dp") * ranks + rank) * my_rows
    bound_logit_grad = lax.dynamic_slice_in_dim(logit_sum, at, my_rows)
    mix_mine = after(mix_mine, in_parts)
    mix_grads, mix_sums = return_columns(swap_columns(mix_mine[:, : 4 * my_width]), mix_weights)
    out_mine = mix_mine[:, 4 * my_width :].reshape(ranks, my_rows, my_width)
    out_mine = lax.ppermute(out_mine, ("dp", "seq"), [(b, a) for a, b in row_route()])
    output_weight_grad = jnp.moveaxis(out_mine, 0, 1).reshape(my_rows, width).astype(f32)
    query_weight_grad, forget_weight_grad, input_weight_grad, output_gate_weight_grad = mix_grads
    mix_gain_grad = mix_sums / mix_gain.astype(f32)
    ffn_gain_grad = ffn_sums / ffn_gain.astype(f32)
    return (
        block_output.reshape(rows, length, width),
        input_grad.reshape(rows, length, width),
        mix_gain_grad,
        bound_logit_grad,
        query_weight_grad,
        forget_weight_grad,
        input_weight_grad,
        output_gate_weight_grad,
        output_weight_grad,
        ffn_gain_grad,
        ffn_gate_weight_grad,
        ffn_up_weight_grad,
        ffn_down_weight_grad,
    )


def solution(mesh):
    by_token = P("dp", "seq", None)
    vector = P(("dp", "seq"))
    matrix = P(("dp", "seq"), None)
    return jax.shard_map(
        local,
        mesh=mesh,
        in_specs=(by_token, P("dp", "seq"), vector, vector)
        + (matrix,) * 5
        + (vector,)
        + (matrix,) * 3
        + (by_token,),
        out_specs=(by_token, by_token, vector, vector) + (matrix,) * 5 + (vector,) + (matrix,) * 3,
        check_vma=False,
    )
```
